32 devices in a mesh: req: 8 (over z, y), ad: 4 (over x, core).
Axes of the slice: x: 2, y: 2, z: 4, core: 2. Of those that a mesh axis runs over, the one named last changes fastest.
Arguments:
- layer_input_hidden: bfloat16 [28672, 1536], P(('req', 'ad')), may hold values from -6 to 6
- input_norm_scale: float32 [1536], replicated, may hold values from 0.25 to 1.75
- query_key_value_weight: bfloat16 [1536, 3072], P(None, 'ad')
- output_weight: bfloat16 [1536, 1536], replicated, may hold values from -0.15625 to 0.15625
- adapter_down_weight: bfloat16 [8, 32, 1536], P('req'), may hold values from -0.15625 to 0.15625
- adapter_up_weight: bfloat16 [8, 16, 2304], P('req'), may hold values from -1.5 to 1.5
- prompt_token_length: int32 [32, 64], P(('req', 'ad')), may hold values from 12 to 16, as said below
- request_adapter_index: int32 [32, 64], P(('req', 'ad')), may hold values from 0 to 7, as said below
- adapter_holder_index: int32 [8], replicated, may hold values from 0 to 7, each once
Outputs:
- mixed: bfloat16 [28672, 1536], P(('req', 'ad'))
The draws below stay inside these ranges and needn't reach their ends.
Inputs may be any that keep to these rules, and one draw needn't show every extreme that they name: `prompt_token_length`: requests 2i and 2i + 1 of one device hold 28 tokens together; request j has 16 tokens wherever j is a multiple of 8. `request_adapter_index`: on one device, requests j and k name the same adapter exactly when j - k is a multiple of 8; every request j that is a multiple of 8 names one adapter, the same on all devices. So one device's tokens naming one adapter number at most 128, and exactly 128 for that common adapter.
All inputs are finite; a program needn't handle non-finite values.
Results may differ from the reference program's by a relative error of at most 0.012.
Values may be sent and summed in bfloat16 or wider, within the bound.
No kernel may reach another device: no remote copies, remote signals or barrier semaphores. Data moves between devices by JAX's collectives and lax.ppermute only.
A program may use at most 128 MiB of HBM per device.

```python
import math
import jax
import jax.numpy as jnp
from jax import lax

MODEL_WIDTH = 1536
HEADS = 16
KV_HEADS = 8
HEAD_DIM = 96
ADAPTER_RANK = 16
MAXLEN = 16
PAIR = 28
REQ_DEV = 64
QUERY_FEATURES = 1536
KEY_FEATURES = 768
TOK_DEV = 896
TOKENS = 28672
ADAPTER_TOTAL = 8
CAP = 128
N_REQ = 8
N_AD = 4


def draw_prompt_token_length(key, part):
    row_count = N_REQ * N_AD
    pair_count = REQ_DEV // 2
    first_len = jax.random.randint(jax.random.fold_in(key, 101), (row_count, pair_count), PAIR - MAXLEN, MAXLEN + 1).astype(jnp.int32)
    pair_index = jnp.arange(pair_count, dtype=jnp.int32)
    forced = 2 * pair_index % ADAPTER_TOTAL == 0
    first_len = jnp.where(forced[None, :], MAXLEN, first_len).astype(jnp.int32)
    stacked = jnp.stack([first_len, PAIR - first_len], axis=-1)
    return stacked.reshape(row_count, REQ_DEV).astype(jnp.int32)


def draw_request_adapter_index(key, part):
    row_count = N_REQ * N_AD
    common = jax.random.randint(jax.random.fold_in(key, 202), (), 0, ADAPTER_TOTAL).astype(jnp.int32)
    raw_scores = jax.random.randint(jax.random.fold_in(key, 303), (row_count, ADAPTER_TOTAL), 0, 1 << 20).astype(jnp.int32)
    distinct = raw_scores * ADAPTER_TOTAL + jnp.arange(ADAPTER_TOTAL, dtype=jnp.int32)[None, :]
    shuffled = jnp.argsort(distinct, axis=1, stable=True).astype(jnp.int32)
    swapped = jnp.where(shuffled == common, shuffled[:, :1], shuffled)
    swapped = swapped.at[:, 0].set(common)
    column_index = jnp.arange(REQ_DEV, dtype=jnp.int32) % ADAPTER_TOTAL
    return swapped[:, column_index].astype(jnp.int32)


def draw_query_key_value_weight(key, part):
    values = jax.random.normal(jax.random.fold_in(key, 404), (MODEL_WIDTH, QUERY_FEATURES + 2 * KEY_FEATURES), jnp.float32) * MODEL_WIDTH ** (-0.5)
    return values.astype(jnp.bfloat16)


def level_of(rng, extent, split, least, top_value):
    def one(dim, shards_of):
        heights = jax.random.uniform(jax.random.fold_in(jax.random.fold_in(rng, 6), dim), (shards_of,), jnp.float32, least / len(split), top_value / len(split))
        return jnp.repeat(jnp.exp(heights), extent[dim] // shards_of).reshape((-1,) + (1,) * (len(extent) - dim - 1))

    loudness = one(*split[0])
    for cut in split[1:]:
        loudness = loudness * one(*cut)
    return loudness


def gaussian(stream_key, shape, deviation, reach, cuts=(), kind=jnp.bfloat16):
    result = jax.random.normal(stream_key, shape, jnp.float32) * deviation
    if len(cuts) > 0:
        result = level_of(stream_key, shape, cuts, -0.22, 0.18) * result
    return jnp.clip(result, min=-reach, max=reach).astype(kind)


def setup_inputs(seed: int = 0) -> dict:
    streams_of = jax.random.split(jax.random.key(seed), 10)
    return {
        "layer_input_hidden": gaussian(streams_of[0], (TOKENS, MODEL_WIDTH), 1.0, 6.0, ((0, 32),)),
        "input_norm_scale": jnp.clip(1.0 + 0.15 * jax.random.normal(streams_of[1], (MODEL_WIDTH,), jnp.float32), 0.25, 1.75),
        "query_key_value_weight": draw_query_key_value_weight(jax.random.fold_in(streams_of[9], 71), 0),
        "output_weight": gaussian(streams_of[3], (QUERY_FEATURES, MODEL_WIDTH), QUERY_FEATURES ** -0.5, 0.15625),
        "adapter_down_weight": gaussian(streams_of[4], (ADAPTER_TOTAL, 2 * ADAPTER_RANK, MODEL_WIDTH), MODEL_WIDTH ** -0.5, 0.15625, ((0, 8),)),
        "adapter_up_weight": gaussian(streams_of[5], (ADAPTER_TOTAL, ADAPTER_RANK, QUERY_FEATURES + KEY_FEATURES), ADAPTER_RANK ** -0.5, 1.5, ((0, 8),)),
        "prompt_token_length": draw_prompt_token_length(jax.random.fold_in(streams_of[9], 71), 0),
        "request_adapter_index": draw_request_adapter_index(jax.random.fold_in(streams_of[9], 71), 0),
        "adapter_holder_index": jax.random.permutation(streams_of[8], ADAPTER_TOTAL).astype(jnp.int32),
    }


rope_theta = 100000.0

def token_layout(lengths, adapters, owner, tok_count, capacity):
    req_count = lengths.shape[0]
    req_ends = jnp.cumsum(lengths).astype(jnp.int32)
    req_starts = (req_ends - lengths).astype(jnp.int32)
    tok_index = jnp.arange(tok_count, dtype=jnp.int32)
    member = (tok_index[:, None] >= req_starts[None, :]) & (tok_index[:, None] < req_ends[None, :])
    inside = (tok_index - lax.optimization_barrier(jnp.sum(jnp.where(member, req_starts[None, :], 0), axis=1))).astype(jnp.int32)
    adapter_ids = jnp.arange(owner.shape[0], dtype=jnp.int32)
    slot_req = lax.optimization_barrier(jnp.sum(jnp.where(adapters[:, None] == adapter_ids[None, :], owner[None, :], 0), axis=1)).astype(jnp.int32)
    req_order = jnp.arange(req_count, dtype=jnp.int32)
    earlier = (slot_req[:, None] == slot_req[None, :]) & (req_order[None, :] < req_order[:, None])
    offset_req = lax.optimization_barrier(jnp.sum(jnp.where(earlier, lengths[None, :], 0), axis=1)).astype(jnp.int32)
    slot_token_rows = lax.optimization_barrier(jnp.sum(jnp.where(member, slot_req[None, :], 0), axis=1)).astype(jnp.int32)
    offset_tok = lax.optimization_barrier(jnp.sum(jnp.where(member, offset_req[None, :], 0), axis=1)).astype(jnp.int32)
    request = lax.optimization_barrier(jnp.sum(jnp.where(member, req_order[None, :], 0), axis=1)).astype(jnp.int32)
    dest_row = (slot_token_rows * capacity + offset_tok + inside).astype(jnp.int32)
    return (inside, slot_token_rows, dest_row, request)

def rotate(values, position):
    half_width = values.shape[-1] // 2
    inverse_freq = jnp.exp(-math.log(rope_theta) * 2.0 * jnp.arange(half_width, dtype=jnp.float32) / values.shape[-1])
    angles = position.astype(jnp.float32)[:, None] * inverse_freq[None, :]
    cosine = jnp.cos(angles)[:, None, :]
    sine_part = jnp.sin(angles)[:, None, :]
    first_half = values[..., :half_width]
    second_half = values[..., half_width:]
    return jnp.concatenate([first_half * cosine - second_half * sine_part, second_half * cosine + first_half * sine_part], axis=-1)

def attend(query, key, value, request):
    tok_count = query.shape[0]
    pair_count = tok_count // PAIR
    group_size = HEADS // KV_HEADS
    score_scale = 1.0 / math.sqrt(HEAD_DIM)
    query_g = query.reshape(pair_count, PAIR, KV_HEADS, group_size, HEAD_DIM).transpose(2, 0, 3, 1, 4)
    key_g = key.reshape(pair_count, PAIR, KV_HEADS, HEAD_DIM).transpose(2, 0, 1, 3)
    value_g = value.reshape(pair_count, PAIR, KV_HEADS, HEAD_DIM).transpose(2, 0, 1, 3)
    req_pair = request.reshape(pair_count, PAIR)
    inner = jnp.arange(PAIR, dtype=jnp.int32)
    allowed = (req_pair[:, :, None] == req_pair[:, None, :]) & (inner[None, :] <= inner[:, None])[None]

    def head_group(operands):
        q_blk, k_blk, v_blk = operands
        scores = jnp.einsum('pgqd,pkd->pgqk', q_blk.astype(jnp.float32), k_blk.astype(jnp.float32)) * score_scale
        scores = jnp.where(allowed[:, None], scores, -jnp.inf)
        row_max = lax.optimization_barrier(jnp.max(scores, axis=-1, keepdims=True))
        weights = jnp.exp(scores - row_max)
        probs = (weights / lax.optimization_barrier(jnp.sum(weights, axis=-1, keepdims=True))).astype(jnp.bfloat16)
        return jnp.einsum('pgqk,pkd->pgqd', probs.astype(jnp.float32), v_blk.astype(jnp.float32)).astype(jnp.bfloat16)
    attended = lax.map(head_group, (query_g, key_g, value_g))
    return attended.transpose(1, 3, 0, 2, 4).reshape(tok_count, HEADS * HEAD_DIM)

def reference(layer_input_hidden, input_norm_scale, query_key_value_weight, output_weight, adapter_down_weight, adapter_up_weight, prompt_token_length, request_adapter_index, adapter_holder_index):
    query_column_width = HEADS * HEAD_DIM
    kv_width = KV_HEADS * HEAD_DIM
    block_count = prompt_token_length.shape[0]
    blocks = layer_input_hidden.reshape(block_count, TOK_DEV, MODEL_WIDTH)

    def one_block(operands):
        hidden, lengths, adapters = operands
        widened = hidden.astype(jnp.float32)
        normed = (widened * lax.rsqrt(lax.optimization_barrier(jnp.mean(widened * widened, axis=-1, keepdims=True)) + 1e-05) * input_norm_scale).astype(jnp.bfloat16)
        position, slot_token_rows, dest_row, request = token_layout(lengths, adapters, adapter_holder_index, TOK_DEV, CAP)
        projected = jnp.dot(normed, query_key_value_weight, preferred_element_type=jnp.float32)
        down_token_rows = adapter_down_weight[slot_token_rows].astype(jnp.float32)
        low_rows = jnp.einsum('td,trd->tr', normed.astype(jnp.float32), down_token_rows).astype(jnp.bfloat16)
        up_token_rows = adapter_up_weight[slot_token_rows].astype(jnp.float32)
        low_wide = low_rows.astype(jnp.float32)
        delta_q = jnp.einsum('tr,tre->te', low_wide[:, :ADAPTER_RANK], up_token_rows[:, :, :query_column_width]).astype(jnp.bfloat16)
        delta_v = jnp.einsum('tr,tre->te', low_wide[:, ADAPTER_RANK:], up_token_rows[:, :, query_column_width:]).astype(jnp.bfloat16)
        query = projected[:, :query_column_width] + delta_q.astype(jnp.float32)
        key = projected[:, query_column_width:query_column_width + kv_width]
        value = (projected[:, query_column_width + kv_width:] + delta_v.astype(jnp.float32)).astype(jnp.bfloat16)
        query = rotate(query.reshape(TOK_DEV, HEADS, HEAD_DIM), position).astype(jnp.bfloat16)
        key = rotate(key.reshape(TOK_DEV, KV_HEADS, HEAD_DIM), position).astype(jnp.bfloat16)
        value = value.reshape(TOK_DEV, KV_HEADS, HEAD_DIM)
        attended = attend(query, key, value, request)
        return (widened + jnp.dot(attended, output_weight, preferred_element_type=jnp.float32)).astype(jnp.bfloat16)
    mixed = lax.map(one_block, (blocks, prompt_token_length, request_adapter_index))
    return mixed.reshape(block_count * TOK_DEV, MODEL_WIDTH)
```

```python
import functools
import math

import jax
import jax.numpy as jnp
import numpy as np
from jax import lax
from jax.experimental import pallas as pl
from jax.experimental.pallas import tpu as pltpu
from jax.sharding import PartitionSpec as P

HEADS = 16
KV_HEADS = 8
HEAD_DIM = 96
HALF = HEAD_DIM // 2
MAXLEN = 16
PAIR = 28
EPS = 1e-05
ROPE_THETA = 100000.0

GROUP = 4
BLOCK = GROUP * PAIR
LANES = 128
CHUNKS = 4
SHARD_HEADS = 8
CHUNK_ROWS = 2 * HEAD_DIM
LOG2E = 1.4426950408889634

F32 = jnp.float32
BF16 = jnp.bfloat16
VMEM = pl.BlockSpec(memory_space=pltpu.VMEM)
SMEM = pl.BlockSpec(memory_space=pltpu.SMEM)


def params(mib):
    return pltpu.CompilerParams(vmem_limit_bytes=mib * 1024 * 1024)


def dot_nt(left, right):
    return lax.dot_general(left, right, (((1,), (1,)), ((), ())), preferred_element_type=F32)


def dot_nn(left, right):
    return lax.dot_general(left, right, (((1,), (0,)), ((), ())), preferred_element_type=F32)


def rope_tables():
    inverse = np.exp(-math.log(ROPE_THETA) * 2.0 * np.arange(HALF, dtype=np.float64) / HEAD_DIM)
    angles = inverse[:, None] * np.arange(MAXLEN, dtype=np.float64)[None, :]
    cosine, sine = np.cos(angles), np.sin(angles)
    scale = LOG2E / math.sqrt(HEAD_DIM)
    return np.concatenate([cosine, sine, cosine * scale, sine * scale], axis=0).astype(np.float32)


def group_of(index):
    found = jnp.zeros_like(index)
    for edge in range(1, GROUP + 1):
        found = found + jnp.where(index >= edge * PAIR, 1, 0)
    return found


def transpose_kernel(w_ref, own_ref, *rest):
    send_refs, turned = rest[:CHUNKS], rest[CHUNKS]
    shard = lax.axis_index("ad")
    half = lax.rem(lax.axis_index("req"), 2)
    step = 4 * HEAD_DIM
    for g in range(w_ref.shape[1] // step):
        turned[g * step : (g + 1) * step, :] = w_ref[:, g * step : (g + 1) * step].T
    is_kv = shard >= 2
    for i in range(CHUNKS):
        for p in range(2):
            head = jnp.where(is_kv, i + 4 * p, 2 * i + p)
            own_ref[i, p] = turned[pl.ds(pl.multiple_of(head * HEAD_DIM, HEAD_DIM), HEAD_DIM), :]
        send_refs[i][...] = own_ref[i, half]


def norm_kernel(x_ref, scale_ref, table_ref, len_ref, adapter_ref, holder_ref, normed_ref, rope_ref, bias_ref, slot_ref):
    blocks = normed_ref.shape[0] // LANES
    gain = scale_ref[...]
    lane = lax.broadcasted_iota(jnp.int32, (1, LANES), 1)
    group = group_of(lane)
    within = lane - PAIR * group
    key_row = lax.broadcasted_iota(jnp.int32, (BLOCK, LANES), 0)
    query_col = lax.broadcasted_iota(jnp.int32, (BLOCK, LANES), 1)
    key_group = group_of(key_row)
    key_within = key_row - PAIR * key_group
    query_group = group_of(query_col)
    query_within = query_col - PAIR * query_group
    same_pair = (key_group == query_group) & (key_row <= query_col)
    dead = query_col >= BLOCK
    position_row = lax.broadcasted_iota(jnp.int32, (MAXLEN, LANES), 0)
    for b in range(blocks):
        rows = x_ref[b * BLOCK : (b + 1) * BLOCK, :].astype(F32)
        mean = jnp.mean(rows * rows, axis=-1, keepdims=True)
        normed = (rows * lax.rsqrt(mean + EPS) * gain).astype(BF16)
        normed_ref[b * LANES : b * LANES + BLOCK, :] = normed
        normed_ref[b * LANES + BLOCK : (b + 1) * LANES, :] = jnp.zeros((LANES - BLOCK, normed.shape[1]), BF16)
        first = jnp.zeros((1, LANES), jnp.int32)
        slot_first = jnp.zeros((1, LANES), jnp.int32)
        slot_second = jnp.zeros((1, LANES), jnp.int32)
        for g in range(GROUP):
            r = 2 * (GROUP * b + g)
            first = jnp.where(group == g, len_ref[0, r], first)
            slot_first = jnp.where(group == g, holder_ref[adapter_ref[0, r]], slot_first)
            slot_second = jnp.where(group == g, holder_ref[adapter_ref[0, r + 1]], slot_second)
        position = jnp.where(within < first, within, within - first)
        slot_ref[:, b * LANES : (b + 1) * LANES] = jnp.where(within < first, slot_first, slot_second)
        onehot = jnp.where(position_row == position, 1.0, 0.0).astype(F32)
        rope_ref[:, b * LANES : (b + 1) * LANES] = jnp.dot(
            table_ref[...], onehot, preferred_element_type=F32, precision=lax.Precision.HIGHEST
        )
        split = (key_within >= first) | (query_within < first)
        allowed = (same_pair & split) | dead
        bias_ref[b] = jnp.where(allowed, 0.0, -jnp.inf).astype(F32)


def make_low_kernel(adapters, rank):
    def kernel(down_ref, up_ref, normed_ref, slot_ref, low_ref, up_t_ref):
        low = dot_nt(down_ref[...], normed_ref[...]).astype(BF16)
        slot = slot_ref[...]
        for a in range(adapters):
            mine = slot == a
            for part in range(2):
                r = (2 * a + part) * rank
                low_ref[part, a * rank : (a + 1) * rank, :] = jnp.where(mine, low[r : r + rank, :], jnp.zeros((), BF16))
        step = 3 * LANES
        for g in range(up_ref.shape[1] // step):
            up_t_ref[g * step : (g + 1) * step, :] = up_ref[:, g * step : (g + 1) * step].T

    return kernel


def rotated(rows, rope_ref, base):
    cosine = rope_ref[base : base + HALF, :]
    sine = rope_ref[base + HALF : base + 2 * HALF, :]
    first, second = rows[:HALF, :], rows[HALF:, :]
    return (first * cosine - second * sine).astype(BF16), (second * cosine + first * sine).astype(BF16)


def put_rotated(target, index, rows, rope_ref, base):
    first, second = rotated(rows, rope_ref, base)
    target[index + (slice(0, HALF),)] = first
    target[index + (slice(HALF, HEAD_DIM),)] = second


def value_rows(up_t_ref, i, p):
    start = (HEADS + i + 4 * p) * HEAD_DIM
    return up_t_ref[start : start + HEAD_DIM, :]


def local_kernel(own_ref, near_ref, normed_ref, rope_ref, low_ref, up_t_ref, out_ref, total):
    shard = lax.axis_index("ad")
    side, core = shard // 2, lax.rem(shard, 2)
    normed = normed_ref[...]
    for w_ref, place in ((own_ref, core), (near_ref, 1 - core)):
        source = 2 * side + place
        total[...] = dot_nt(w_ref[...], normed)

        @pl.when(side == 0)
        def _():
            for i in range(CHUNKS):
                start = pl.multiple_of(place * (SHARD_HEADS * HEAD_DIM) + i * CHUNK_ROWS, CHUNK_ROWS)
                delta = dot_nn(up_t_ref[pl.ds(start, CHUNK_ROWS), :], low_ref[0])
                for p in range(2):
                    row = i * CHUNK_ROWS + p * HEAD_DIM
                    rows = total[row : row + HEAD_DIM, :] + delta[p * HEAD_DIM : (p + 1) * HEAD_DIM, :]
                    put_rotated(out_ref, (place, i, p), rows, rope_ref, 2 * HALF)

        @pl.when(source == 2)
        def _():
            for i in range(CHUNKS):
                for p in range(2):
                    row = i * CHUNK_ROWS + p * HEAD_DIM
                    put_rotated(out_ref, (place, i, p), total[row : row + HEAD_DIM, :], rope_ref, 0)

        @pl.when(source == 3)
        def _():
            for i in range(CHUNKS):
                for p in range(2):
                    row = i * CHUNK_ROWS + p * HEAD_DIM
                    delta = dot_nn(value_rows(up_t_ref, i, p), low_ref[1])
                    out_ref[place, i, p] = (total[row : row + HEAD_DIM, :] + delta).astype(BF16)


def make_step_kernel(i):
    def kernel(
        near_x, near_xy, far_x, far_xy, normed_ref, rope_ref, low_ref, up_t_ref, bias_ref, local_ref, out_ref,
        weight, total, parts, attended,
    ):
        shard = lax.axis_index("ad")
        half = lax.rem(lax.axis_index("req"), 2)
        side, core = shard // 2, lax.rem(shard, 2)
        weight[core, half] = near_x[...]
        weight[core, 1 - half] = near_xy[...]
        weight[1 - core, half] = far_x[...]
        weight[1 - core, 1 - half] = far_xy[...]
        rows = weight[...].reshape(4 * HEAD_DIM, weight.shape[-1])
        total[...] = dot_nt(rows, normed_ref[...])

        @pl.when(side == 0)
        def _():
            for p in range(2):
                put_rotated(parts, (2, p), total[p * HEAD_DIM : (p + 1) * HEAD_DIM, :], rope_ref, 0)
                delta = dot_nn(value_rows(up_t_ref, i, p), low_ref[1])
                parts[3, p] = (total[(2 + p) * HEAD_DIM : (3 + p) * HEAD_DIM, :] + delta).astype(BF16)
                for c in range(2):
                    parts[c, p] = local_ref[c, 0, p]

        @pl.when(side == 1)
        def _():
            for c in range(2):
                start = c * SHARD_HEADS * HEAD_DIM + i * CHUNK_ROWS
                delta = dot_nn(up_t_ref[start : start + CHUNK_ROWS, :], low_ref[0])
                for p in range(2):
                    row = (2 * c + p) * HEAD_DIM
                    rows = total[row : row + HEAD_DIM, :] + delta[p * HEAD_DIM : (p + 1) * HEAD_DIM, :]
                    put_rotated(parts, (c, p), rows, rope_ref, 2 * HALF)
                    parts[2 + c, p] = local_ref[c, 0, p]

        blocks = bias_ref.shape[0]
        for b in range(blocks):
            lanes = slice(b * LANES, (b + 1) * LANES)
            bias = jnp.concatenate([bias_ref[b], bias_ref[b]], axis=1)
            for p in range(2):
                key = parts[2, p, :, lanes].T[:BLOCK, :]
                query = jnp.concatenate([parts[p, 0, :, lanes], parts[p, 1, :, lanes]], axis=1)
                scores = dot_nn(key, query) + bias
                weights = jnp.exp2(scores - jnp.max(scores, axis=0, keepdims=True))
                probs = (weights * (1.0 / jnp.sum(weights, axis=0, keepdims=True))).astype(BF16)
                probs = jnp.concatenate([probs, jnp.zeros((LANES - BLOCK, 2 * LANES), BF16)], axis=0)
                result = dot_nn(parts[3, p, :, lanes], probs).astype(BF16)
                for h in range(2):
                    row = (2 * p + h) * HEAD_DIM
                    attended[row : row + HEAD_DIM, :] = result[:, h * LANES : (h + 1) * LANES]
            out_ref[b * BLOCK : (b + 1) * BLOCK, :] = attended[...].T[:BLOCK, :]

    return kernel


def mix_kernel(x_ref, w_ref, *rest):
    parts, out_ref = rest[:CHUNKS], rest[CHUNKS]
    half = SHARD_HEADS * HEAD_DIM
    columns = 2 * LANES
    for n in range(out_ref.shape[1] // columns):
        cols = slice(n * columns, (n + 1) * columns)
        total = x_ref[:, cols].astype(F32)
        for i in range(CHUNKS):
            weight = jnp.concatenate(
                [w_ref[c * half + i * CHUNK_ROWS : c * half + (i + 1) * CHUNK_ROWS, cols] for c in range(2)], axis=0
            )
            total = total + dot_nn(parts[i][...], weight)
        out_ref[:, cols] = total.astype(BF16)


def body(
    layer_input_hidden,
    input_norm_scale,
    query_key_value_weight,
    output_weight,
    adapter_down_weight,
    adapter_up_weight,
    prompt_token_length,
    request_adapter_index,
    adapter_holder_index,
):
    tokens, width = layer_input_hidden.shape
    blocks = tokens // BLOCK
    padded = blocks * LANES
    adapters = adapter_holder_index.shape[0]
    rank = adapter_up_weight.shape[1]
    shard_cols = query_key_value_weight.shape[1]
    shards, requests = lax.axis_size("ad"), lax.axis_size("req")
    other_side = [(a, a ^ 2) for a in range(shards)]
    other_core = [(a, a ^ 1) for a in range(shards)]
    other_row = [(r, r ^ 1) for r in range(requests)]

    down = lax.all_gather(adapter_down_weight, "req", axis=0, tiled=True).reshape(adapters * 2 * rank, width)
    up = lax.all_gather(adapter_up_weight, "req", axis=0, tiled=True).reshape(adapters * rank, adapter_up_weight.shape[2])

    head = jax.ShapeDtypeStruct((HEAD_DIM, width), BF16)
    turned = pl.pallas_call(
        transpose_kernel,
        out_shape=[jax.ShapeDtypeStruct((CHUNKS, 2, HEAD_DIM, width), BF16)] + [head] * CHUNKS,
        in_specs=[VMEM],
        out_specs=[VMEM] * (CHUNKS + 1),
        scratch_shapes=[pltpu.VMEM((shard_cols, width), BF16)],
        compiler_params=params(24),
        name="turn_weight",
    )(query_key_value_weight)
    own, sends = turned[0], turned[1:]
    near = lax.ppermute(own, "ad", other_core)
    remote = []
    for i in range(CHUNKS):
        near_x = lax.ppermute(sends[i], "ad", other_side)
        near_xy = lax.ppermute(near_x, "req", other_row)
        far_x = lax.ppermute(near_x, "ad", other_core)
        far_xy = lax.ppermute(near_xy, "ad", other_core)
        remote.append((near_x, near_xy, far_x, far_xy))

    normed, rope, bias, slot = pl.pallas_call(
        norm_kernel,
        out_shape=[
            jax.ShapeDtypeStruct((padded, width), BF16),
            jax.ShapeDtypeStruct((4 * HALF, padded), F32),
            jax.ShapeDtypeStruct((blocks, BLOCK, LANES), F32),
            jax.ShapeDtypeStruct((1, padded), jnp.int32),
        ],
        in_specs=[VMEM] * 3 + [SMEM] * 3,
        out_specs=[VMEM] * 4,
        compiler_params=params(24),
        name="norm_tokens",
    )(
        layer_input_hidden, input_norm_scale.reshape(1, width), jnp.asarray(rope_tables()),
        prompt_token_length, request_adapter_index, adapter_holder_index,
    )

    low, up_t = pl.pallas_call(
        make_low_kernel(adapters, rank),
        out_shape=[
            jax.ShapeDtypeStruct((2, adapters * rank, padded), BF16),
            jax.ShapeDtypeStruct((up.shape[1], adapters * rank), BF16),
        ],
        in_specs=[VMEM] * 4,
        out_specs=[VMEM] * 2,
        compiler_params=params(48 if adapters > 8 else 24),
        name="adapter_low",
    )(down, up, normed, slot)

    local = pl.pallas_call(
        local_kernel,
        out_shape=jax.ShapeDtypeStruct((2, CHUNKS, 2, HEAD_DIM, padded), BF16),
        in_specs=[VMEM] * 6,
        out_specs=VMEM,
        scratch_shapes=[pltpu.VMEM((shard_cols, padded), F32)],
        compiler_params=params(40),
        name="project_local",
    )(own.reshape(shard_cols, width), near.reshape(shard_cols, width), normed, rope, low, up_t)

    attended = []
    for i in range(CHUNKS):
        attended.append(
            pl.pallas_call(
                make_step_kernel(i),
                out_shape=jax.ShapeDtypeStruct((tokens, 4 * HEAD_DIM), BF16),
                grid=(1,),
                in_specs=[VMEM] * 9
                + [pl.BlockSpec((2, 1, 2, HEAD_DIM, padded), functools.partial(lambda k, _: (0, k, 0, 0, 0), i))],
                out_specs=VMEM,
                scratch_shapes=[
                    pltpu.VMEM((2, 2, HEAD_DIM, width), BF16),
                    pltpu.VMEM((4 * HEAD_DIM, padded), F32),
                    pltpu.VMEM((4, 2, HEAD_DIM, padded), BF16),
                    pltpu.VMEM((4 * HEAD_DIM, LANES), BF16),
                ],
                compiler_params=params(40),
                name=f"attend_{i}",
            )(*remote[i], normed, rope, low, up_t, bias, local)
        )

    return pl.pallas_call(
        mix_kernel,
        out_shape=jax.ShapeDtypeStruct((tokens, width), BF16),
        in_specs=[VMEM] * (2 + CHUNKS),
        out_specs=VMEM,
        compiler_params=params(32),
        name="mix_output",
    )(layer_input_hidden, output_weight, *attended)


def solution(mesh):
    placed = (
        P(("req", "ad"), None),
        P(),
        P(None, "ad"),
        P(),
        P("req", None, None),
        P("req", None, None),
        P(("req", "ad"), None),
        P(("req", "ad"), None),
        P(),
    )
    return jax.shard_map(
        body, mesh=mesh, in_specs=placed, out_specs=P(("req", "ad"), None), check_vma=False
    )
```

```python
import math

import jax
import jax.numpy as jnp
import numpy as np
from jax import lax
from jax.experimental import pallas as pl
from jax.experimental.pallas import tpu as pltpu
from jax.sharding import PartitionSpec as P

HEADS = 16
KV_HEADS = 8
HEAD_DIM = 96
HALF = HEAD_DIM // 2
MAXLEN = 16
PAIR = 28
EPS = 1e-05
ROPE_THETA = 100000.0

GROUP = 4
BLOCK = GROUP * PAIR
LANES = 128
CHUNKS = 4
SHARD_HEADS = 8
CHUNK_ROWS = 2 * HEAD_DIM
LOG2E = 1.4426950408889634

F32 = jnp.float32
BF16 = jnp.bfloat16
VMEM = pl.BlockSpec(memory_space=pltpu.VMEM)
SMEM = pl.BlockSpec(memory_space=pltpu.SMEM)


def params(mib):
    return pltpu.CompilerParams(vmem_limit_bytes=mib * 1024 * 1024)


def dot_nt(left, right):
    return lax.dot_general(left, right, (((1,), (1,)), ((), ())), preferred_element_type=F32)


def dot_nn(left, right):
    return lax.dot_general(left, right, (((1,), (0,)), ((), ())), preferred_element_type=F32)


def rope_tables():
    inverse = np.exp(-math.log(ROPE_THETA) * 2.0 * np.arange(HALF, dtype=np.float64) / HEAD_DIM)
    angles = inverse[:, None] * np.arange(MAXLEN, dtype=np.float64)[None, :]
    cosine, sine = np.cos(angles), np.sin(angles)
    scale = LOG2E / math.sqrt(HEAD_DIM)
    return np.concatenate([cosine, sine, cosine * scale, sine * scale], axis=0).astype(np.float32)


def group_of(index):
    found = jnp.zeros_like(index)
    for edge in range(1, GROUP + 1):
        found = found + jnp.where(index >= edge * PAIR, 1, 0)
    return found


def pack_kernel(down_ref, up_ref, out_ref):
    core = lax.rem(lax.axis_index("ad"), 2)
    rank, width = up_ref.shape[1], down_ref.shape[2]
    value_cols = up_ref.shape[2] - width

    @pl.when(core == 0)
    def _():
        out_ref[...] = down_ref[...]

    @pl.when(core == 1)
    def _():
        out_ref[0, :rank, :] = up_ref[0, :, :width]
        out_ref[0, rank:, :value_cols] = up_ref[0, :, width:]
        out_ref[0, rank:, value_cols:] = jnp.zeros((rank, width - value_cols), BF16)


def turn_kernel(w_ref, own_ref, *rest):
    send_refs, turned = rest[:CHUNKS], rest[CHUNKS]
    shard = lax.axis_index("ad")
    half = lax.rem(lax.axis_index("req"), 2)
    step = 4 * HEAD_DIM
    for g in range(w_ref.shape[1] // step):
        turned[g * step : (g + 1) * step, :] = w_ref[:, g * step : (g + 1) * step].T
    is_kv = shard >= 2
    for i in range(CHUNKS):
        for p in range(2):
            head = jnp.where(is_kv, i + 4 * p, 2 * i + p)
            own_ref[i, p] = turned[pl.ds(pl.multiple_of(head * HEAD_DIM, HEAD_DIM), HEAD_DIM), :]
        send_refs[i][...] = own_ref[i, half]


def norm_kernel(x_ref, scale_ref, table_ref, len_ref, adapter_ref, holder_ref, normed_ref, rope_ref, bias_ref, slot_ref):
    blocks = normed_ref.shape[0] // LANES
    gain = scale_ref[...]
    lane = lax.broadcasted_iota(jnp.int32, (1, LANES), 1)
    group = group_of(lane)
    within = lane - PAIR * group
    key_row = lax.broadcasted_iota(jnp.int32, (BLOCK, LANES), 0)
    query_col = lax.broadcasted_iota(jnp.int32, (BLOCK, LANES), 1)
    key_group = group_of(key_row)
    key_within = key_row - PAIR * key_group
    query_group = group_of(query_col)
    query_within = query_col - PAIR * query_group
    same_pair = (key_group == query_group) & (key_row <= query_col)
    dead = query_col >= BLOCK
    position_row = lax.broadcasted_iota(jnp.int32, (MAXLEN, LANES), 0)
    for b in range(blocks):
        rows = x_ref[b * BLOCK : (b + 1) * BLOCK, :].astype(F32)
        mean = jnp.mean(rows * rows, axis=-1, keepdims=True)
        normed = (rows * lax.rsqrt(mean + EPS) * gain).astype(BF16)
        normed_ref[b * LANES : b * LANES + BLOCK, :] = normed
        normed_ref[b * LANES + BLOCK : (b + 1) * LANES, :] = jnp.zeros((LANES - BLOCK, normed.shape[1]), BF16)
        first = jnp.zeros((1, LANES), jnp.int32)
        slot_first = jnp.zeros((1, LANES), jnp.int32)
        slot_second = jnp.zeros((1, LANES), jnp.int32)
        for g in range(GROUP):
            r = 2 * (GROUP * b + g)
            first = jnp.where(group == g, len_ref[0, r], first)
            slot_first = jnp.where(group == g, holder_ref[adapter_ref[0, r]], slot_first)
            slot_second = jnp.where(group == g, holder_ref[adapter_ref[0, r + 1]], slot_second)
        position = jnp.where(within < first, within, within - first)
        slot_ref[:, b * LANES : (b + 1) * LANES] = jnp.where(within < first, slot_first, slot_second)
        onehot = jnp.where(position_row == position, 1.0, 0.0).astype(F32)
        rope_ref[:, b * LANES : (b + 1) * LANES] = jnp.dot(
            table_ref[...], onehot, preferred_element_type=F32, precision=lax.Precision.HIGHEST
        )
        split = (key_within >= first) | (query_within < first)
        allowed = (same_pair & split) | dead
        bias_ref[b] = jnp.where(allowed, 0.0, -jnp.inf).astype(F32)


def make_low_kernel(codes, rank):
    def kernel(mine_ref, other_ref, normed_ref, slot_ref, low_ref, up_t_ref, adapter):
        core = lax.rem(lax.axis_index("ad"), 2)
        me = lax.axis_index("req")
        count, rows, width = mine_ref.shape
        adapter[core] = mine_ref[...]
        adapter[1 - core] = other_ref[...]
        low = dot_nt(adapter[0].reshape(count * rows, width), normed_ref[...]).astype(BF16)
        slot = slot_ref[...]
        for j, code in enumerate(codes):
            mine = slot == me ^ code
            for part in range(2):
                r = (2 * j + part) * rank
                low_ref[part, j * rank : (j + 1) * rank, :] = jnp.where(mine, low[r : r + rank, :], jnp.zeros((), BF16))
        for part in range(2):
            stop = min(width, up_t_ref.shape[0] - part * width)
            step = 3 * LANES
            for start in range(0, stop, step):
                piece = adapter[1, :, part * rank : (part + 1) * rank, start : start + step]
                up_t_ref[part * width + start : part * width + start + step, :] = piece.reshape(count * rank, step).T

    return kernel


def project_kernel(w_ref, normed_ref, *out_refs):
    for i, out_ref in enumerate(out_refs):
        out_ref[...] = dot_nt(w_ref[i].reshape(CHUNK_ROWS, w_ref.shape[-1]), normed_ref[...])


def project_remote_kernel(near_x, near_xy, far_x, far_xy, normed_ref, out_ref, weight):
    half = lax.rem(lax.axis_index("req"), 2)
    core = lax.rem(lax.axis_index("ad"), 2)
    weight[core, half] = near_x[...]
    weight[core, 1 - half] = near_xy[...]
    weight[1 - core, half] = far_x[...]
    weight[1 - core, 1 - half] = far_xy[...]
    rows = dot_nt(weight[...].reshape(4 * HEAD_DIM, weight.shape[-1]), normed_ref[...])
    out_ref[...] = rows.reshape(out_ref.shape)


def put_rotated(target, index, rows, rope_ref, base):
    cosine = rope_ref[base : base + HALF, :]
    sine = rope_ref[base + HALF : base + 2 * HALF, :]
    first, second = rows[:HALF, :], rows[HALF:, :]
    target[index + (slice(0, HALF),)] = (first * cosine - second * sine).astype(BF16)
    target[index + (slice(HALF, HEAD_DIM),)] = (second * cosine + first * sine).astype(BF16)


def make_attend_kernel(i):
    def fill(query_rows, key_rows, value_rows, rope_ref, low_ref, up_t_ref, parts):
        for c in range(2):
            start = c * SHARD_HEADS * HEAD_DIM + i * CHUNK_ROWS
            delta = dot_nn(up_t_ref[start : start + CHUNK_ROWS, :], low_ref[0])
            for p in range(2):
                put_rotated(parts, (c, p), query_rows(c, p) + delta[p * HEAD_DIM : (p + 1) * HEAD_DIM, :], rope_ref, 2 * HALF)
        for p in range(2):
            start = (HEADS + i + 4 * p) * HEAD_DIM
            delta = dot_nn(up_t_ref[start : start + HEAD_DIM, :], low_ref[1])
            put_rotated(parts, (2, p), key_rows(p), rope_ref, 0)
            parts[3, p] = (value_rows(p) + delta).astype(BF16)

    def kernel(own_ref, near_ref, remote_ref, rope_ref, low_ref, up_t_ref, bias_ref, out_ref, local, parts, attended):
        shard = lax.axis_index("ad")
        side, core = shard // 2, lax.rem(shard, 2)
        local[core] = own_ref[...].reshape(local.shape[1:])
        local[1 - core] = near_ref[...].reshape(local.shape[1:])

        @pl.when(side == 0)
        def _():
            fill(
                lambda c, p: local[c, p], lambda p: remote_ref[0, p], lambda p: remote_ref[1, p],
                rope_ref, low_ref, up_t_ref, parts,
            )

        @pl.when(side == 1)
        def _():
            fill(
                lambda c, p: remote_ref[c, p], lambda p: local[0, p], lambda p: local[1, p],
                rope_ref, low_ref, up_t_ref, parts,
            )

        def lanes(b):
            return slice(b * LANES, (b + 1) * LANES)

        def score(b, p):
            key = parts[2, p, :, lanes(b)].T[:BLOCK, :]
            query = jnp.concatenate([parts[p, 0, :, lanes(b)], parts[p, 1, :, lanes(b)]], axis=1)
            return dot_nn(key, query)

        def soften(b, scores):
            bias = bias_ref[b]
            scores = scores + jnp.concatenate([bias, bias], axis=1)
            weights = jnp.exp2(scores - jnp.max(scores, axis=0, keepdims=True))
            probs = (weights * (1.0 / jnp.sum(weights, axis=0, keepdims=True))).astype(BF16)
            return jnp.concatenate([probs, jnp.zeros((LANES - BLOCK, 2 * LANES), BF16)], axis=0)

        def mingle(b, p, probs):
            result = dot_nn(parts[3, p, :, lanes(b)], probs).astype(BF16)
            for h in range(2):
                row = (2 * p + h) * HEAD_DIM
                attended[row : row + HEAD_DIM, lanes(b)] = result[:, h * LANES : (h + 1) * LANES]

        work = [(b, p) for b in range(bias_ref.shape[0]) for p in range(2)]
        ahead = 2
        scores = [score(*work[n]) for n in range(ahead)]
        probs = {}
        for n, (b, p) in enumerate(work):
            if n + ahead < len(work):
                scores.append(score(*work[n + ahead]))
            probs[n] = soften(b, scores[n])
            if n >= 1:
                mingle(*work[n - 1], probs.pop(n - 1))
        mingle(*work[-1], probs.pop(len(work) - 1))
        for b in range(bias_ref.shape[0]):
            out_ref[b * BLOCK : (b + 1) * BLOCK, :] = attended[:, lanes(b)].T[:BLOCK, :]

    return kernel


def mix_kernel(x_ref, w_ref, *rest):
    parts, out_ref = rest[:CHUNKS], rest[CHUNKS]
    half = SHARD_HEADS * HEAD_DIM
    columns = 2 * LANES
    attended = jnp.concatenate([part[...] for part in parts], axis=1)
    for n in range(out_ref.shape[1] // columns):
        cols = slice(n * columns, (n + 1) * columns)
        weight = jnp.concatenate(
            [
                w_ref[c * half + i * CHUNK_ROWS : c * half + (i + 1) * CHUNK_ROWS, cols]
                for i in range(CHUNKS)
                for c in range(2)
            ],
            axis=0,
        )
        out_ref[:, cols] = (x_ref[:, cols].astype(F32) + dot_nn(attended, weight)).astype(BF16)


def after(value, *others):
    return lax.optimization_barrier((value,) + others)[0]


def cost(flops, size):
    return pl.CostEstimate(flops=int(flops), bytes_accessed=int(size), transcendentals=0)


def body(
    layer_input_hidden,
    input_norm_scale,
    query_key_value_weight,
    output_weight,
    adapter_down_weight,
    adapter_up_weight,
    prompt_token_length,
    request_adapter_index,
    adapter_holder_index,
):
    tokens, width = layer_input_hidden.shape
    blocks = tokens // BLOCK
    padded = blocks * LANES
    rank = adapter_up_weight.shape[1]
    features = adapter_up_weight.shape[2]
    shard_cols = query_key_value_weight.shape[1]
    shards, requests = lax.axis_size("ad"), lax.axis_size("req")
    other_side = [(a, a ^ 2) for a in range(shards)]
    other_core = [(a, a ^ 1) for a in range(shards)]

    def other_row(bit):
        return [(r, r ^ bit) for r in range(requests)]

    packed = pl.pallas_call(
        pack_kernel,
        out_shape=jax.ShapeDtypeStruct((1, 2 * rank, width), BF16),
        in_specs=[VMEM] * 2,
        out_specs=VMEM,
        name="pack_adapter",
    )(adapter_down_weight, adapter_up_weight)

    head = jax.ShapeDtypeStruct((HEAD_DIM, width), BF16)
    turned = pl.pallas_call(
        turn_kernel,
        out_shape=[jax.ShapeDtypeStruct((CHUNKS, 2, HEAD_DIM, width), BF16)] + [head] * CHUNKS,
        in_specs=[VMEM],
        out_specs=[VMEM] * (CHUNKS + 1),
        scratch_shapes=[pltpu.VMEM((shard_cols, width), BF16)],
        compiler_params=params(24),
        name="turn_weight",
    )(query_key_value_weight)
    own, sends = turned[0], turned[1:]

    normed, rope, bias, slot = pl.pallas_call(
        norm_kernel,
        out_shape=[
            jax.ShapeDtypeStruct((padded, width), BF16),
            jax.ShapeDtypeStruct((4 * HALF, padded), F32),
            jax.ShapeDtypeStruct((blocks, BLOCK, LANES), F32),
            jax.ShapeDtypeStruct((1, padded), jnp.int32),
        ],
        in_specs=[VMEM] * 3 + [SMEM] * 3,
        out_specs=[VMEM] * 4,
        compiler_params=params(24),
        cost_estimate=cost(2e9, 8e6),
        name="norm_tokens",
    )(
        layer_input_hidden, input_norm_scale.reshape(1, width), jnp.asarray(rope_tables()),
        prompt_token_length, request_adapter_index, adapter_holder_index,
    )

    def project(weight, name):
        return pl.pallas_call(
            project_kernel,
            out_shape=[jax.ShapeDtypeStruct((CHUNK_ROWS, padded), F32)] * CHUNKS,
            in_specs=[VMEM] * 2,
            out_specs=[VMEM] * CHUNKS,
            compiler_params=params(24),
            cost_estimate=cost(2 * shard_cols * padded * width, 9e6),
            name=name,
        )(weight, normed)

    def project_remote(i, pieces, token):
        return pl.pallas_call(
            project_remote_kernel,
            out_shape=jax.ShapeDtypeStruct((2, 2, HEAD_DIM, padded), F32),
            in_specs=[VMEM] * 5,
            out_specs=VMEM,
            scratch_shapes=[pltpu.VMEM((2, 2, HEAD_DIM, width), BF16)],
            compiler_params=params(24),
            cost_estimate=cost(2 * 4 * HEAD_DIM * padded * width, 6e6),
            name=f"project_{i}",
        )(*pieces, after(normed, token))

    def attend(i, rows):
        return pl.pallas_call(
            make_attend_kernel(i),
            out_shape=jax.ShapeDtypeStruct((tokens, 4 * HEAD_DIM), BF16),
            in_specs=[VMEM] * 7,
            out_specs=VMEM,
            scratch_shapes=[
                pltpu.VMEM((2, 2, HEAD_DIM, padded), F32),
                pltpu.VMEM((4, 2, HEAD_DIM, padded), BF16),
                pltpu.VMEM((4 * HEAD_DIM, padded), BF16),
            ],
            compiler_params=params(32),
            cost_estimate=cost(4e9, 8e6),
            name=f"attend_{i}",
        )(own_parts[i], near_parts[i], rows, rope, low, up_t, bias)

    def gather_adapters(packed, codes, bit, token):
        got = lax.ppermute(after(packed, token), "req", other_row(bit))
        return jnp.concatenate([packed, got], axis=0), codes + [code ^ bit for code in codes]

    bits = []
    while 2 ** len(bits) < requests:
        bits.append(2 ** len(bits))
    bits = bits[:0:-1][:1] + bits[:1] + bits[:0:-1][1:]
    codes = [0]

    def across(i):
        return lax.ppermute(sends[i], "ad", other_side)

    def along(piece, token):
        return lax.ppermute(after(piece, token), "req", other_row(1))

    def beside(piece, token):
        return lax.ppermute(after(piece, token), "ad", other_core)

    near = beside(own, own)
    x_pieces = [across(i) for i in range(CHUNKS)]
    xy_pieces, far_x, far_xy = [None] * CHUNKS, [None] * CHUNKS, [None] * CHUNKS

    def forward(i, token):
        xy_pieces[i] = along(x_pieces[i], token)
        far_x[i] = beside(x_pieces[i], token)

    def arrived(i):
        return x_pieces[i], xy_pieces[i], far_x[i], far_xy[i]

    for bit in bits[:1]:
        packed, codes = gather_adapters(packed, codes, bit, packed)
    forward(0, normed)
    for bit in bits[1:2]:
        packed, codes = gather_adapters(packed, codes, bit, normed)
    own_parts = project(after(own, normed), "project_own")
    for bit in bits[2:]:
        packed, codes = gather_adapters(packed, codes, bit, own_parts[0])
    forward(1, own_parts[0])
    near_parts = project(after(near, own_parts[0]), "project_near")
    far_xy[0] = beside(xy_pieces[0], near_parts[0])
    packed_other = beside(packed, near_parts[0])
    forward(2, near_parts[0])
    rows = project_remote(0, arrived(0), near_parts[0])
    far_xy[1] = beside(xy_pieces[1], rows)
    low, up_t = pl.pallas_call(
        make_low_kernel(codes, rank),
        out_shape=[
            jax.ShapeDtypeStruct((2, len(codes) * rank, padded), BF16),
            jax.ShapeDtypeStruct((features, len(codes) * rank), BF16),
        ],
        in_specs=[VMEM] * 4,
        out_specs=[VMEM] * 2,
        scratch_shapes=[pltpu.VMEM((2,) + packed.shape, BF16)],
        compiler_params=params(56 if len(codes) > 8 else 24),
        cost_estimate=cost(1e9, 8e6),
        name="adapter_low",
    )(packed, packed_other, after(normed, rows), slot)
    forward(3, rows)
    attended = [attend(0, rows)]
    far_xy[2] = beside(xy_pieces[2], attended[0])
    rows = project_remote(1, arrived(1), attended[0])
    attended.append(attend(1, rows))
    far_xy[3] = beside(xy_pieces[3], attended[1])
    rows = project_remote(2, arrived(2), attended[1])
    attended.append(attend(2, rows))
    rows = project_remote(3, arrived(3), attended[2])
    attended.append(attend(3, rows))

    return pl.pallas_call(
        mix_kernel,
        out_shape=jax.ShapeDtypeStruct((tokens, width), BF16),
        in_specs=[VMEM] * (2 + CHUNKS),
        out_specs=VMEM,
        compiler_params=params(32),
        cost_estimate=cost(2 * tokens * width * width, 13e6),
        name="mix_output",
    )(layer_input_hidden, output_weight, *attended)


def solution(mesh):
    placed = (
        P(("req", "ad"), None),
        P(),
        P(None, "ad"),
        P(),
        P("req", None, None),
        P("req", None, None),
        P(("req", "ad"), None),
        P(("req", "ad"), None),
        P(),
    )
    return jax.shard_map(
        body, mesh=mesh, in_specs=placed, out_specs=P(("req", "ad"), None), check_vma=False
    )
```

```python
import math

import jax
import jax.numpy as jnp
import numpy as np
from jax import lax
from jax.experimental import pallas as pl
from jax.experimental.pallas import tpu as pltpu
from jax.sharding import PartitionSpec as P

HEADS = 16
KV_HEADS = 8
HEAD_DIM = 96
HALF = HEAD_DIM // 2
MAXLEN = 16
PAIR = 28
EPS = 1e-05
ROPE_THETA = 100000.0

GROUP = 4
BLOCK = GROUP * PAIR
LANES = 128
CHUNKS = 4
SHARD_HEADS = 8
CHUNK_ROWS = 2 * HEAD_DIM
LOG2E = 1.4426950408889634

F32 = jnp.float32
BF16 = jnp.bfloat16
VMEM = pl.BlockSpec(memory_space=pltpu.VMEM)
SMEM = pl.BlockSpec(memory_space=pltpu.SMEM)


def params(mib):
    return pltpu.CompilerParams(vmem_limit_bytes=mib * 1024 * 1024)


def dot_nt(left, right):
    return lax.dot_general(left, right, (((1,), (1,)), ((), ())), preferred_element_type=F32)


def dot_nn(left, right):
    return lax.dot_general(left, right, (((1,), (0,)), ((), ())), preferred_element_type=F32)


def rope_tables():
    inverse = np.exp(-math.log(ROPE_THETA) * 2.0 * np.arange(HALF, dtype=np.float64) / HEAD_DIM)
    angles = inverse[:, None] * np.arange(MAXLEN, dtype=np.float64)[None, :]
    cosine, sine = np.cos(angles), np.sin(angles)
    scale = LOG2E / math.sqrt(HEAD_DIM)
    return np.concatenate([cosine, sine, cosine * scale, sine * scale], axis=0).astype(np.float32)


def group_of(index):
    found = jnp.zeros_like(index)
    for edge in range(1, GROUP + 1):
        found = found + jnp.where(index >= edge * PAIR, 1, 0)
    return found


def turn_kernel(w_ref, down_ref, up_ref, own_ref, pack_ref, *rest):
    send_refs, turned = rest[:CHUNKS], rest[CHUNKS]
    shard = lax.axis_index("ad")
    half = lax.rem(lax.axis_index("req"), 2)
    step = 4 * HEAD_DIM
    for g in range(w_ref.shape[1] // step):
        turned[g * step : (g + 1) * step, :] = w_ref[:, g * step : (g + 1) * step].T
    is_kv = shard >= 2
    for i in range(CHUNKS):
        for p in range(2):
            head = jnp.where(is_kv, i + 4 * p, 2 * i + p)
            own_ref[i, p] = turned[pl.ds(pl.multiple_of(head * HEAD_DIM, HEAD_DIM), HEAD_DIM), :]
        send_refs[i][...] = own_ref[i, half]
    core = lax.rem(shard, 2)
    rank, width = up_ref.shape[1], down_ref.shape[2]
    value_cols = up_ref.shape[2] - width

    @pl.when(core == 0)
    def _():
        pack_ref[...] = down_ref[...]

    @pl.when(core == 1)
    def _():
        pack_ref[0, :rank, :] = up_ref[0, :, :width]
        pack_ref[0, rank:, :value_cols] = up_ref[0, :, width:]
        pack_ref[0, rank:, value_cols:] = jnp.zeros((rank, width - value_cols), BF16)


def norm_kernel(x_ref, scale_ref, table_ref, len_ref, adapter_ref, holder_ref, normed_ref, rope_ref, bias_ref, slot_ref):
    b = pl.program_id(0)
    lane = lax.broadcasted_iota(jnp.int32, (1, LANES), 1)
    group = group_of(lane)
    within = lane - PAIR * group
    key_row = lax.broadcasted_iota(jnp.int32, (BLOCK, LANES), 0)
    query_col = lax.broadcasted_iota(jnp.int32, (BLOCK, LANES), 1)
    key_group = group_of(key_row)
    key_within = key_row - PAIR * key_group
    query_group = group_of(query_col)
    query_within = query_col - PAIR * query_group
    same_pair = (key_group == query_group) & (key_row <= query_col)
    dead = query_col >= BLOCK
    position_row = lax.broadcasted_iota(jnp.int32, (MAXLEN, LANES), 0)

    rows = x_ref[...].astype(F32)
    mean = jnp.mean(rows * rows, axis=-1, keepdims=True)
    normed_ref[:BLOCK, :] = (rows * lax.rsqrt(mean + EPS) * scale_ref[...]).astype(BF16)
    normed_ref[BLOCK:, :] = jnp.zeros((LANES - BLOCK, rows.shape[1]), BF16)
    first = jnp.zeros((1, LANES), jnp.int32)
    slot_first = jnp.zeros((1, LANES), jnp.int32)
    slot_second = jnp.zeros((1, LANES), jnp.int32)
    for g in range(GROUP):
        r = 2 * (GROUP * b + g)
        first = jnp.where(group == g, len_ref[0, r], first)
        slot_first = jnp.where(group == g, holder_ref[adapter_ref[0, r]], slot_first)
        slot_second = jnp.where(group == g, holder_ref[adapter_ref[0, r + 1]], slot_second)
    position = jnp.where(within < first, within, within - first)
    slot_ref[...] = jnp.where(within < first, slot_first, slot_second)
    onehot = jnp.where(position_row == position, 1.0, 0.0).astype(F32)
    rope_ref[...] = jnp.dot(table_ref[...], onehot, preferred_element_type=F32, precision=lax.Precision.HIGHEST)
    split = (key_within >= first) | (query_within < first)
    bias_ref[0] = jnp.where((same_pair & split) | dead, 0.0, -jnp.inf).astype(F32)


def make_low_kernel(codes, rank):
    def kernel(mine_ref, other_ref, normed_ref, slot_ref, low_ref, up_t_ref, adapter):
        core = lax.rem(lax.axis_index("ad"), 2)
        me = lax.axis_index("req")
        count, rows, width = mine_ref.shape
        adapter[core] = mine_ref[...]
        adapter[1 - core] = other_ref[...]
        low = dot_nt(adapter[0].reshape(count * rows, width), normed_ref[...]).astype(BF16)
        slot = slot_ref[...]
        for j, code in enumerate(codes):
            mine = slot == me ^ code
            for part in range(2):
                r = (2 * j + part) * rank
                low_ref[part, j * rank : (j + 1) * rank, :] = jnp.where(mine, low[r : r + rank, :], jnp.zeros((), BF16))
        for part in range(2):
            stop = min(width, up_t_ref.shape[0] - part * width)
            step = 3 * LANES
            for start in range(0, stop, step):
                piece = adapter[1, :, part * rank : (part + 1) * rank, start : start + step]
                up_t_ref[part * width + start : part * width + start + step, :] = piece.reshape(count * rank, step).T

    return kernel


def project_kernel(w_ref, normed_ref, *out_refs):
    rows = dot_nt(w_ref[...].reshape(CHUNKS * CHUNK_ROWS, w_ref.shape[-1]), normed_ref[...])
    for i, out_ref in enumerate(out_refs):
        out_ref[...] = rows[i * CHUNK_ROWS : (i + 1) * CHUNK_ROWS, :]


def project_remote_kernel(near_x, near_xy, far_x, far_xy, normed_ref, out_ref, weight):
    half = lax.rem(lax.axis_index("req"), 2)
    core = lax.rem(lax.axis_index("ad"), 2)
    weight[core, half] = near_x[...]
    weight[core, 1 - half] = near_xy[...]
    weight[1 - core, half] = far_x[...]
    weight[1 - core, 1 - half] = far_xy[...]
    rows = dot_nt(weight[...].reshape(4 * HEAD_DIM, weight.shape[-1]), normed_ref[...])
    out_ref[...] = rows.reshape(out_ref.shape)


def put_rotated(target, index, rows, rope_ref, base):
    cosine = rope_ref[base : base + HALF, :]
    sine = rope_ref[base + HALF : base + 2 * HALF, :]
    first, second = rows[:HALF, :], rows[HALF:, :]
    target[index + (slice(0, HALF),)] = (first * cosine - second * sine).astype(BF16)
    target[index + (slice(HALF, HEAD_DIM),)] = (second * cosine + first * sine).astype(BF16)


def make_attend_kernel(i):
    def fill(query_rows, key_rows, value_rows, rope_ref, low_ref, up_t_ref, parts):
        for c in range(2):
            start = c * SHARD_HEADS * HEAD_DIM + i * CHUNK_ROWS
            delta = dot_nn(up_t_ref[start : start + CHUNK_ROWS, :], low_ref[0])
            for p in range(2):
                put_rotated(parts, (c, p), query_rows(c, p) + delta[p * HEAD_DIM : (p + 1) * HEAD_DIM, :], rope_ref, 2 * HALF)
        for p in range(2):
            start = (HEADS + i + 4 * p) * HEAD_DIM
            delta = dot_nn(up_t_ref[start : start + HEAD_DIM, :], low_ref[1])
            put_rotated(parts, (2, p), key_rows(p), rope_ref, 0)
            parts[3, p] = (value_rows(p) + delta).astype(BF16)

    def kernel(own_ref, near_ref, remote_ref, rope_ref, low_ref, up_t_ref, bias_ref, out_ref, local, parts, attended):
        shard = lax.axis_index("ad")
        side, core = shard // 2, lax.rem(shard, 2)
        local[core] = own_ref[...].reshape(local.shape[1:])
        local[1 - core] = near_ref[...].reshape(local.shape[1:])

        @pl.when(side == 0)
        def _():
            fill(
                lambda c, p: local[c, p], lambda p: remote_ref[0, p], lambda p: remote_ref[1, p],
                rope_ref, low_ref, up_t_ref, parts,
            )

        @pl.when(side == 1)
        def _():
            fill(
                lambda c, p: remote_ref[c, p], lambda p: local[0, p], lambda p: local[1, p],
                rope_ref, low_ref, up_t_ref, parts,
            )

        def lanes(b):
            return slice(b * LANES, (b + 1) * LANES)

        def score(b, p):
            key = parts[2, p, :, lanes(b)].T[:BLOCK, :]
            query = jnp.concatenate([parts[p, 0, :, lanes(b)], parts[p, 1, :, lanes(b)]], axis=1)
            return dot_nn(key, query)

        def soften(b, scores):
            bias = bias_ref[b]
            scores = scores + jnp.concatenate([bias, bias], axis=1)
            weights = jnp.exp2(scores - jnp.max(scores, axis=0, keepdims=True))
            probs = (weights * (1.0 / jnp.sum(weights, axis=0, keepdims=True))).astype(BF16)
            return jnp.concatenate([probs, jnp.zeros((LANES - BLOCK, 2 * LANES), BF16)], axis=0)

        def mingle(b, p, probs):
            result = dot_nn(parts[3, p, :, lanes(b)], probs).astype(BF16)
            for h in range(2):
                row = (2 * p + h) * HEAD_DIM
                attended[row : row + HEAD_DIM, lanes(b)] = result[:, h * LANES : (h + 1) * LANES]

        work = [(b, p) for b in range(bias_ref.shape[0]) for p in range(2)]
        ahead = 2
        scores = [score(*work[n]) for n in range(ahead)]
        probs = {}
        for n, (b, p) in enumerate(work):
            if n + ahead < len(work):
                scores.append(score(*work[n + ahead]))
            probs[n] = soften(b, scores[n])
            if n >= 1:
                mingle(*work[n - 1], probs.pop(n - 1))
        mingle(*work[-1], probs.pop(len(work) - 1))
        for b in range(bias_ref.shape[0]):
            out_ref[b * BLOCK : (b + 1) * BLOCK, :] = attended[:, lanes(b)].T[:BLOCK, :]

    return kernel


def weight_rows(w_ref, chunks, cols):
    half = SHARD_HEADS * HEAD_DIM
    pieces = [
        w_ref[c * half + i * CHUNK_ROWS : c * half + (i + 1) * CHUNK_ROWS, cols] for i in chunks for c in range(2)
    ]
    return jnp.concatenate(pieces, axis=0)


def make_mix_kernel(chunks):
    def kernel(x_ref, w_ref, *rest):
        parts, out_ref = rest[:-1], rest[-1]
        columns = 2 * LANES
        attended = jnp.concatenate([part[...] for part in parts], axis=1)
        for n in range(out_ref.shape[1] // columns):
            cols = slice(n * columns, (n + 1) * columns)
            total = x_ref[:, cols].astype(F32) + dot_nn(attended, weight_rows(w_ref, chunks, cols))
            out_ref[:, cols] = total.astype(out_ref.dtype)

    return kernel


def after(value, *others):
    return lax.optimization_barrier((value,) + others)[0]


def body(
    layer_input_hidden,
    input_norm_scale,
    query_key_value_weight,
    output_weight,
    adapter_down_weight,
    adapter_up_weight,
    prompt_token_length,
    request_adapter_index,
    adapter_holder_index,
):
    tokens, width = layer_input_hidden.shape
    blocks = tokens // BLOCK
    padded = blocks * LANES
    rank = adapter_up_weight.shape[1]
    features = adapter_up_weight.shape[2]
    shard_cols = query_key_value_weight.shape[1]
    shards, requests = lax.axis_size("ad"), lax.axis_size("req")
    other_side = [(a, a ^ 2) for a in range(shards)]
    other_core = [(a, a ^ 1) for a in range(shards)]

    def other_row(bit):
        return [(r, r ^ bit) for r in range(requests)]

    head = jax.ShapeDtypeStruct((HEAD_DIM, width), BF16)
    turned = pl.pallas_call(
        turn_kernel,
        out_shape=[
            jax.ShapeDtypeStruct((CHUNKS, 2, HEAD_DIM, width), BF16),
            jax.ShapeDtypeStruct((1, 2 * rank, width), BF16),
        ]
        + [head] * CHUNKS,
        in_specs=[VMEM] * 3,
        out_specs=[VMEM] * (CHUNKS + 2),
        scratch_shapes=[pltpu.VMEM((shard_cols, width), BF16)],
        compiler_params=params(16),
        name="turn_weight",
    )(query_key_value_weight, adapter_down_weight, adapter_up_weight)
    own, packed, sends = turned[0], turned[1], turned[2:]

    normed, rope, bias, slot = pl.pallas_call(
        norm_kernel,
        grid=(blocks,),
        out_shape=[
            jax.ShapeDtypeStruct((padded, width), BF16),
            jax.ShapeDtypeStruct((4 * HALF, padded), F32),
            jax.ShapeDtypeStruct((blocks, BLOCK, LANES), F32),
            jax.ShapeDtypeStruct((1, padded), jnp.int32),
        ],
        in_specs=[
            pl.BlockSpec((BLOCK, width), lambda b: (b, 0)),
            pl.BlockSpec((1, width), lambda b: (0, 0)),
            pl.BlockSpec((4 * HALF, MAXLEN), lambda b: (0, 0)),
        ]
        + [SMEM] * 3,
        out_specs=[
            pl.BlockSpec((LANES, width), lambda b: (b, 0)),
            pl.BlockSpec((4 * HALF, LANES), lambda b: (0, b)),
            pl.BlockSpec((1, BLOCK, LANES), lambda b: (b, 0, 0)),
            pl.BlockSpec((1, LANES), lambda b: (0, b)),
        ],
        compiler_params=params(16),
        name="norm_tokens",
    )(
        layer_input_hidden, input_norm_scale.reshape(1, width), jnp.asarray(rope_tables()),
        prompt_token_length, request_adapter_index, adapter_holder_index,
    )

    def project(weight, name):
        return pl.pallas_call(
            project_kernel,
            out_shape=[jax.ShapeDtypeStruct((CHUNK_ROWS, padded), F32)] * CHUNKS,
            in_specs=[VMEM] * 2,
            out_specs=[VMEM] * CHUNKS,
            compiler_params=params(24),
            name=name,
        )(weight, normed)

    def project_remote(i, pieces, token):
        return pl.pallas_call(
            project_remote_kernel,
            out_shape=jax.ShapeDtypeStruct((2, 2, HEAD_DIM, padded), F32),
            in_specs=[VMEM] * 5,
            out_specs=VMEM,
            scratch_shapes=[pltpu.VMEM((2, 2, HEAD_DIM, width), BF16)],
            compiler_params=params(24),
            name=f"project_{i}",
        )(*pieces, after(normed, token))

    def attend(i, rows):
        return pl.pallas_call(
            make_attend_kernel(i),
            out_shape=jax.ShapeDtypeStruct((tokens, 4 * HEAD_DIM), BF16),
            in_specs=[VMEM] * 7,
            out_specs=VMEM,
            scratch_shapes=[
                pltpu.VMEM((2, 2, HEAD_DIM, padded), F32),
                pltpu.VMEM((4, 2, HEAD_DIM, padded), BF16),
                pltpu.VMEM((4 * HEAD_DIM, padded), BF16),
            ],
            compiler_params=params(16 if len(codes) <= 8 else 24),
            name=f"attend_{i}",
        )(own_parts[i], near_parts[i], rows, rope, low, up_t, bias)

    def gather_adapters(packed, codes, bit, before, then):
        got = after(lax.ppermute(after(packed, before), "req", other_row(bit)), then)
        return jnp.concatenate([packed, got], axis=0), codes + [code ^ bit for code in codes]

    bits = []
    while 2 ** len(bits) < requests:
        bits.append(2 ** len(bits))
    bits = bits[:0:-1][:1] + bits[:1] + bits[:0:-1][1:]
    codes = [0]

    def across(i):
        return lax.ppermute(sends[i], "ad", other_side)

    def along(piece, token):
        return lax.ppermute(after(piece, token), "req", other_row(1))

    def beside(piece, token):
        return lax.ppermute(after(piece, token), "ad", other_core)

    near = beside(own, own)
    x_pieces = [across(i) for i in range(CHUNKS)]
    xy_pieces, far_x, far_xy = [None] * CHUNKS, [None] * CHUNKS, [None] * CHUNKS

    def forward(i, token):
        xy_pieces[i] = along(x_pieces[i], token)
        far_x[i] = beside(x_pieces[i], token)

    def arrived(i):
        return x_pieces[i], xy_pieces[i], far_x[i], far_xy[i]

    for bit in bits[:1]:
        packed, codes = gather_adapters(packed, codes, bit, packed, normed)
    forward(0, normed)
    own_parts = project(after(own, x_pieces[0]), "project_own")
    for bit in bits[1:2]:
        packed, codes = gather_adapters(packed, codes, bit, x_pieces[0], own_parts[0])
    forward(1, own_parts[0])
    far_xy[0] = beside(xy_pieces[0], own_parts[0])
    near_parts = project(after(near, x_pieces[1]), "project_near")
    rows_0 = project_remote(0, arrived(0), near_parts[0])
    forward(2, rows_0)
    far_xy[1] = beside(xy_pieces[1], rows_0)
    rows_1 = project_remote(1, arrived(1), x_pieces[2])
    for bit in bits[2:]:
        packed, codes = gather_adapters(packed, codes, bit, own_parts[0], rows_1)
    packed_other = beside(packed, rows_1)
    forward(3, rows_1)
    far_xy[2] = beside(xy_pieces[2], rows_1)
    low, up_t = pl.pallas_call(
        make_low_kernel(codes, rank),
        out_shape=[
            jax.ShapeDtypeStruct((2, len(codes) * rank, padded), BF16),
            jax.ShapeDtypeStruct((features, len(codes) * rank), BF16),
        ],
        in_specs=[VMEM] * 4,
        out_specs=[VMEM] * 2,
        scratch_shapes=[pltpu.VMEM((2,) + packed.shape, BF16)],
        compiler_params=params(16 if len(codes) <= 8 else 48),
        name="adapter_low",
    )(packed, packed_other, after(normed, rows_1), slot)
    attended = [attend(0, rows_0), attend(1, rows_1)]
    far_xy[3] = beside(xy_pieces[3], attended[0])
    rows = project_remote(2, arrived(2), attended[1])
    attended.append(attend(2, rows))

    def mix(base, chunks, kind, name):
        return pl.pallas_call(
            make_mix_kernel(chunks),
            out_shape=jax.ShapeDtypeStruct((tokens, width), kind),
            in_specs=[VMEM] * (2 + len(chunks)),
            out_specs=VMEM,
            compiler_params=params(24),
            name=name,
        )(base, output_weight, *[attended[i] for i in chunks])

    partial = mix(layer_input_hidden, range(CHUNKS - 1), F32, "mix_first")
    rows = project_remote(CHUNKS - 1, arrived(CHUNKS - 1), partial)
    attended.append(attend(CHUNKS - 1, rows))
    return mix(partial, range(CHUNKS - 1, CHUNKS), BF16, "mix_last")


def solution(mesh):
    placed = (
        P(("req", "ad"), None),
        P(),
        P(None, "ad"),
        P(),
        P("req", None, None),
        P("req", None, None),
        P(("req", "ad"), None),
        P(("req", "ad"), None),
        P(),
    )
    return jax.shard_map(
        body, mesh=mesh, in_specs=placed, out_specs=P(("req", "ad"), None), check_vma=False
    )
```

```python
import math

import jax
import jax.numpy as jnp
import numpy as np
from jax import lax
from jax.experimental import pallas as pl
from jax.experimental.pallas import tpu as pltpu
from jax.sharding import PartitionSpec as P

HEADS = 16
KV_HEADS = 8
HEAD_DIM = 96
HALF = HEAD_DIM // 2
MAXLEN = 16
PAIR = 28
EPS = 1e-05
ROPE_THETA = 100000.0

GROUP = 4
BLOCK = GROUP * PAIR
LANES = 128
CHUNKS = 4
SHARD_HEADS = 8
CHUNK_ROWS = 2 * HEAD_DIM
SHARED = ((0, 1), (2,))
DIRECT = (3,)
LOG2E = 1.4426950408889634

F32 = jnp.float32
BF16 = jnp.bfloat16
VMEM = pl.BlockSpec(memory_space=pltpu.VMEM)
SMEM = pl.BlockSpec(memory_space=pltpu.SMEM)
HBM = pl.BlockSpec(memory_space=pltpu.HBM)
NO_COST = pl.CostEstimate(flops=0, bytes_accessed=0, transcendentals=0)


def params(mib):
    return pltpu.CompilerParams(vmem_limit_bytes=mib * 1024 * 1024)


def dot_nt(left, right):
    return lax.dot_general(left, right, (((1,), (1,)), ((), ())), preferred_element_type=F32)


def dot_nn(left, right):
    return lax.dot_general(left, right, (((1,), (0,)), ((), ())), preferred_element_type=F32)


def rope_tables():
    inverse = np.exp(-math.log(ROPE_THETA) * 2.0 * np.arange(HALF, dtype=np.float64) / HEAD_DIM)
    angles = inverse[:, None] * np.arange(MAXLEN, dtype=np.float64)[None, :]
    cosine, sine = np.cos(angles), np.sin(angles)
    scale = LOG2E / math.sqrt(HEAD_DIM)
    return np.concatenate([cosine, sine, cosine * scale, sine * scale], axis=0).astype(np.float32)


def group_of(index):
    found = jnp.zeros_like(index)
    for edge in range(1, GROUP + 1):
        found = found + jnp.where(index >= edge * PAIR, 1, 0)
    return found


def turn_kernel(w_ref, own_ref, *rest):
    send_refs, turned = rest[:-1], rest[-1]
    shard = lax.axis_index("ad")
    half = lax.rem(lax.axis_index("req"), 2)
    step = 4 * HEAD_DIM
    for g in range(w_ref.shape[1] // step):
        turned[g * step : (g + 1) * step, :] = w_ref[:, g * step : (g + 1) * step].T
    is_kv = shard >= 2
    for i in range(CHUNKS):
        for p in range(2):
            head = jnp.where(is_kv, i + 4 * p, 2 * i + p)
            own_ref[i, p] = turned[pl.ds(pl.multiple_of(head * HEAD_DIM, HEAD_DIM), HEAD_DIM), :]
    for send_ref, chunks in zip(send_refs, SHARED):
        for n, i in enumerate(chunks):
            send_ref[n] = own_ref[i, half]
    for n, i in enumerate(DIRECT):
        send_refs[-1][n] = own_ref[i]


def pack(down_ref, up_ref, out_ref):
    core = lax.rem(lax.axis_index("ad"), 2)
    rank, width = up_ref.shape[1], down_ref.shape[2]
    value_cols = up_ref.shape[2] - width

    @pl.when(core == 0)
    def _():
        out_ref[...] = down_ref[...]

    @pl.when(core == 1)
    def _():
        out_ref[0, :rank, :] = up_ref[0, :, :width]
        out_ref[0, rank:, :value_cols] = up_ref[0, :, width:]
        out_ref[0, rank:, value_cols:] = jnp.zeros((rank, width - value_cols), BF16)


def norm_kernel(
    x_ref, scale_ref, table_ref, down_ref, up_ref, len_ref, adapter_ref, holder_ref,
    normed_ref, rope_ref, bias_ref, slot_ref, pack_ref,
):
    pack(down_ref, up_ref, pack_ref)
    gain = scale_ref[...].reshape(1, scale_ref.shape[0])
    lane = lax.broadcasted_iota(jnp.int32, (1, LANES), 1)
    group = group_of(lane)
    within = lane - PAIR * group
    key_row = lax.broadcasted_iota(jnp.int32, (BLOCK, LANES), 0)
    query_col = lax.broadcasted_iota(jnp.int32, (BLOCK, LANES), 1)
    key_group = group_of(key_row)
    key_within = key_row - PAIR * key_group
    query_group = group_of(query_col)
    query_within = query_col - PAIR * query_group
    same_pair = (key_group == query_group) & (key_row <= query_col)
    dead = query_col >= BLOCK
    position_row = lax.broadcasted_iota(jnp.int32, (MAXLEN, LANES), 0)
    for b in range(bias_ref.shape[0]):
        lanes = slice(b * LANES, (b + 1) * LANES)
        first = jnp.zeros((1, LANES), jnp.int32)
        slot_first = jnp.zeros((1, LANES), jnp.int32)
        slot_second = jnp.zeros((1, LANES), jnp.int32)
        for g in range(GROUP):
            r = 2 * (GROUP * b + g)
            first = jnp.where(group == g, len_ref[0, r], first)
            slot_first = jnp.where(group == g, holder_ref[adapter_ref[0, r]], slot_first)
            slot_second = jnp.where(group == g, holder_ref[adapter_ref[0, r + 1]], slot_second)
        position = jnp.where(within < first, within, within - first)
        slot_ref[:, lanes] = jnp.where(within < first, slot_first, slot_second)
        onehot = jnp.where(position_row == position, 1.0, 0.0).astype(F32)
        rope_ref[:, lanes] = jnp.dot(
            table_ref[...], onehot, preferred_element_type=F32, precision=lax.Precision.HIGHEST
        )
        split = (key_within >= first) | (query_within < first)
        bias_ref[b] = jnp.where((same_pair & split) | dead, 0.0, -jnp.inf).astype(F32)
        rows = x_ref[b * BLOCK : (b + 1) * BLOCK, :].astype(F32)
        mean = jnp.mean(rows * rows, axis=-1, keepdims=True)
        normed_ref[b * LANES : b * LANES + BLOCK, :] = (rows * lax.rsqrt(mean + EPS) * gain).astype(BF16)
        normed_ref[b * LANES + BLOCK : (b + 1) * LANES, :] = jnp.zeros((LANES - BLOCK, rows.shape[1]), BF16)


def make_low_kernel(codes, rank):
    def kernel(mine_ref, other_ref, normed_ref, slot_ref, low_ref, up_t_ref, adapter):
        core = lax.rem(lax.axis_index("ad"), 2)
        me = lax.axis_index("req")
        count, rows, width = mine_ref.shape
        adapter[core] = mine_ref[...]
        adapter[1 - core] = other_ref[...]
        low = dot_nt(adapter[0].reshape(count * rows, width), normed_ref[...]).astype(BF16)
        slot = slot_ref[...]
        for j, code in enumerate(codes):
            mine = slot == me ^ code
            for part in range(2):
                r = (2 * j + part) * rank
                low_ref[part, j * rank : (j + 1) * rank, :] = jnp.where(mine, low[r : r + rank, :], jnp.zeros((), BF16))
        for part in range(2):
            stop = min(width, up_t_ref.shape[0] - part * width)
            step = 3 * LANES
            for start in range(0, stop, step):
                piece = adapter[1, :, part * rank : (part + 1) * rank, start : start + step]
                up_t_ref[part * width + start : part * width + start + step, :] = piece.reshape(count * rank, step).T

    return kernel


def project_kernel(w_ref, normed_ref, *out_refs):
    rows = dot_nt(w_ref[...].reshape(CHUNKS * CHUNK_ROWS, w_ref.shape[-1]), normed_ref[...])
    for i, out_ref in enumerate(out_refs):
        out_ref[...] = rows[i * CHUNK_ROWS : (i + 1) * CHUNK_ROWS, :]


def project_shared_kernel(near_x, near_xy, far_x, far_xy, normed_ref, *rest):
    out_refs, weight = rest[:-1], rest[-1]
    half = lax.rem(lax.axis_index("req"), 2)
    core = lax.rem(lax.axis_index("ad"), 2)
    for n in range(len(out_refs)):
        weight[n, core, half] = near_x[n]
        weight[n, core, 1 - half] = near_xy[n]
        weight[n, 1 - core, half] = far_x[n]
        weight[n, 1 - core, 1 - half] = far_xy[n]
    project_chunks(weight, normed_ref, out_refs)


def project_direct_kernel(near_x, far_x, normed_ref, *rest):
    out_refs, weight = rest[:-1], rest[-1]
    core = lax.rem(lax.axis_index("ad"), 2)
    for n in range(len(out_refs)):
        weight[n, core] = near_x[n]
        weight[n, 1 - core] = far_x[n]
    project_chunks(weight, normed_ref, out_refs)


def project_chunks(weight, normed_ref, out_refs):
    step = 4 * HEAD_DIM
    rows = dot_nt(weight[...].reshape(len(out_refs) * step, weight.shape[-1]), normed_ref[...])
    for n, out_ref in enumerate(out_refs):
        out_ref[...] = rows[n * step : (n + 1) * step, :].reshape(out_ref.shape)


def put_rotated(target, index, rows, rope_ref, base):
    cosine = rope_ref[base : base + HALF, :]
    sine = rope_ref[base + HALF : base + 2 * HALF, :]
    first, second = rows[:HALF, :], rows[HALF:, :]
    target[index + (slice(0, HALF),)] = (first * cosine - second * sine).astype(BF16)
    target[index + (slice(HALF, HEAD_DIM),)] = (second * cosine + first * sine).astype(BF16)


def make_attend_kernel(i):
    def fill(query_rows, key_rows, value_rows, rope_ref, low_ref, up_t_ref, parts):
        for c in range(2):
            start = c * SHARD_HEADS * HEAD_DIM + i * CHUNK_ROWS
            delta = dot_nn(up_t_ref[start : start + CHUNK_ROWS, :], low_ref[0])
            for p in range(2):
                put_rotated(parts, (c, p), query_rows(c, p) + delta[p * HEAD_DIM : (p + 1) * HEAD_DIM, :], rope_ref, 2 * HALF)
        for p in range(2):
            start = (HEADS + i + 4 * p) * HEAD_DIM
            delta = dot_nn(up_t_ref[start : start + HEAD_DIM, :], low_ref[1])
            put_rotated(parts, (2, p), key_rows(p), rope_ref, 0)
            parts[3, p] = (value_rows(p) + delta).astype(BF16)

    def kernel(own_ref, near_ref, remote_ref, rope_ref, low_ref, up_t_ref, bias_ref, out_ref, local, parts, attended):
        shard = lax.axis_index("ad")
        side, core = shard // 2, lax.rem(shard, 2)
        local[core] = own_ref[...].reshape(local.shape[1:])
        local[1 - core] = near_ref[...].reshape(local.shape[1:])

        @pl.when(side == 0)
        def _():
            fill(
                lambda c, p: local[c, p], lambda p: remote_ref[0, p], lambda p: remote_ref[1, p],
                rope_ref, low_ref, up_t_ref, parts,
            )

        @pl.when(side == 1)
        def _():
            fill(
                lambda c, p: remote_ref[c, p], lambda p: local[0, p], lambda p: local[1, p],
                rope_ref, low_ref, up_t_ref, parts,
            )

        def lanes(b):
            return slice(b * LANES, (b + 1) * LANES)

        def score(b, p):
            key = parts[2, p, :, lanes(b)].T[:BLOCK, :]
            query = jnp.concatenate([parts[p, 0, :, lanes(b)], parts[p, 1, :, lanes(b)]], axis=1)
            return dot_nn(key, query)

        def soften(b, scores):
            bias = bias_ref[b]
            scores = scores + jnp.concatenate([bias, bias], axis=1)
            weights = jnp.exp2(scores - jnp.max(scores, axis=0, keepdims=True))
            probs = (weights * (1.0 / jnp.sum(weights, axis=0, keepdims=True))).astype(BF16)
            return jnp.concatenate([probs, jnp.zeros((LANES - BLOCK, 2 * LANES), BF16)], axis=0)

        def mingle(b, p, probs):
            result = dot_nn(parts[3, p, :, lanes(b)], probs).astype(BF16)
            for h in range(2):
                row = (2 * p + h) * HEAD_DIM
                attended[row : row + HEAD_DIM, lanes(b)] = result[:, h * LANES : (h + 1) * LANES]

        work = [(b, p) for b in range(bias_ref.shape[0]) for p in range(2)]
        ahead = 2
        scores = [score(*work[n]) for n in range(ahead)]
        probs = {}
        for n, (b, p) in enumerate(work):
            if n + ahead < len(work):
                scores.append(score(*work[n + ahead]))
            probs[n] = soften(b, scores[n])
            if n >= 1:
                mingle(*work[n - 1], probs.pop(n - 1))
        mingle(*work[-1], probs.pop(len(work) - 1))
        for b in range(bias_ref.shape[0]):
            out_ref[b * BLOCK : (b + 1) * BLOCK, :] = attended[:, lanes(b)].T[:BLOCK, :]

    return kernel


def weight_rows(w_ref, chunks, cols):
    half = SHARD_HEADS * HEAD_DIM
    pieces = [
        w_ref[c * half + i * CHUNK_ROWS : c * half + (i + 1) * CHUNK_ROWS, cols] for i in chunks for c in range(2)
    ]
    return jnp.concatenate(pieces, axis=0)


def make_mix_kernel(chunks):
    def kernel(x_ref, w_ref, *rest):
        parts, out_ref = rest[:-1], rest[-1]
        columns = 2 * LANES
        attended = jnp.concatenate([part[...] for part in parts], axis=1)
        for n in range(out_ref.shape[1] // columns):
            cols = slice(n * columns, (n + 1) * columns)
            total = x_ref[:, cols].astype(F32) + dot_nn(attended, weight_rows(w_ref, chunks, cols))
            out_ref[:, cols] = total.astype(out_ref.dtype)

    return kernel


def make_finish_kernel(chunks):
    def kernel(x_ref, w_ref, *rest):
        parts, out_hbm, ready, sems = rest[:-3], rest[-3], rest[-2], rest[-1]
        columns = ready.shape[2]
        attended = jnp.concatenate([part[...] for part in parts], axis=1)
        copies = []
        for n in range(ready.shape[0]):
            cols = slice(n * columns, (n + 1) * columns)
            total = x_ref[:, cols].astype(F32) + dot_nn(attended, weight_rows(w_ref, chunks, cols))
            ready[n] = total.astype(BF16)
            copies.append(pltpu.make_async_copy(ready.at[n], out_hbm.at[:, pl.ds(n * columns, columns)], sems.at[n]))
            copies[-1].start()
        for copy in copies:
            copy.wait()

    return kernel


def after(value, *others):
    return lax.optimization_barrier((value,) + others)[0]


def body(
    layer_input_hidden,
    input_norm_scale,
    query_key_value_weight,
    output_weight,
    adapter_down_weight,
    adapter_up_weight,
    prompt_token_length,
    request_adapter_index,
    adapter_holder_index,
):
    tokens, width = layer_input_hidden.shape
    blocks = tokens // BLOCK
    padded = blocks * LANES
    rank = adapter_up_weight.shape[1]
    features = adapter_up_weight.shape[2]
    shard_cols = query_key_value_weight.shape[1]
    shards, requests = lax.axis_size("ad"), lax.axis_size("req")
    other_side = [(a, a ^ 2) for a in range(shards)]
    other_core = [(a, a ^ 1) for a in range(shards)]

    def other_row(bit):
        return [(r, r ^ bit) for r in range(requests)]

    turned = pl.pallas_call(
        turn_kernel,
        out_shape=[jax.ShapeDtypeStruct((CHUNKS, 2, HEAD_DIM, width), BF16)]
        + [jax.ShapeDtypeStruct((len(chunks), HEAD_DIM, width), BF16) for chunks in SHARED]
        + [jax.ShapeDtypeStruct((len(DIRECT), 2, HEAD_DIM, width), BF16)],
        in_specs=[VMEM],
        out_specs=[VMEM] * (2 + len(SHARED)),
        scratch_shapes=[pltpu.VMEM((shard_cols, width), BF16)],
        compiler_params=params(20),
        name="turn_weight",
    )(query_key_value_weight)
    own, sends = turned[0], turned[1:]

    normed, rope, bias, slot, packed = pl.pallas_call(
        norm_kernel,
        out_shape=[
            jax.ShapeDtypeStruct((padded, width), BF16),
            jax.ShapeDtypeStruct((4 * HALF, padded), F32),
            jax.ShapeDtypeStruct((blocks, BLOCK, LANES), F32),
            jax.ShapeDtypeStruct((1, padded), jnp.int32),
            jax.ShapeDtypeStruct((1, 2 * rank, width), BF16),
        ],
        in_specs=[VMEM] * 5 + [SMEM] * 3,
        out_specs=[VMEM] * 5,
        compiler_params=params(16),
        cost_estimate=NO_COST,
        name="norm_tokens",
    )(
        layer_input_hidden, input_norm_scale, jnp.asarray(rope_tables()), adapter_down_weight, adapter_up_weight,
        prompt_token_length, request_adapter_index, adapter_holder_index,
    )

    def project(weight, name):
        return pl.pallas_call(
            project_kernel,
            out_shape=[jax.ShapeDtypeStruct((CHUNK_ROWS, padded), F32)] * CHUNKS,
            in_specs=[VMEM] * 2,
            out_specs=[VMEM] * CHUNKS,
            compiler_params=params(24),
            cost_estimate=NO_COST,
            name=name,
        )(weight, normed)

    def project_remote(kernel, chunks, arrays, token):
        return pl.pallas_call(
            kernel,
            out_shape=[jax.ShapeDtypeStruct((2, 2, HEAD_DIM, padded), F32)] * len(chunks),
            in_specs=[VMEM] * (len(arrays) + 1),
            out_specs=[VMEM] * len(chunks),
            scratch_shapes=[pltpu.VMEM((len(chunks), 2, 2, HEAD_DIM, width), BF16)],
            compiler_params=params(20),
            cost_estimate=NO_COST,
            name=f"project_{chunks[0]}",
        )(*arrays, after(normed, token))

    def attend(i, rows):
        return pl.pallas_call(
            make_attend_kernel(i),
            out_shape=jax.ShapeDtypeStruct((tokens, 4 * HEAD_DIM), BF16),
            in_specs=[VMEM] * 7,
            out_specs=VMEM,
            scratch_shapes=[
                pltpu.VMEM((2, 2, HEAD_DIM, padded), F32),
                pltpu.VMEM((4, 2, HEAD_DIM, padded), BF16),
                pltpu.VMEM((4 * HEAD_DIM, padded), BF16),
            ],
            compiler_params=params(16 if len(codes) <= 8 else 24),
            cost_estimate=NO_COST,
            name=f"attend_{i}",
        )(own_parts[i], near_parts[i], rows, rope, low, up_t, bias)

    def gather_adapters(packed, codes, bit, before, then):
        got = after(lax.ppermute(after(packed, before), "req", other_row(bit)), then)
        return jnp.concatenate([packed, got], axis=0), codes + [code ^ bit for code in codes]

    bits = []
    while 2 ** len(bits) < requests:
        bits.append(2 ** len(bits))
    bits = bits[:1] + bits[:0:-1]
    codes = [0]

    def along(piece, token):
        return lax.ppermute(after(piece, token), "req", other_row(1))

    def beside(piece, token):
        return lax.ppermute(after(piece, token), "ad", other_core)

    x_0, x_1, x_2 = [lax.ppermute(send, "ad", other_side) for send in sends]
    near = beside(own, own)
    for bit in bits[:1]:
        packed, codes = gather_adapters(packed, codes, bit, packed, packed)
    for bit in bits[1:2]:
        packed, codes = gather_adapters(packed, codes, bit, normed, normed)
    own_parts = project(after(own, normed), "project_own")
    xy_0, far_x_0 = along(x_0, own_parts[0]), beside(x_0, own_parts[0])
    near_parts = project(after(near, x_0), "project_near")
    for bit in bits[2:]:
        packed, codes = gather_adapters(packed, codes, bit, own_parts[0], own_parts[0])
    xy_1, far_x_1 = along(x_1, near_parts[0]), beside(x_1, own_parts[0])
    far_xy_0 = beside(xy_0, x_1)
    packed_other = beside(packed, own_parts[0])
    rows_0, rows_1 = project_remote(project_shared_kernel, SHARED[0], (x_0, xy_0, far_x_0, far_xy_0), near_parts[0])
    low, up_t = pl.pallas_call(
        make_low_kernel(codes, rank),
        out_shape=[
            jax.ShapeDtypeStruct((2, len(codes) * rank, padded), BF16),
            jax.ShapeDtypeStruct((features, len(codes) * rank), BF16),
        ],
        in_specs=[VMEM] * 4,
        out_specs=[VMEM] * 2,
        scratch_shapes=[pltpu.VMEM((2,) + packed.shape, BF16)],
        compiler_params=params(16 if len(codes) <= 8 else 48),
        cost_estimate=NO_COST,
        name="adapter_low",
    )(packed, packed_other, after(normed, rows_0), slot)
    attended = [attend(0, rows_0), attend(1, rows_1)]
    far_x_2 = beside(x_2, rows_0)
    far_xy_1 = beside(xy_1, low)
    (rows_2,) = project_remote(project_shared_kernel, SHARED[1], (x_1, xy_1, far_x_1, far_xy_1), attended[1])
    attended.append(attend(2, rows_2))

    def mix(base, chunks, kind, name):
        return pl.pallas_call(
            make_mix_kernel(chunks),
            out_shape=jax.ShapeDtypeStruct((tokens, width), kind),
            in_specs=[VMEM] * (2 + len(chunks)),
            out_specs=VMEM,
            compiler_params=params(24),
            cost_estimate=NO_COST,
            name=name,
        )(base, output_weight, *[attended[i] for i in chunks])

    partial = mix(layer_input_hidden, range(CHUNKS - 1), F32, "mix_first")
    (rows_3,) = project_remote(project_direct_kernel, DIRECT, (x_2, far_x_2), partial)
    attended.append(attend(CHUNKS - 1, rows_3))
    columns = 2 * LANES
    return pl.pallas_call(
        make_finish_kernel(range(CHUNKS - 1, CHUNKS)),
        out_shape=jax.ShapeDtypeStruct((tokens, width), BF16),
        in_specs=[VMEM] * 3,
        out_specs=HBM,
        scratch_shapes=[
            pltpu.VMEM((width // columns, tokens, columns), BF16),
            pltpu.SemaphoreType.DMA((width // columns,)),
        ],
        compiler_params=params(20),
        name="mix_last",
    )(partial, output_weight, attended[-1])


def solution(mesh):
    placed = (
        P(("req", "ad"), None),
        P(),
        P(None, "ad"),
        P(),
        P("req", None, None),
        P("req", None, None),
        P(("req", "ad"), None),
        P(("req", "ad"), None),
        P(),
    )
    return jax.shard_map(
        body, mesh=mesh, in_specs=placed, out_specs=P(("req", "ad"), None), check_vma=False
    )
```

```python
import math

import jax
import jax.numpy as jnp
import numpy as np
from jax import lax
from jax.experimental import pallas as pl
from jax.experimental.pallas import tpu as pltpu
from jax.sharding import PartitionSpec as P

HEADS = 16
KV_HEADS = 8
HEAD_DIM = 96
HALF = HEAD_DIM // 2
MAXLEN = 16
PAIR = 28
EPS = 1e-05
ROPE_THETA = 100000.0

GROUP = 4
BLOCK = GROUP * PAIR
LANES = 128
CHUNKS = 4
SHARD_HEADS = 8
CHUNK_ROWS = 2 * HEAD_DIM
SHARED = ((0, 1), (2,))
DIRECT = (3,)
LOG2E = 1.4426950408889634

F32 = jnp.float32
BF16 = jnp.bfloat16
VMEM = pl.BlockSpec(memory_space=pltpu.VMEM)
SMEM = pl.BlockSpec(memory_space=pltpu.SMEM)
HBM = pl.BlockSpec(memory_space=pltpu.HBM)
NO_COST = pl.CostEstimate(flops=0, bytes_accessed=0, transcendentals=0)


def params(mib):
    return pltpu.CompilerParams(vmem_limit_bytes=mib * 1024 * 1024)


def dot_nt(left, right):
    return lax.dot_general(left, right, (((1,), (1,)), ((), ())), preferred_element_type=F32)


def dot_nn(left, right):
    return lax.dot_general(left, right, (((1,), (0,)), ((), ())), preferred_element_type=F32)


def rope_tables():
    inverse = np.exp(-math.log(ROPE_THETA) * 2.0 * np.arange(HALF, dtype=np.float64) / HEAD_DIM)
    angles = inverse[:, None] * np.arange(MAXLEN, dtype=np.float64)[None, :]
    cosine, sine = np.cos(angles), np.sin(angles)
    scale = LOG2E / math.sqrt(HEAD_DIM)
    return np.concatenate([cosine, sine, cosine * scale, sine * scale], axis=0).astype(np.float32)


def group_of(index):
    found = jnp.zeros_like(index)
    for edge in range(1, GROUP + 1):
        found = found + jnp.where(index >= edge * PAIR, 1, 0)
    return found


def turn_kernel(w_ref, own_ref, *rest):
    send_refs, turned = rest[:-1], rest[-1]
    shard = lax.axis_index("ad")
    half = lax.rem(lax.axis_index("req"), 2)
    step = 4 * HEAD_DIM
    for g in range(w_ref.shape[1] // step):
        turned[g * step : (g + 1) * step, :] = w_ref[:, g * step : (g + 1) * step].T
    is_kv = shard >= 2
    for i in range(CHUNKS):
        for p in range(2):
            head = jnp.where(is_kv, i + 4 * p, 2 * i + p)
            own_ref[i, p] = turned[pl.ds(pl.multiple_of(head * HEAD_DIM, HEAD_DIM), HEAD_DIM), :]
    for send_ref, chunks in zip(send_refs, SHARED):
        for n, i in enumerate(chunks):
            send_ref[n] = own_ref[i, half]
    for n, i in enumerate(DIRECT):
        send_refs[-1][n] = own_ref[i]


def pack(down_ref, up_ref, out_ref):
    core = lax.rem(lax.axis_index("ad"), 2)
    rank, width = up_ref.shape[1], down_ref.shape[2]
    value_cols = up_ref.shape[2] - width

    @pl.when(core == 0)
    def _():
        out_ref[...] = down_ref[...]

    @pl.when(core == 1)
    def _():
        out_ref[0, :rank, :] = up_ref[0, :, :width]
        out_ref[0, rank:, :value_cols] = up_ref[0, :, width:]
        out_ref[0, rank:, value_cols:] = jnp.zeros((rank, width - value_cols), BF16)


def norm_kernel(
    x_ref, scale_ref, table_ref, down_ref, up_ref, len_ref, adapter_ref, holder_ref,
    normed_ref, rope_ref, bias_ref, slot_ref, pack_ref,
):
    pack(down_ref, up_ref, pack_ref)
    gain = scale_ref[...].reshape(1, scale_ref.shape[0])
    lane = lax.broadcasted_iota(jnp.int32, (1, LANES), 1)
    group = group_of(lane)
    within = lane - PAIR * group
    key_row = lax.broadcasted_iota(jnp.int32, (BLOCK, LANES), 0)
    query_col = lax.broadcasted_iota(jnp.int32, (BLOCK, LANES), 1)
    key_group = group_of(key_row)
    key_within = key_row - PAIR * key_group
    query_group = group_of(query_col)
    query_within = query_col - PAIR * query_group
    same_pair = (key_group == query_group) & (key_row <= query_col)
    dead = query_col >= BLOCK
    position_row = lax.broadcasted_iota(jnp.int32, (MAXLEN, LANES), 0)
    for b in range(bias_ref.shape[0]):
        lanes = slice(b * LANES, (b + 1) * LANES)
        first = jnp.zeros((1, LANES), jnp.int32)
        slot_first = jnp.zeros((1, LANES), jnp.int32)
        slot_second = jnp.zeros((1, LANES), jnp.int32)
        for g in range(GROUP):
            r = 2 * (GROUP * b + g)
            first = jnp.where(group == g, len_ref[0, r], first)
            slot_first = jnp.where(group == g, holder_ref[adapter_ref[0, r]], slot_first)
            slot_second = jnp.where(group == g, holder_ref[adapter_ref[0, r + 1]], slot_second)
        position = jnp.where(within < first, within, within - first)
        slot_ref[:, lanes] = jnp.where(within < first, slot_first, slot_second)
        onehot = jnp.where(position_row == position, 1.0, 0.0).astype(F32)
        rope_ref[:, lanes] = jnp.dot(
            table_ref[...], onehot, preferred_element_type=F32, precision=lax.Precision.HIGHEST
        )
        split = (key_within >= first) | (query_within < first)
        bias_ref[b] = jnp.where((same_pair & split) | dead, 0.0, -jnp.inf).astype(F32)
        rows = x_ref[b * BLOCK : (b + 1) * BLOCK, :].astype(F32)
        mean = jnp.mean(rows * rows, axis=-1, keepdims=True)
        normed_ref[b * LANES : b * LANES + BLOCK, :] = (rows * lax.rsqrt(mean + EPS) * gain).astype(BF16)
        normed_ref[b * LANES + BLOCK : (b + 1) * LANES, :] = jnp.zeros((LANES - BLOCK, rows.shape[1]), BF16)


def make_low_kernel(codes, rank):
    def kernel(mine_ref, other_ref, normed_ref, slot_ref, low_ref, up_t_ref, adapter):
        core = lax.rem(lax.axis_index("ad"), 2)
        me = lax.axis_index("req")
        count, rows, width = mine_ref.shape
        adapter[core] = mine_ref[...]
        adapter[1 - core] = other_ref[...]
        low = dot_nt(adapter[0].reshape(count * rows, width), normed_ref[...]).astype(BF16)
        slot = slot_ref[...]
        for j, code in enumerate(codes):
            mine = slot == me ^ code
            for part in range(2):
                r = (2 * j + part) * rank
                low_ref[part, j * rank : (j + 1) * rank, :] = jnp.where(mine, low[r : r + rank, :], jnp.zeros((), BF16))
        for part in range(2):
            stop = min(width, up_t_ref.shape[0] - part * width)
            step = 3 * LANES
            for start in range(0, stop, step):
                piece = adapter[1, :, part * rank : (part + 1) * rank, start : start + step]
                up_t_ref[part * width + start : part * width + start + step, :] = piece.reshape(count * rank, step).T

    return kernel


def project_kernel(w_ref, normed_ref, *out_refs):
    rows = dot_nt(w_ref[...].reshape(CHUNKS * CHUNK_ROWS, w_ref.shape[-1]), normed_ref[...])
    for i, out_ref in enumerate(out_refs):
        out_ref[...] = rows[i * CHUNK_ROWS : (i + 1) * CHUNK_ROWS, :]


def project_shared_kernel(near_x, near_xy, far_x, far_xy, normed_ref, *rest):
    out_refs, weight = rest[:-1], rest[-1]
    half = lax.rem(lax.axis_index("req"), 2)
    core = lax.rem(lax.axis_index("ad"), 2)
    for n in range(len(out_refs)):
        weight[n, core, half] = near_x[n]
        weight[n, core, 1 - half] = near_xy[n]
        weight[n, 1 - core, half] = far_x[n]
        weight[n, 1 - core, 1 - half] = far_xy[n]
    project_chunks(weight, normed_ref, out_refs)


def project_direct_kernel(near_x, far_x, normed_ref, *rest):
    out_refs, weight = rest[:-1], rest[-1]
    core = lax.rem(lax.axis_index("ad"), 2)
    for n in range(len(out_refs)):
        weight[n, core] = near_x[n]
        weight[n, 1 - core] = far_x[n]
    project_chunks(weight, normed_ref, out_refs)


def project_chunks(weight, normed_ref, out_refs):
    step = 4 * HEAD_DIM
    rows = dot_nt(weight[...].reshape(len(out_refs) * step, weight.shape[-1]), normed_ref[...])
    for n, out_ref in enumerate(out_refs):
        out_ref[...] = rows[n * step : (n + 1) * step, :].reshape(out_ref.shape)


def put_rotated(target, index, rows, rope_ref, base):
    cosine = rope_ref[base : base + HALF, :]
    sine = rope_ref[base + HALF : base + 2 * HALF, :]
    first, second = rows[:HALF, :], rows[HALF:, :]
    target[index + (slice(0, HALF),)] = (first * cosine - second * sine).astype(BF16)
    target[index + (slice(HALF, HEAD_DIM),)] = (second * cosine + first * sine).astype(BF16)


def make_attend_kernel(i):
    def fill(query_rows, key_rows, value_rows, rope_ref, low_ref, up_t_ref, parts):
        for c in range(2):
            start = c * SHARD_HEADS * HEAD_DIM + i * CHUNK_ROWS
            delta = dot_nn(up_t_ref[start : start + CHUNK_ROWS, :], low_ref[0])
            for p in range(2):
                put_rotated(parts, (c, p), query_rows(c, p) + delta[p * HEAD_DIM : (p + 1) * HEAD_DIM, :], rope_ref, 2 * HALF)
        for p in range(2):
            start = (HEADS + i + 4 * p) * HEAD_DIM
            delta = dot_nn(up_t_ref[start : start + HEAD_DIM, :], low_ref[1])
            put_rotated(parts, (2, p), key_rows(p), rope_ref, 0)
            parts[3, p] = (value_rows(p) + delta).astype(BF16)

    def kernel(own_ref, near_ref, remote_ref, rope_ref, low_ref, up_t_ref, bias_ref, out_ref, local, parts, attended):
        shard = lax.axis_index("ad")
        side, core = shard // 2, lax.rem(shard, 2)
        local[core] = own_ref[...].reshape(local.shape[1:])
        local[1 - core] = near_ref[...].reshape(local.shape[1:])

        @pl.when(side == 0)
        def _():
            fill(
                lambda c, p: local[c, p], lambda p: remote_ref[0, p], lambda p: remote_ref[1, p],
                rope_ref, low_ref, up_t_ref, parts,
            )

        @pl.when(side == 1)
        def _():
            fill(
                lambda c, p: remote_ref[c, p], lambda p: local[0, p], lambda p: local[1, p],
                rope_ref, low_ref, up_t_ref, parts,
            )

        def lanes(b):
            return slice(b * LANES, (b + 1) * LANES)

        def score(b, p):
            key = parts[2, p, :, lanes(b)].T[:BLOCK, :]
            query = jnp.concatenate([parts[p, 0, :, lanes(b)], parts[p, 1, :, lanes(b)]], axis=1)
            return dot_nn(key, query)

        def soften(b, scores):
            bias = bias_ref[b]
            scores = scores + jnp.concatenate([bias, bias], axis=1)
            weights = jnp.exp2(scores - jnp.max(scores, axis=0, keepdims=True))
            probs = (weights * (1.0 / jnp.sum(weights, axis=0, keepdims=True))).astype(BF16)
            return jnp.concatenate([probs, jnp.zeros((LANES - BLOCK, 2 * LANES), BF16)], axis=0)

        def mingle(b, p, probs):
            result = dot_nn(parts[3, p, :, lanes(b)], probs).astype(BF16)
            for h in range(2):
                row = (2 * p + h) * HEAD_DIM
                attended[row : row + HEAD_DIM, lanes(b)] = result[:, h * LANES : (h + 1) * LANES]

        work = [(b, p) for b in range(bias_ref.shape[0]) for p in range(2)]
        ahead = 2
        scores = [score(*work[n]) for n in range(ahead)]
        probs = {}
        for n, (b, p) in enumerate(work):
            if n + ahead < len(work):
                scores.append(score(*work[n + ahead]))
            probs[n] = soften(b, scores[n])
            if n >= 1:
                mingle(*work[n - 1], probs.pop(n - 1))
        mingle(*work[-1], probs.pop(len(work) - 1))
        for b in range(bias_ref.shape[0]):
            out_ref[b * BLOCK : (b + 1) * BLOCK, :] = attended[:, lanes(b)].T[:BLOCK, :]

    return kernel


def weight_rows(w_ref, chunks, cols):
    half = SHARD_HEADS * HEAD_DIM
    pieces = [
        w_ref[c * half + i * CHUNK_ROWS : c * half + (i + 1) * CHUNK_ROWS, cols] for i in chunks for c in range(2)
    ]
    return jnp.concatenate(pieces, axis=0)


def make_mix_kernel(chunks):
    def kernel(x_ref, w_ref, *rest):
        parts, out_ref = rest[:-1], rest[-1]
        columns = 2 * LANES
        attended = jnp.concatenate([part[...] for part in parts], axis=1)
        for n in range(out_ref.shape[1] // columns):
            cols = slice(n * columns, (n + 1) * columns)
            total = x_ref[:, cols].astype(F32) + dot_nn(attended, weight_rows(w_ref, chunks, cols))
            out_ref[:, cols] = total.astype(out_ref.dtype)

    return kernel


def make_finish_kernel(chunks):
    def kernel(x_ref, w_ref, *rest):
        parts, out_hbm, ready, sems = rest[:-3], rest[-3], rest[-2], rest[-1]
        columns = ready.shape[2]
        attended = jnp.concatenate([part[...] for part in parts], axis=1)
        copies = []
        for n in range(ready.shape[0]):
            cols = slice(n * columns, (n + 1) * columns)
            total = x_ref[:, cols].astype(F32) + dot_nn(attended, weight_rows(w_ref, chunks, cols))
            ready[n] = total.astype(BF16)
            copies.append(pltpu.make_async_copy(ready.at[n], out_hbm.at[:, pl.ds(n * columns, columns)], sems.at[n]))
            copies[-1].start()
        for copy in copies:
            copy.wait()

    return kernel


def after(value, *others):
    return lax.optimization_barrier((value,) + others)[0]


def body(
    layer_input_hidden,
    input_norm_scale,
    query_key_value_weight,
    output_weight,
    adapter_down_weight,
    adapter_up_weight,
    prompt_token_length,
    request_adapter_index,
    adapter_holder_index,
):
    tokens, width = layer_input_hidden.shape
    blocks = tokens // BLOCK
    padded = blocks * LANES
    rank = adapter_up_weight.shape[1]
    features = adapter_up_weight.shape[2]
    shard_cols = query_key_value_weight.shape[1]
    shards, requests = lax.axis_size("ad"), lax.axis_size("req")
    other_side = [(a, a ^ 2) for a in range(shards)]
    other_core = [(a, a ^ 1) for a in range(shards)]

    def other_row(bit):
        return [(r, r ^ bit) for r in range(requests)]

    turned = pl.pallas_call(
        turn_kernel,
        out_shape=[jax.ShapeDtypeStruct((CHUNKS, 2, HEAD_DIM, width), BF16)]
        + [jax.ShapeDtypeStruct((len(chunks), HEAD_DIM, width), BF16) for chunks in SHARED]
        + [jax.ShapeDtypeStruct((len(DIRECT), 2, HEAD_DIM, width), BF16)],
        in_specs=[VMEM],
        out_specs=[VMEM] * (2 + len(SHARED)),
        scratch_shapes=[pltpu.VMEM((shard_cols, width), BF16)],
        compiler_params=params(20),
        name="turn_weight",
    )(query_key_value_weight)
    own, sends = turned[0], turned[1:]

    normed, rope, bias, slot, packed = pl.pallas_call(
        norm_kernel,
        out_shape=[
            jax.ShapeDtypeStruct((padded, width), BF16),
            jax.ShapeDtypeStruct((4 * HALF, padded), F32),
            jax.ShapeDtypeStruct((blocks, BLOCK, LANES), F32),
            jax.ShapeDtypeStruct((1, padded), jnp.int32),
            jax.ShapeDtypeStruct((1, 2 * rank, width), BF16),
        ],
        in_specs=[VMEM] * 5 + [SMEM] * 3,
        out_specs=[VMEM] * 5,
        compiler_params=params(16),
        cost_estimate=NO_COST,
        name="norm_tokens",
    )(
        layer_input_hidden, input_norm_scale, jnp.asarray(rope_tables()), adapter_down_weight, adapter_up_weight,
        prompt_token_length, request_adapter_index, adapter_holder_index,
    )

    def project(weight, name):
        return pl.pallas_call(
            project_kernel,
            out_shape=[jax.ShapeDtypeStruct((CHUNK_ROWS, padded), F32)] * CHUNKS,
            in_specs=[VMEM] * 2,
            out_specs=[VMEM] * CHUNKS,
            compiler_params=params(24),
            cost_estimate=NO_COST,
            name=name,
        )(weight, normed)

    def project_remote(kernel, chunks, arrays, token):
        return pl.pallas_call(
            kernel,
            out_shape=[jax.ShapeDtypeStruct((2, 2, HEAD_DIM, padded), F32)] * len(chunks),
            in_specs=[VMEM] * (len(arrays) + 1),
            out_specs=[VMEM] * len(chunks),
            scratch_shapes=[pltpu.VMEM((len(chunks), 2, 2, HEAD_DIM, width), BF16)],
            compiler_params=params(20),
            cost_estimate=NO_COST,
            name=f"project_{chunks[0]}",
        )(*arrays, after(normed, token))

    def attend(i, rows):
        return pl.pallas_call(
            make_attend_kernel(i),
            out_shape=jax.ShapeDtypeStruct((tokens, 4 * HEAD_DIM), BF16),
            in_specs=[VMEM] * 7,
            out_specs=VMEM,
            scratch_shapes=[
                pltpu.VMEM((2, 2, HEAD_DIM, padded), F32),
                pltpu.VMEM((4, 2, HEAD_DIM, padded), BF16),
                pltpu.VMEM((4 * HEAD_DIM, padded), BF16),
            ],
            compiler_params=params(16 if len(codes) <= 8 else 24),
            cost_estimate=NO_COST,
            name=f"attend_{i}",
        )(own_parts[i], near_parts[i], rows, rope, low, up_t, bias)

    def gather_adapters(packed, codes, bit, before, then):
        got = after(lax.ppermute(after(packed, before), "req", other_row(bit)), then)
        return jnp.concatenate([packed, got], axis=0), codes + [code ^ bit for code in codes]

    bits = []
    while 2 ** len(bits) < requests:
        bits.append(2 ** len(bits))
    bits = bits[:0:-1][:1] + bits[:1] + bits[:0:-1][1:]
    codes = [0]

    def along(piece, token):
        return lax.ppermute(after(piece, token), "req", other_row(1))

    def beside(piece, token):
        return lax.ppermute(after(piece, token), "ad", other_core)

    x_0, x_1, x_2 = [lax.ppermute(send, "ad", other_side) for send in sends]
    near = beside(own, own)
    for bit in bits[:1]:
        packed, codes = gather_adapters(packed, codes, bit, packed, packed)
    own_parts = project(after(own, normed), "project_own")
    xy_0, far_x_0 = along(x_0, own_parts[0]), beside(x_0, own_parts[0])
    near_parts = project(after(near, x_0), "project_near")
    for bit in bits[1:2]:
        packed, codes = gather_adapters(packed, codes, bit, normed, near_parts[0])
    for bit in bits[2:]:
        packed, codes = gather_adapters(packed, codes, bit, own_parts[0], own_parts[0])
    xy_1, far_x_1 = along(x_1, near_parts[0]), beside(x_1, own_parts[0])
    far_xy_0 = beside(xy_0, x_1)
    packed_other = beside(packed, own_parts[0])
    rows_0, rows_1 = project_remote(project_shared_kernel, SHARED[0], (x_0, xy_0, far_x_0, far_xy_0), near_parts[0])
    low, up_t = pl.pallas_call(
        make_low_kernel(codes, rank),
        out_shape=[
            jax.ShapeDtypeStruct((2, len(codes) * rank, padded), BF16),
            jax.ShapeDtypeStruct((features, len(codes) * rank), BF16),
        ],
        in_specs=[VMEM] * 4,
        out_specs=[VMEM] * 2,
        scratch_shapes=[pltpu.VMEM((2,) + packed.shape, BF16)],
        compiler_params=params(16 if len(codes) <= 8 else 48),
        cost_estimate=NO_COST,
        name="adapter_low",
    )(packed, packed_other, after(normed, rows_0), slot)
    attended = [attend(0, rows_0), attend(1, rows_1)]
    far_x_2 = beside(x_2, rows_0)
    far_xy_1 = beside(xy_1, low)
    (rows_2,) = project_remote(project_shared_kernel, SHARED[1], (x_1, xy_1, far_x_1, far_xy_1), attended[1])
    attended.append(attend(2, rows_2))

    def mix(base, chunks, kind, name):
        return pl.pallas_call(
            make_mix_kernel(chunks),
            out_shape=jax.ShapeDtypeStruct((tokens, width), kind),
            in_specs=[VMEM] * (2 + len(chunks)),
            out_specs=VMEM,
            compiler_params=params(24),
            cost_estimate=NO_COST,
            name=name,
        )(base, output_weight, *[attended[i] for i in chunks])

    partial = mix(layer_input_hidden, range(CHUNKS - 1), F32, "mix_first")
    (rows_3,) = project_remote(project_direct_kernel, DIRECT, (x_2, far_x_2), partial)
    attended.append(attend(CHUNKS - 1, rows_3))
    columns = 2 * LANES
    return pl.pallas_call(
        make_finish_kernel(range(CHUNKS - 1, CHUNKS)),
        out_shape=jax.ShapeDtypeStruct((tokens, width), BF16),
        in_specs=[VMEM] * 3,
        out_specs=HBM,
        scratch_shapes=[
            pltpu.VMEM((width // columns, tokens, columns), BF16),
            pltpu.SemaphoreType.DMA((width // columns,)),
        ],
        compiler_params=params(20),
        name="mix_last",
    )(partial, output_weight, attended[-1])


def solution(mesh):
    placed = (
        P(("req", "ad"), None),
        P(),
        P(None, "ad"),
        P(),
        P("req", None, None),
        P("req", None, None),
        P(("req", "ad"), None),
        P(("req", "ad"), None),
        P(),
    )
    return jax.shard_map(
        body, mesh=mesh, in_specs=placed, out_specs=P(("req", "ad"), None), check_vma=False
    )
```

```python
import math

import jax
import jax.numpy as jnp
import numpy as np
from jax import lax
from jax.experimental import pallas as pl
from jax.experimental.pallas import tpu as pltpu
from jax.sharding import PartitionSpec as P

HEADS = 16
KV_HEADS = 8
HEAD_DIM = 96
HALF = HEAD_DIM // 2
MAXLEN = 16
PAIR = 28
EPS = 1e-05
ROPE_THETA = 100000.0

GROUP = 4
BLOCK = GROUP * PAIR
LANES = 128
CHUNKS = 4
SHARD_HEADS = 8
CHUNK_ROWS = 2 * HEAD_DIM
SHARED = ((0, 1), (2,))
DIRECT = (3,)
LOG2E = 1.4426950408889634

F32 = jnp.float32
BF16 = jnp.bfloat16
VMEM = pl.BlockSpec(memory_space=pltpu.VMEM)
SMEM = pl.BlockSpec(memory_space=pltpu.SMEM)
HBM = pl.BlockSpec(memory_space=pltpu.HBM)
NO_COST = pl.CostEstimate(flops=0, bytes_accessed=0, transcendentals=0)


def params(mib):
    return pltpu.CompilerParams(vmem_limit_bytes=mib * 1024 * 1024)


def dot_nt(left, right):
    return lax.dot_general(left, right, (((1,), (1,)), ((), ())), preferred_element_type=F32)


def dot_nn(left, right):
    return lax.dot_general(left, right, (((1,), (0,)), ((), ())), preferred_element_type=F32)


def rope_tables():
    inverse = np.exp(-math.log(ROPE_THETA) * 2.0 * np.arange(HALF, dtype=np.float64) / HEAD_DIM)
    angles = inverse[:, None] * np.arange(MAXLEN, dtype=np.float64)[None, :]
    cosine, sine = np.cos(angles), np.sin(angles)
    scale = LOG2E / math.sqrt(HEAD_DIM)
    return np.concatenate([cosine, sine, cosine * scale, sine * scale], axis=0).astype(np.float32)


def group_of(index):
    found = jnp.zeros_like(index)
    for edge in range(1, GROUP + 1):
        found = found + jnp.where(index >= edge * PAIR, 1, 0)
    return found


def turn_kernel(w_ref, own_ref, *rest):
    send_refs, turned = rest[:-1], rest[-1]
    shard = lax.axis_index("ad")
    half = lax.rem(lax.axis_index("req"), 2)
    step = 4 * HEAD_DIM
    for g in range(w_ref.shape[1] // step):
        turned[g * step : (g + 1) * step, :] = w_ref[:, g * step : (g + 1) * step].T
    is_kv = shard >= 2
    for i in range(CHUNKS):
        for p in range(2):
            head = jnp.where(is_kv, i + 4 * p, 2 * i + p)
            own_ref[i, p] = turned[pl.ds(pl.multiple_of(head * HEAD_DIM, HEAD_DIM), HEAD_DIM), :]
    for send_ref, chunks in zip(send_refs, SHARED):
        for n, i in enumerate(chunks):
            send_ref[n] = own_ref[i, half]
    for n, i in enumerate(DIRECT):
        send_refs[-1][n] = own_ref[i]


def pack(down_ref, up_ref, out_ref):
    core = lax.rem(lax.axis_index("ad"), 2)
    rank, width = up_ref.shape[1], down_ref.shape[2]
    value_cols = up_ref.shape[2] - width

    @pl.when(core == 0)
    def _():
        out_ref[...] = down_ref[...]

    @pl.when(core == 1)
    def _():
        out_ref[0, :rank, :] = up_ref[0, :, :width]
        out_ref[0, rank:, :value_cols] = up_ref[0, :, width:]
        out_ref[0, rank:, value_cols:] = jnp.zeros((rank, width - value_cols), BF16)


def norm_kernel(
    x_ref, scale_ref, table_ref, down_ref, up_ref, len_ref, adapter_ref, holder_ref,
    normed_ref, rope_ref, bias_ref, slot_ref, pack_ref,
):
    pack(down_ref, up_ref, pack_ref)
    gain = scale_ref[...].reshape(1, scale_ref.shape[0])
    lane = lax.broadcasted_iota(jnp.int32, (1, LANES), 1)
    group = group_of(lane)
    within = lane - PAIR * group
    key_row = lax.broadcasted_iota(jnp.int32, (BLOCK, LANES), 0)
    query_col = lax.broadcasted_iota(jnp.int32, (BLOCK, LANES), 1)
    key_group = group_of(key_row)
    key_within = key_row - PAIR * key_group
    query_group = group_of(query_col)
    query_within = query_col - PAIR * query_group
    same_pair = (key_group == query_group) & (key_row <= query_col)
    dead = query_col >= BLOCK
    position_row = lax.broadcasted_iota(jnp.int32, (MAXLEN, LANES), 0)
    for b in range(bias_ref.shape[0]):
        lanes = slice(b * LANES, (b + 1) * LANES)
        first = jnp.zeros((1, LANES), jnp.int32)
        slot_first = jnp.zeros((1, LANES), jnp.int32)
        slot_second = jnp.zeros((1, LANES), jnp.int32)
        for g in range(GROUP):
            r = 2 * (GROUP * b + g)
            first = jnp.where(group == g, len_ref[0, r], first)
            slot_first = jnp.where(group == g, holder_ref[adapter_ref[0, r]], slot_first)
            slot_second = jnp.where(group == g, holder_ref[adapter_ref[0, r + 1]], slot_second)
        position = jnp.where(within < first, within, within - first)
        slot_ref[:, lanes] = jnp.where(within < first, slot_first, slot_second)
        onehot = jnp.where(position_row == position, 1.0, 0.0).astype(F32)
        rope_ref[:, lanes] = jnp.dot(
            table_ref[...], onehot, preferred_element_type=F32, precision=lax.Precision.HIGHEST
        )
        split = (key_within >= first) | (query_within < first)
        bias_ref[b] = jnp.where((same_pair & split) | dead, 0.0, -jnp.inf).astype(F32)
        rows = x_ref[b * BLOCK : (b + 1) * BLOCK, :].astype(F32)
        mean = jnp.mean(rows * rows, axis=-1, keepdims=True)
        normed_ref[b * LANES : b * LANES + BLOCK, :] = (rows * lax.rsqrt(mean + EPS) * gain).astype(BF16)
        normed_ref[b * LANES + BLOCK : (b + 1) * LANES, :] = jnp.zeros((LANES - BLOCK, rows.shape[1]), BF16)


def make_low_kernel(codes, rank):
    def kernel(mine_ref, other_ref, normed_ref, slot_ref, low_ref, up_t_ref, adapter):
        core = lax.rem(lax.axis_index("ad"), 2)
        me = lax.axis_index("req")
        count, rows, width = mine_ref.shape
        adapter[core] = mine_ref[...]
        adapter[1 - core] = other_ref[...]
        low = dot_nt(adapter[0].reshape(count * rows, width), normed_ref[...]).astype(BF16)
        slot = slot_ref[...]
        for j, code in enumerate(codes):
            mine = slot == me ^ code
            for part in range(2):
                r = (2 * j + part) * rank
                low_ref[part, j * rank : (j + 1) * rank, :] = jnp.where(mine, low[r : r + rank, :], jnp.zeros((), BF16))
        for part in range(2):
            stop = min(width, up_t_ref.shape[0] - part * width)
            step = 3 * LANES
            for start in range(0, stop, step):
                piece = adapter[1, :, part * rank : (part + 1) * rank, start : start + step]
                up_t_ref[part * width + start : part * width + start + step, :] = piece.reshape(count * rank, step).T

    return kernel


def project_kernel(w_ref, normed_ref, *out_refs):
    rows = dot_nt(w_ref[...].reshape(CHUNKS * CHUNK_ROWS, w_ref.shape[-1]), normed_ref[...])
    for i, out_ref in enumerate(out_refs):
        out_ref[...] = rows[i * CHUNK_ROWS : (i + 1) * CHUNK_ROWS, :]


def project_shared_kernel(near_x, near_xy, far_x, far_xy, normed_ref, *rest):
    out_refs, weight = rest[:-1], rest[-1]
    half = lax.rem(lax.axis_index("req"), 2)
    core = lax.rem(lax.axis_index("ad"), 2)
    for n in range(len(out_refs)):
        weight[n, core, half] = near_x[n]
        weight[n, core, 1 - half] = near_xy[n]
        weight[n, 1 - core, half] = far_x[n]
        weight[n, 1 - core, 1 - half] = far_xy[n]
    project_chunks(weight, normed_ref, out_refs)


def project_direct_kernel(near_x, far_x, normed_ref, *rest):
    out_refs, weight = rest[:-1], rest[-1]
    core = lax.rem(lax.axis_index("ad"), 2)
    for n in range(len(out_refs)):
        weight[n, core] = near_x[n]
        weight[n, 1 - core] = far_x[n]
    project_chunks(weight, normed_ref, out_refs)


def project_chunks(weight, normed_ref, out_refs):
    step = 4 * HEAD_DIM
    rows = dot_nt(weight[...].reshape(len(out_refs) * step, weight.shape[-1]), normed_ref[...])
    for n, out_ref in enumerate(out_refs):
        out_ref[...] = rows[n * step : (n + 1) * step, :].reshape(out_ref.shape)


def put_rotated(target, index, lanes, rows, rope_ref, base):
    cosine = rope_ref[base : base + HALF, lanes]
    sine = rope_ref[base + HALF : base + 2 * HALF, lanes]
    first, second = rows[:HALF, :], rows[HALF:, :]
    target[index + (slice(0, HALF), lanes)] = (first * cosine - second * sine).astype(BF16)
    target[index + (slice(HALF, HEAD_DIM), lanes)] = (second * cosine + first * sine).astype(BF16)


def make_attend_kernel(i):
    def run(query_rows, key_rows, value_rows, rope_ref, low_ref, up_t_ref, bias_ref, out_ref, parts):
        query_up = jnp.concatenate(
            [up_t_ref[start : start + CHUNK_ROWS, :] for start in (i * CHUNK_ROWS, (SHARD_HEADS + 2 * i) * HEAD_DIM)],
            axis=0,
        )
        value_up = jnp.concatenate(
            [up_t_ref[start : start + HEAD_DIM, :] for start in ((HEADS + i) * HEAD_DIM, (HEADS + i + 4) * HEAD_DIM)],
            axis=0,
        )

        def fill(g):
            lanes = slice(2 * g * LANES, 2 * (g + 1) * LANES)
            query_delta = dot_nn(query_up, low_ref[0, :, lanes])
            value_delta = dot_nn(value_up, low_ref[1, :, lanes])
            for p in range(2):
                put_rotated(parts, (2, p), lanes, key_rows(p, lanes), rope_ref, 0)
                for c in range(2):
                    row = (2 * c + p) * HEAD_DIM
                    rows = query_rows(c, p, lanes) + query_delta[row : row + HEAD_DIM, :]
                    put_rotated(parts, (c, p), lanes, rows, rope_ref, 2 * HALF)
                rows = value_rows(p, lanes) + value_delta[p * HEAD_DIM : (p + 1) * HEAD_DIM, :]
                parts[3, p, :, lanes] = rows.astype(BF16)

        def lanes_of(b):
            return slice(b * LANES, (b + 1) * LANES)

        def score(b, p):
            lanes = lanes_of(b)
            key = parts[2, p, :, lanes].T[:BLOCK, :]
            query = jnp.concatenate([parts[p, 0, :, lanes], parts[p, 1, :, lanes]], axis=1)
            return dot_nn(key, query)

        def soften(b, scores):
            bias = bias_ref[b]
            scores = scores + jnp.concatenate([bias, bias], axis=1)
            weights = jnp.exp2(scores - jnp.max(scores, axis=0, keepdims=True))
            probs = (weights * (1.0 / jnp.sum(weights, axis=0, keepdims=True))).astype(BF16)
            return jnp.concatenate([probs, jnp.zeros((LANES - BLOCK, 2 * LANES), BF16)], axis=0)

        def mingle(b, p, probs):
            result = dot_nn(parts[3, p, :, lanes_of(b)], probs).astype(BF16)
            return [result[:, :LANES], result[:, LANES:]]

        blocks = bias_ref.shape[0]
        work = [(b, p) for b in range(blocks) for p in range(2)]
        ahead = 3
        filled = 0
        scores, results = {}, {}
        for n in range(len(work) + ahead + 1):
            if n < len(work):
                while filled < blocks // 2 and 2 * filled <= min(work[n][0] + 2, blocks - 1):
                    fill(filled)
                    filled += 1
                scores[n] = score(*work[n])
            m = n - ahead
            if 0 <= m < len(work):
                scores[m] = soften(work[m][0], scores[m])
            m -= 1
            if 0 <= m < len(work):
                b, p = work[m]
                results[p] = mingle(b, p, scores.pop(m))
                if p == 1:
                    heads = jnp.concatenate(results.pop(0) + results.pop(1), axis=0)
                    out_ref[b * BLOCK : (b + 1) * BLOCK, :] = heads.T[:BLOCK, :]

    def kernel(own_ref, near_ref, remote_ref, rope_ref, low_ref, up_t_ref, bias_ref, out_ref, local, parts):
        shard = lax.axis_index("ad")
        side, core = shard // 2, lax.rem(shard, 2)
        local[core] = own_ref[...].reshape(local.shape[1:])
        local[1 - core] = near_ref[...].reshape(local.shape[1:])
        rest = (rope_ref, low_ref, up_t_ref, bias_ref, out_ref, parts)

        @pl.when(side == 0)
        def _():
            run(
                lambda c, p, lanes: local[c, p, :, lanes],
                lambda p, lanes: remote_ref[0, p, :, lanes],
                lambda p, lanes: remote_ref[1, p, :, lanes],
                *rest,
            )

        @pl.when(side == 1)
        def _():
            run(
                lambda c, p, lanes: remote_ref[c, p, :, lanes],
                lambda p, lanes: local[0, p, :, lanes],
                lambda p, lanes: local[1, p, :, lanes],
                *rest,
            )

    return kernel


def weight_rows(w_ref, chunks, cols):
    half = SHARD_HEADS * HEAD_DIM
    pieces = [
        w_ref[c * half + i * CHUNK_ROWS : c * half + (i + 1) * CHUNK_ROWS, cols] for i in chunks for c in range(2)
    ]
    return jnp.concatenate(pieces, axis=0)


def make_mix_kernel(chunks):
    def kernel(x_ref, w_ref, *rest):
        parts, out_ref = rest[:-1], rest[-1]
        columns = 2 * LANES
        attended = jnp.concatenate([part[...] for part in parts], axis=1)
        for n in range(out_ref.shape[1] // columns):
            cols = slice(n * columns, (n + 1) * columns)
            total = x_ref[:, cols].astype(F32) + dot_nn(attended, weight_rows(w_ref, chunks, cols))
            out_ref[:, cols] = total.astype(out_ref.dtype)

    return kernel


def make_finish_kernel(chunks):
    def kernel(x_ref, w_ref, *rest):
        parts, out_hbm, ready, sems = rest[:-3], rest[-3], rest[-2], rest[-1]
        groups = sems.shape[0]
        rows = ready.shape[0] // groups
        weight = weight_rows(w_ref, chunks, slice(None))
        copies = []
        for n in range(groups):
            part = slice(n * rows, (n + 1) * rows)
            attended = jnp.concatenate([part_ref[part, :] for part_ref in parts], axis=1)
            ready[part, :] = (x_ref[part, :].astype(F32) + dot_nn(attended, weight)).astype(BF16)
            copies.append(pltpu.make_async_copy(ready.at[part], out_hbm.at[part], sems.at[n]))
            copies[-1].start()
        for copy in copies:
            copy.wait()

    return kernel


def after(value, *others):
    return lax.optimization_barrier((value,) + others)[0]


def body(
    layer_input_hidden,
    input_norm_scale,
    query_key_value_weight,
    output_weight,
    adapter_down_weight,
    adapter_up_weight,
    prompt_token_length,
    request_adapter_index,
    adapter_holder_index,
):
    tokens, width = layer_input_hidden.shape
    blocks = tokens // BLOCK
    padded = blocks * LANES
    rank = adapter_up_weight.shape[1]
    features = adapter_up_weight.shape[2]
    shard_cols = query_key_value_weight.shape[1]
    shards, requests = lax.axis_size("ad"), lax.axis_size("req")
    other_side = [(a, a ^ 2) for a in range(shards)]
    other_core = [(a, a ^ 1) for a in range(shards)]

    def other_row(bit):
        return [(r, r ^ bit) for r in range(requests)]

    turned = pl.pallas_call(
        turn_kernel,
        out_shape=[jax.ShapeDtypeStruct((CHUNKS, 2, HEAD_DIM, width), BF16)]
        + [jax.ShapeDtypeStruct((len(chunks), HEAD_DIM, width), BF16) for chunks in SHARED]
        + [jax.ShapeDtypeStruct((len(DIRECT), 2, HEAD_DIM, width), BF16)],
        in_specs=[VMEM],
        out_specs=[VMEM] * (2 + len(SHARED)),
        scratch_shapes=[pltpu.VMEM((shard_cols, width), BF16)],
        compiler_params=params(20),
        name="turn_weight",
    )(query_key_value_weight)
    own, sends = turned[0], turned[1:]

    normed, rope, bias, slot, packed = pl.pallas_call(
        norm_kernel,
        out_shape=[
            jax.ShapeDtypeStruct((padded, width), BF16),
            jax.ShapeDtypeStruct((4 * HALF, padded), F32),
            jax.ShapeDtypeStruct((blocks, BLOCK, LANES), F32),
            jax.ShapeDtypeStruct((1, padded), jnp.int32),
            jax.ShapeDtypeStruct((1, 2 * rank, width), BF16),
        ],
        in_specs=[VMEM] * 5 + [SMEM] * 3,
        out_specs=[VMEM] * 5,
        compiler_params=params(16),
        cost_estimate=NO_COST,
        name="norm_tokens",
    )(
        layer_input_hidden, input_norm_scale, jnp.asarray(rope_tables()), adapter_down_weight, adapter_up_weight,
        prompt_token_length, request_adapter_index, adapter_holder_index,
    )

    def project(weight, name):
        return pl.pallas_call(
            project_kernel,
            out_shape=[jax.ShapeDtypeStruct((CHUNK_ROWS, padded), F32)] * CHUNKS,
            in_specs=[VMEM] * 2,
            out_specs=[VMEM] * CHUNKS,
            compiler_params=params(24),
            cost_estimate=NO_COST,
            name=name,
        )(weight, normed)

    def project_remote(kernel, chunks, arrays, token):
        return pl.pallas_call(
            kernel,
            out_shape=[jax.ShapeDtypeStruct((2, 2, HEAD_DIM, padded), F32)] * len(chunks),
            in_specs=[VMEM] * (len(arrays) + 1),
            out_specs=[VMEM] * len(chunks),
            scratch_shapes=[pltpu.VMEM((len(chunks), 2, 2, HEAD_DIM, width), BF16)],
            compiler_params=params(20),
            cost_estimate=NO_COST,
            name=f"project_{chunks[0]}",
        )(*arrays, after(normed, token))

    def attend(i, rows):
        return pl.pallas_call(
            make_attend_kernel(i),
            out_shape=jax.ShapeDtypeStruct((tokens, 4 * HEAD_DIM), BF16),
            in_specs=[VMEM] * 7,
            out_specs=VMEM,
            scratch_shapes=[
                pltpu.VMEM((2, 2, HEAD_DIM, padded), F32),
                pltpu.VMEM((4, 2, HEAD_DIM, padded), BF16),
            ],
            compiler_params=params(16 if len(codes) <= 8 else 24),
            cost_estimate=NO_COST,
            name=f"attend_{i}",
        )(own_parts[i], near_parts[i], rows, rope, low, up_t, bias)

    def gather_adapters(packed, codes, bit, before, then):
        got = after(lax.ppermute(after(packed, before), "req", other_row(bit)), then)
        return jnp.concatenate([packed, got], axis=0), codes + [code ^ bit for code in codes]

    bits = []
    while 2 ** len(bits) < requests:
        bits.append(2 ** len(bits))
    bits = bits[:0:-1][:1] + bits[:1] + bits[:0:-1][1:]
    codes = [0]

    def along(piece, token):
        return lax.ppermute(after(piece, token), "req", other_row(1))

    def beside(piece, token):
        return lax.ppermute(after(piece, token), "ad", other_core)

    x_0, x_1, x_2 = [lax.ppermute(send, "ad", other_side) for send in sends]
    near = beside(own, own)
    for bit in bits[:1]:
        packed, codes = gather_adapters(packed, codes, bit, packed, packed)
    own_parts = project(after(own, normed), "project_own")
    xy_0, far_x_0 = along(x_0, own_parts[0]), beside(x_0, own_parts[0])
    near_parts = project(after(near, x_0), "project_near")
    for bit in bits[1:2]:
        packed, codes = gather_adapters(packed, codes, bit, normed, near_parts[0])
    for bit in bits[2:]:
        packed, codes = gather_adapters(packed, codes, bit, own_parts[0], own_parts[0])
    xy_1, far_x_1 = along(x_1, near_parts[0]), beside(x_1, own_parts[0])
    far_xy_0 = beside(xy_0, x_1)
    packed_other = beside(packed, own_parts[0])
    rows_0, rows_1 = project_remote(project_shared_kernel, SHARED[0], (x_0, xy_0, far_x_0, far_xy_0), near_parts[0])
    low, up_t = pl.pallas_call(
        make_low_kernel(codes, rank),
        out_shape=[
            jax.ShapeDtypeStruct((2, len(codes) * rank, padded), BF16),
            jax.ShapeDtypeStruct((features, len(codes) * rank), BF16),
        ],
        in_specs=[VMEM] * 4,
        out_specs=[VMEM] * 2,
        scratch_shapes=[pltpu.VMEM((2,) + packed.shape, BF16)],
        compiler_params=params(16 if len(codes) <= 8 else 48),
        cost_estimate=NO_COST,
        name="adapter_low",
    )(packed, packed_other, after(normed, rows_0), slot)
    attended = [attend(0, rows_0), attend(1, rows_1)]
    far_x_2 = beside(x_2, rows_0)
    far_xy_1 = beside(xy_1, attended[0])
    (rows_2,) = project_remote(project_shared_kernel, SHARED[1], (x_1, xy_1, far_x_1, far_xy_1), attended[1])
    attended.append(attend(2, rows_2))

    def mix(base, chunks, kind, name):
        return pl.pallas_call(
            make_mix_kernel(chunks),
            out_shape=jax.ShapeDtypeStruct((tokens, width), kind),
            in_specs=[VMEM] * (2 + len(chunks)),
            out_specs=VMEM,
            compiler_params=params(24),
            cost_estimate=NO_COST,
            name=name,
        )(base, output_weight, *[attended[i] for i in chunks])

    partial = mix(layer_input_hidden, range(CHUNKS - 1), F32, "mix_first")
    (rows_3,) = project_remote(project_direct_kernel, DIRECT, (x_2, far_x_2), partial)
    attended.append(attend(CHUNKS - 1, rows_3))
    return pl.pallas_call(
        make_finish_kernel(range(CHUNKS - 1, CHUNKS)),
        out_shape=jax.ShapeDtypeStruct((tokens, width), BF16),
        in_specs=[VMEM] * 3,
        out_specs=HBM,
        scratch_shapes=[pltpu.VMEM((tokens, width), BF16), pltpu.SemaphoreType.DMA((tokens // (2 * BLOCK),))],
        compiler_params=params(20),
        name="mix_last",
    )(partial, output_weight, attended[-1])


def solution(mesh):
    placed = (
        P(("req", "ad"), None),
        P(),
        P(None, "ad"),
        P(),
        P("req", None, None),
        P("req", None, None),
        P(("req", "ad"), None),
        P(("req", "ad"), None),
        P(),
    )
    return jax.shard_map(
        body, mesh=mesh, in_specs=placed, out_specs=P(("req", "ad"), None), check_vma=False
    )
```

```python
import math

import jax
import jax.numpy as jnp
import numpy as np
from jax import lax
from jax.experimental import pallas as pl
from jax.experimental.pallas import tpu as pltpu
from jax.sharding import PartitionSpec as P

HEADS = 16
KV_HEADS = 8
HEAD_DIM = 96
HALF = HEAD_DIM // 2
MAXLEN = 16
PAIR = 28
EPS = 1e-05
ROPE_THETA = 100000.0

GROUP = 4
BLOCK = GROUP * PAIR
LANES = 128
CHUNKS = 4
SHARD_HEADS = 8
CHUNK_ROWS = 2 * HEAD_DIM
SHARED = ((0, 1), (2,))
DIRECT = (3,)
LOG2E = 1.4426950408889634

F32 = jnp.float32
BF16 = jnp.bfloat16
VMEM = pl.BlockSpec(memory_space=pltpu.VMEM)
SMEM = pl.BlockSpec(memory_space=pltpu.SMEM)
HBM = pl.BlockSpec(memory_space=pltpu.HBM)
NO_COST = pl.CostEstimate(flops=0, bytes_accessed=0, transcendentals=0)


def params(mib):
    return pltpu.CompilerParams(vmem_limit_bytes=mib * 1024 * 1024)


def dot_nt(left, right):
    return lax.dot_general(left, right, (((1,), (1,)), ((), ())), preferred_element_type=F32)


def dot_nn(left, right):
    return lax.dot_general(left, right, (((1,), (0,)), ((), ())), preferred_element_type=F32)


def rope_tables():
    inverse = np.exp(-math.log(ROPE_THETA) * 2.0 * np.arange(HALF, dtype=np.float64) / HEAD_DIM)
    angles = inverse[:, None] * np.arange(MAXLEN, dtype=np.float64)[None, :]
    cosine, sine = np.cos(angles), np.sin(angles)
    scale = LOG2E / math.sqrt(HEAD_DIM)
    return np.concatenate([cosine, sine, cosine * scale, sine * scale], axis=0).astype(np.float32)


def group_of(index):
    found = jnp.zeros_like(index)
    for edge in range(1, GROUP + 1):
        found = found + jnp.where(index >= edge * PAIR, 1, 0)
    return found


def turn_kernel(w_ref, own_ref, *rest):
    send_refs, turned = rest[:-1], rest[-1]
    shard = lax.axis_index("ad")
    half = lax.rem(lax.axis_index("req"), 2)
    step = 4 * HEAD_DIM
    for g in range(w_ref.shape[1] // step):
        turned[g * step : (g + 1) * step, :] = w_ref[:, g * step : (g + 1) * step].T
    is_kv = shard >= 2
    for i in range(CHUNKS):
        for p in range(2):
            head = jnp.where(is_kv, i + 4 * p, 2 * i + p)
            own_ref[i, p] = turned[pl.ds(pl.multiple_of(head * HEAD_DIM, HEAD_DIM), HEAD_DIM), :]
    for send_ref, chunks in zip(send_refs, SHARED):
        for n, i in enumerate(chunks):
            send_ref[n] = own_ref[i, half]
    for n, i in enumerate(DIRECT):
        send_refs[-1][n] = own_ref[i]


def pack(down_ref, up_ref, out_ref):
    core = lax.rem(lax.axis_index("ad"), 2)
    rank, width = up_ref.shape[1], down_ref.shape[2]
    value_cols = up_ref.shape[2] - width

    @pl.when(core == 0)
    def _():
        out_ref[...] = down_ref[...]

    @pl.when(core == 1)
    def _():
        out_ref[0, :rank, :] = up_ref[0, :, :width]
        out_ref[0, rank:, :value_cols] = up_ref[0, :, width:]
        out_ref[0, rank:, value_cols:] = jnp.zeros((rank, width - value_cols), BF16)


def norm_kernel(
    x_ref, scale_ref, table_ref, down_ref, up_ref, len_ref, adapter_ref, holder_ref,
    normed_ref, rope_ref, bias_ref, slot_ref, pack_ref,
):
    pack(down_ref, up_ref, pack_ref)
    gain = scale_ref[...].reshape(1, scale_ref.shape[0])
    lane = lax.broadcasted_iota(jnp.int32, (1, LANES), 1)
    group = group_of(lane)
    within = lane - PAIR * group
    key_row = lax.broadcasted_iota(jnp.int32, (BLOCK, LANES), 0)
    query_col = lax.broadcasted_iota(jnp.int32, (BLOCK, LANES), 1)
    key_group = group_of(key_row)
    key_within = key_row - PAIR * key_group
    query_group = group_of(query_col)
    query_within = query_col - PAIR * query_group
    same_pair = (key_group == query_group) & (key_row <= query_col)
    dead = query_col >= BLOCK
    position_row = lax.broadcasted_iota(jnp.int32, (MAXLEN, LANES), 0)
    for b in range(bias_ref.shape[0]):
        lanes = slice(b * LANES, (b + 1) * LANES)
        first = jnp.zeros((1, LANES), jnp.int32)
        slot_first = jnp.zeros((1, LANES), jnp.int32)
        slot_second = jnp.zeros((1, LANES), jnp.int32)
        for g in range(GROUP):
            r = 2 * (GROUP * b + g)
            first = jnp.where(group == g, len_ref[0, r], first)
            slot_first = jnp.where(group == g, holder_ref[adapter_ref[0, r]], slot_first)
            slot_second = jnp.where(group == g, holder_ref[adapter_ref[0, r + 1]], slot_second)
        position = jnp.where(within < first, within, within - first)
        slot_ref[:, lanes] = jnp.where(within < first, slot_first, slot_second)
        onehot = jnp.where(position_row == position, 1.0, 0.0).astype(F32)
        rope_ref[:, lanes] = jnp.dot(
            table_ref[...], onehot, preferred_element_type=F32, precision=lax.Precision.HIGHEST
        )
        split = (key_within >= first) | (query_within < first)
        bias_ref[b] = jnp.where((same_pair & split) | dead, 0.0, -jnp.inf).astype(F32)
        rows = x_ref[b * BLOCK : (b + 1) * BLOCK, :].astype(F32)
        mean = jnp.mean(rows * rows, axis=-1, keepdims=True)
        normed_ref[b * LANES : b * LANES + BLOCK, :] = (rows * lax.rsqrt(mean + EPS) * gain).astype(BF16)
        normed_ref[b * LANES + BLOCK : (b + 1) * LANES, :] = jnp.zeros((LANES - BLOCK, rows.shape[1]), BF16)


def make_low_kernel(codes, rank):
    def kernel(mine_ref, other_ref, normed_ref, slot_ref, low_ref, up_t_ref, adapter):
        core = lax.rem(lax.axis_index("ad"), 2)
        me = lax.axis_index("req")
        count, rows, width = mine_ref.shape
        adapter[core] = mine_ref[...]
        adapter[1 - core] = other_ref[...]
        low = dot_nt(adapter[0].reshape(count * rows, width), normed_ref[...]).astype(BF16)
        slot = slot_ref[...]
        for j, code in enumerate(codes):
            mine = slot == me ^ code
            for part in range(2):
                r = (2 * j + part) * rank
                low_ref[part, j * rank : (j + 1) * rank, :] = jnp.where(mine, low[r : r + rank, :], jnp.zeros((), BF16))
        for part in range(2):
            stop = min(width, up_t_ref.shape[0] - part * width)
            step = 3 * LANES
            for start in range(0, stop, step):
                piece = adapter[1, :, part * rank : (part + 1) * rank, start : start + step]
                up_t_ref[part * width + start : part * width + start + step, :] = piece.reshape(count * rank, step).T

    return kernel


def project_kernel(w_ref, normed_ref, *out_refs):
    rows = dot_nt(w_ref[...].reshape(CHUNKS * CHUNK_ROWS, w_ref.shape[-1]), normed_ref[...])
    for i, out_ref in enumerate(out_refs):
        out_ref[...] = rows[i * CHUNK_ROWS : (i + 1) * CHUNK_ROWS, :]


def project_shared_kernel(near_x, near_xy, far_x, far_xy, normed_ref, *rest):
    out_refs, weight = rest[:-1], rest[-1]
    half = lax.rem(lax.axis_index("req"), 2)
    core = lax.rem(lax.axis_index("ad"), 2)
    for n in range(len(out_refs)):
        weight[n, core, half] = near_x[n]
        weight[n, core, 1 - half] = near_xy[n]
        weight[n, 1 - core, half] = far_x[n]
        weight[n, 1 - core, 1 - half] = far_xy[n]
    project_chunks(weight, normed_ref, out_refs)


def project_direct_kernel(near_x, far_x, normed_ref, *rest):
    out_refs, weight = rest[:-1], rest[-1]
    core = lax.rem(lax.axis_index("ad"), 2)
    for n in range(len(out_refs)):
        weight[n, core] = near_x[n]
        weight[n, 1 - core] = far_x[n]
    project_chunks(weight, normed_ref, out_refs)


def project_chunks(weight, normed_ref, out_refs):
    step = 4 * HEAD_DIM
    rows = dot_nt(weight[...].reshape(len(out_refs) * step, weight.shape[-1]), normed_ref[...])
    for n, out_ref in enumerate(out_refs):
        out_ref[...] = rows[n * step : (n + 1) * step, :].reshape(out_ref.shape)


def put_rotated(target, index, lanes, rows, rope_ref, base):
    cosine = rope_ref[base : base + HALF, lanes]
    sine = rope_ref[base + HALF : base + 2 * HALF, lanes]
    first, second = rows[:HALF, :], rows[HALF:, :]
    target[index + (slice(0, HALF), lanes)] = (first * cosine - second * sine).astype(BF16)
    target[index + (slice(HALF, HEAD_DIM), lanes)] = (second * cosine + first * sine).astype(BF16)


def make_attend_kernel(i):
    def run(query_rows, key_rows, value_rows, rope_ref, low_ref, up_t_ref, bias_ref, out_ref, parts):
        query_up = jnp.concatenate(
            [up_t_ref[start : start + CHUNK_ROWS, :] for start in (i * CHUNK_ROWS, (SHARD_HEADS + 2 * i) * HEAD_DIM)],
            axis=0,
        )
        value_up = jnp.concatenate(
            [up_t_ref[start : start + HEAD_DIM, :] for start in ((HEADS + i) * HEAD_DIM, (HEADS + i + 4) * HEAD_DIM)],
            axis=0,
        )

        def fill(g):
            lanes = slice(2 * g * LANES, 2 * (g + 1) * LANES)
            query_delta = dot_nn(query_up, low_ref[0, :, lanes])
            value_delta = dot_nn(value_up, low_ref[1, :, lanes])
            for p in range(2):
                put_rotated(parts, (2, p), lanes, key_rows(p, lanes), rope_ref, 0)
                for c in range(2):
                    row = (2 * c + p) * HEAD_DIM
                    rows = query_rows(c, p, lanes) + query_delta[row : row + HEAD_DIM, :]
                    put_rotated(parts, (c, p), lanes, rows, rope_ref, 2 * HALF)
                rows = value_rows(p, lanes) + value_delta[p * HEAD_DIM : (p + 1) * HEAD_DIM, :]
                parts[3, p, :, lanes] = rows.astype(BF16)

        def lanes_of(b):
            return slice(b * LANES, (b + 1) * LANES)

        def score(b, p):
            lanes = lanes_of(b)
            key = parts[2, p, :, lanes].T[:BLOCK, :]
            query = jnp.concatenate([parts[p, 0, :, lanes], parts[p, 1, :, lanes]], axis=1)
            return dot_nn(key, query)

        def soften(b, scores):
            bias = bias_ref[b]
            scores = scores + jnp.concatenate([bias, bias], axis=1)
            weights = jnp.exp2(scores - jnp.max(scores, axis=0, keepdims=True))
            probs = (weights * (1.0 / jnp.sum(weights, axis=0, keepdims=True))).astype(BF16)
            return jnp.concatenate([probs, jnp.zeros((LANES - BLOCK, 2 * LANES), BF16)], axis=0)

        def mingle(b, p, probs):
            result = dot_nn(parts[3, p, :, lanes_of(b)], probs).astype(BF16)
            return [result[:, :LANES], result[:, LANES:]]

        blocks = bias_ref.shape[0]
        work = [(b, p) for b in range(blocks) for p in range(2)]
        ahead = 3
        filled = 0
        scores, results = {}, {}
        for n in range(len(work) + ahead + 1):
            if n < len(work):
                while filled < blocks // 2 and 2 * filled <= min(work[n][0] + 2, blocks - 1):
                    fill(filled)
                    filled += 1
                scores[n] = score(*work[n])
            m = n - ahead
            if 0 <= m < len(work):
                scores[m] = soften(work[m][0], scores[m])
            m -= 1
            if 0 <= m < len(work):
                b, p = work[m]
                results[p] = mingle(b, p, scores.pop(m))
                if p == 1:
                    heads = jnp.concatenate(results.pop(0) + results.pop(1), axis=0)
                    out_ref[b * BLOCK : (b + 1) * BLOCK, :] = heads.T[:BLOCK, :]

    def kernel(own_ref, near_ref, remote_ref, rope_ref, low_ref, up_t_ref, bias_ref, out_ref, local, parts):
        shard = lax.axis_index("ad")
        side, core = shard // 2, lax.rem(shard, 2)
        local[core] = own_ref[...].reshape(local.shape[1:])
        local[1 - core] = near_ref[...].reshape(local.shape[1:])
        rest = (rope_ref, low_ref, up_t_ref, bias_ref, out_ref, parts)

        @pl.when(side == 0)
        def _():
            run(
                lambda c, p, lanes: local[c, p, :, lanes],
                lambda p, lanes: remote_ref[0, p, :, lanes],
                lambda p, lanes: remote_ref[1, p, :, lanes],
                *rest,
            )

        @pl.when(side == 1)
        def _():
            run(
                lambda c, p, lanes: remote_ref[c, p, :, lanes],
                lambda p, lanes: local[0, p, :, lanes],
                lambda p, lanes: local[1, p, :, lanes],
                *rest,
            )

    return kernel


def mix_kernel(x_ref, w_ref, *rest):
    parts, out_hbm, ready, sems = rest[:CHUNKS], rest[CHUNKS], rest[CHUNKS + 1], rest[CHUNKS + 2]
    half = SHARD_HEADS * HEAD_DIM
    columns = ready.shape[2]
    attended = jnp.concatenate([part[...] for part in parts], axis=1)
    copies = []
    for n in range(ready.shape[0]):
        cols = slice(n * columns, (n + 1) * columns)
        weight = jnp.concatenate(
            [
                w_ref[c * half + i * CHUNK_ROWS : c * half + (i + 1) * CHUNK_ROWS, cols]
                for i in range(CHUNKS)
                for c in range(2)
            ],
            axis=0,
        )
        ready[n] = (x_ref[:, cols].astype(F32) + dot_nn(attended, weight)).astype(BF16)
        copies.append(pltpu.make_async_copy(ready.at[n], out_hbm.at[:, pl.ds(n * columns, columns)], sems.at[n]))
        copies[-1].start()
    for copy in copies:
        copy.wait()


def after(value, *others):
    return lax.optimization_barrier((value,) + others)[0]


def body(
    layer_input_hidden,
    input_norm_scale,
    query_key_value_weight,
    output_weight,
    adapter_down_weight,
    adapter_up_weight,
    prompt_token_length,
    request_adapter_index,
    adapter_holder_index,
):
    tokens, width = layer_input_hidden.shape
    blocks = tokens // BLOCK
    padded = blocks * LANES
    rank = adapter_up_weight.shape[1]
    features = adapter_up_weight.shape[2]
    shard_cols = query_key_value_weight.shape[1]
    shards, requests = lax.axis_size("ad"), lax.axis_size("req")
    other_side = [(a, a ^ 2) for a in range(shards)]
    other_core = [(a, a ^ 1) for a in range(shards)]

    def other_row(bit):
        return [(r, r ^ bit) for r in range(requests)]

    turned = pl.pallas_call(
        turn_kernel,
        out_shape=[jax.ShapeDtypeStruct((CHUNKS, 2, HEAD_DIM, width), BF16)]
        + [jax.ShapeDtypeStruct((len(chunks), HEAD_DIM, width), BF16) for chunks in SHARED]
        + [jax.ShapeDtypeStruct((len(DIRECT), 2, HEAD_DIM, width), BF16)],
        in_specs=[VMEM],
        out_specs=[VMEM] * (2 + len(SHARED)),
        scratch_shapes=[pltpu.VMEM((shard_cols, width), BF16)],
        compiler_params=params(20),
        name="turn_weight",
    )(query_key_value_weight)
    own, sends = turned[0], turned[1:]

    normed, rope, bias, slot, packed = pl.pallas_call(
        norm_kernel,
        out_shape=[
            jax.ShapeDtypeStruct((padded, width), BF16),
            jax.ShapeDtypeStruct((4 * HALF, padded), F32),
            jax.ShapeDtypeStruct((blocks, BLOCK, LANES), F32),
            jax.ShapeDtypeStruct((1, padded), jnp.int32),
            jax.ShapeDtypeStruct((1, 2 * rank, width), BF16),
        ],
        in_specs=[VMEM] * 5 + [SMEM] * 3,
        out_specs=[VMEM] * 5,
        compiler_params=params(16),
        cost_estimate=NO_COST,
        name="norm_tokens",
    )(
        layer_input_hidden, input_norm_scale, jnp.asarray(rope_tables()), adapter_down_weight, adapter_up_weight,
        prompt_token_length, request_adapter_index, adapter_holder_index,
    )

    def project(weight, name):
        return pl.pallas_call(
            project_kernel,
            out_shape=[jax.ShapeDtypeStruct((CHUNK_ROWS, padded), F32)] * CHUNKS,
            in_specs=[VMEM] * 2,
            out_specs=[VMEM] * CHUNKS,
            compiler_params=params(24),
            cost_estimate=NO_COST,
            name=name,
        )(weight, normed)

    def project_remote(kernel, chunks, arrays, token):
        return pl.pallas_call(
            kernel,
            out_shape=[jax.ShapeDtypeStruct((2, 2, HEAD_DIM, padded), F32)] * len(chunks),
            in_specs=[VMEM] * (len(arrays) + 1),
            out_specs=[VMEM] * len(chunks),
            scratch_shapes=[pltpu.VMEM((len(chunks), 2, 2, HEAD_DIM, width), BF16)],
            compiler_params=params(20),
            cost_estimate=NO_COST,
            name=f"project_{chunks[0]}",
        )(*arrays, after(normed, token))

    def attend(i, rows):
        return pl.pallas_call(
            make_attend_kernel(i),
            out_shape=jax.ShapeDtypeStruct((tokens, 4 * HEAD_DIM), BF16),
            in_specs=[VMEM] * 7,
            out_specs=VMEM,
            scratch_shapes=[
                pltpu.VMEM((2, 2, HEAD_DIM, padded), F32),
                pltpu.VMEM((4, 2, HEAD_DIM, padded), BF16),
            ],
            compiler_params=params(16 if len(codes) <= 8 else 24),
            cost_estimate=NO_COST,
            name=f"attend_{i}",
        )(own_parts[i], near_parts[i], rows, rope, low, up_t, bias)

    def gather_adapters(packed, codes, bit, before, then):
        got = after(lax.ppermute(after(packed, before), "req", other_row(bit)), then)
        return jnp.concatenate([packed, got], axis=0), codes + [code ^ bit for code in codes]

    def along(piece, token):
        return lax.ppermute(after(piece, token), "req", other_row(1))

    def beside(piece, token):
        return lax.ppermute(after(piece, token), "ad", other_core)

    x = [lax.ppermute(send, "ad", other_side) for send in sends]
    near = beside(own, own)
    xy, far_x, far_xy, rows, attended = [], [], [], [], []

    def project_shared(i, *tokens):
        arrays = (x[i], xy[i], far_x[i], far_xy[i])
        rows.extend(project_remote(project_shared_kernel, SHARED[i], arrays, *tokens))

    bits = []
    while 2 ** len(bits) < requests:
        bits.append(2 ** len(bits))
    bits = bits[:1] + bits[:0:-1]
    codes = [0]
    for bit in bits[:1]:
        packed, codes = gather_adapters(packed, codes, bit, packed, packed)
    own_parts = project(after(own, normed, packed), "project_own")
    xy.append(along(x[0], normed))
    far_x.append(beside(x[0], own_parts[0]))
    near_parts = project(after(near, x[0]), "project_near")
    for bit in bits[1:2]:
        packed, codes = gather_adapters(packed, codes, bit, normed, near_parts[0])
    xy.append(along(x[1], near_parts[0]))
    far_x.append(beside(x[1], own_parts[0]))
    far_xy.append(beside(xy[0], x[1]))
    for bit in bits[2:]:
        packed, codes = gather_adapters(packed, codes, bit, own_parts[0], own_parts[0])
    packed_other = beside(packed, own_parts[0])
    project_shared(0, near_parts[0])
    low, up_t = pl.pallas_call(
        make_low_kernel(codes, rank),
        out_shape=[
            jax.ShapeDtypeStruct((2, len(codes) * rank, padded), BF16),
            jax.ShapeDtypeStruct((features, len(codes) * rank), BF16),
        ],
        in_specs=[VMEM] * 4,
        out_specs=[VMEM] * 2,
        scratch_shapes=[pltpu.VMEM((2,) + packed.shape, BF16)],
        compiler_params=params(16 if len(codes) <= 8 else 48),
        cost_estimate=NO_COST,
        name="adapter_low",
    )(packed, packed_other, after(normed, rows[0]), slot)
    attended = [attend(i, rows[i]) for i in SHARED[0]]
    far_x.append(beside(x[2], rows[0]))
    far_xy.append(beside(xy[1], attended[0]))
    project_shared(1, attended[1])
    attended.append(attend(2, rows[2]))
    rows.extend(project_remote(project_direct_kernel, DIRECT, (x[2], far_x[2]), attended[2]))
    attended.append(attend(CHUNKS - 1, rows[-1]))
    columns = 2 * LANES
    return pl.pallas_call(
        mix_kernel,
        out_shape=jax.ShapeDtypeStruct((tokens, width), BF16),
        in_specs=[VMEM] * (2 + CHUNKS),
        out_specs=HBM,
        scratch_shapes=[
            pltpu.VMEM((width // columns, tokens, columns), BF16),
            pltpu.SemaphoreType.DMA((width // columns,)),
        ],
        compiler_params=params(20),
        name="mix_output",
    )(layer_input_hidden, output_weight, *attended)


def solution(mesh):
    placed = (
        P(("req", "ad"), None),
        P(),
        P(None, "ad"),
        P(),
        P("req", None, None),
        P("req", None, None),
        P(("req", "ad"), None),
        P(("req", "ad"), None),
        P(),
    )
    return jax.shard_map(
        body, mesh=mesh, in_specs=placed, out_specs=P(("req", "ad"), None), check_vma=False
    )
```

```python
import math

import jax
import jax.numpy as jnp
import numpy as np
from jax import lax
from jax.experimental import pallas as pl
from jax.experimental.pallas import tpu as pltpu
from jax.sharding import PartitionSpec as P

HEADS = 16
KV_HEADS = 8
HEAD_DIM = 96
HALF = HEAD_DIM // 2
MAXLEN = 16
PAIR = 28
EPS = 1e-05
ROPE_THETA = 100000.0

GROUP = 4
BLOCK = GROUP * PAIR
LANES = 128
CHUNKS = 4
SHARD_HEADS = 8
CHUNK_ROWS = 2 * HEAD_DIM
SHARED = ((0, 1), (2,))
DIRECT = (3,)
LOG2E = 1.4426950408889634

F32 = jnp.float32
BF16 = jnp.bfloat16
VMEM = pl.BlockSpec(memory_space=pltpu.VMEM)
SMEM = pl.BlockSpec(memory_space=pltpu.SMEM)
HBM = pl.BlockSpec(memory_space=pltpu.HBM)
NO_COST = pl.CostEstimate(flops=0, bytes_accessed=0, transcendentals=0)


def params(mib):
    return pltpu.CompilerParams(vmem_limit_bytes=mib * 1024 * 1024)


def dot_nt(left, right):
    return lax.dot_general(left, right, (((1,), (1,)), ((), ())), preferred_element_type=F32)


def dot_nn(left, right):
    return lax.dot_general(left, right, (((1,), (0,)), ((), ())), preferred_element_type=F32)


def rope_tables():
    inverse = np.exp(-math.log(ROPE_THETA) * 2.0 * np.arange(HALF, dtype=np.float64) / HEAD_DIM)
    angles = inverse[:, None] * np.arange(MAXLEN, dtype=np.float64)[None, :]
    cosine, sine = np.cos(angles), np.sin(angles)
    scale = LOG2E / math.sqrt(HEAD_DIM)
    return np.concatenate([cosine, sine, cosine * scale, sine * scale], axis=0).astype(np.float32)


def group_of(index):
    found = jnp.zeros_like(index)
    for edge in range(1, GROUP + 1):
        found = found + jnp.where(index >= edge * PAIR, 1, 0)
    return found


def turn_kernel(w_ref, own_ref, *rest):
    send_refs, turned = rest[:-1], rest[-1]
    shard = lax.axis_index("ad")
    half = lax.rem(lax.axis_index("req"), 2)
    step = 4 * HEAD_DIM
    for g in range(w_ref.shape[1] // step):
        turned[g * step : (g + 1) * step, :] = w_ref[:, g * step : (g + 1) * step].T
    is_kv = shard >= 2
    for i in range(CHUNKS):
        for p in range(2):
            head = jnp.where(is_kv, i + 4 * p, 2 * i + p)
            own_ref[i, p] = turned[pl.ds(pl.multiple_of(head * HEAD_DIM, HEAD_DIM), HEAD_DIM), :]
    for send_ref, chunks in zip(send_refs, SHARED):
        for n, i in enumerate(chunks):
            send_ref[n] = own_ref[i, half]
    for n, i in enumerate(DIRECT):
        send_refs[-1][n] = own_ref[i]


def pack(n, down_ref, up_ref, out_ref):
    core = lax.rem(lax.axis_index("ad"), 2)
    rank, width = up_ref.shape[1], down_ref.shape[2]
    value_cols = up_ref.shape[2] - width

    @pl.when(core == 0)
    def _():
        out_ref[n] = down_ref[0]

    @pl.when(core == 1)
    def _():
        out_ref[n, :rank, :] = up_ref[0, :, :width]
        out_ref[n, rank:, :value_cols] = up_ref[0, :, width:]
        out_ref[n, rank:, value_cols:] = jnp.zeros((rank, width - value_cols), BF16)


def norm_kernel(
    x_ref, scale_ref, table_ref, len_ref, adapter_ref, holder_ref, normed_ref, rope_ref, bias_ref, slot_ref
):
    gain = scale_ref[...].reshape(1, scale_ref.shape[0])
    lane = lax.broadcasted_iota(jnp.int32, (1, LANES), 1)
    group = group_of(lane)
    within = lane - PAIR * group
    key_row = lax.broadcasted_iota(jnp.int32, (BLOCK, LANES), 0)
    query_col = lax.broadcasted_iota(jnp.int32, (BLOCK, LANES), 1)
    key_group = group_of(key_row)
    key_within = key_row - PAIR * key_group
    query_group = group_of(query_col)
    query_within = query_col - PAIR * query_group
    same_pair = (key_group == query_group) & (key_row <= query_col)
    dead = query_col >= BLOCK
    position_row = lax.broadcasted_iota(jnp.int32, (MAXLEN, LANES), 0)
    for b in range(bias_ref.shape[0]):
        lanes = slice(b * LANES, (b + 1) * LANES)
        first = jnp.zeros((1, LANES), jnp.int32)
        slot_first = jnp.zeros((1, LANES), jnp.int32)
        slot_second = jnp.zeros((1, LANES), jnp.int32)
        for g in range(GROUP):
            r = 2 * (GROUP * b + g)
            first = jnp.where(group == g, len_ref[0, r], first)
            slot_first = jnp.where(group == g, holder_ref[adapter_ref[0, r]], slot_first)
            slot_second = jnp.where(group == g, holder_ref[adapter_ref[0, r + 1]], slot_second)
        position = jnp.where(within < first, within, within - first)
        slot_ref[:, lanes] = jnp.where(within < first, slot_first, slot_second)
        onehot = jnp.where(position_row == position, 1.0, 0.0).astype(F32)
        rope_ref[:, lanes] = jnp.dot(
            table_ref[...], onehot, preferred_element_type=F32, precision=lax.Precision.HIGHEST
        )
        split = (key_within >= first) | (query_within < first)
        bias_ref[b] = jnp.where((same_pair & split) | dead, 0.0, -jnp.inf).astype(F32)
        rows = x_ref[b * BLOCK : (b + 1) * BLOCK, :].astype(F32)
        mean = jnp.mean(rows * rows, axis=-1, keepdims=True)
        normed_ref[b * LANES : b * LANES + BLOCK, :] = (rows * lax.rsqrt(mean + EPS) * gain).astype(BF16)
        normed_ref[b * LANES + BLOCK : (b + 1) * LANES, :] = jnp.zeros((LANES - BLOCK, rows.shape[1]), BF16)


def make_low_kernel(codes, rank):
    def kernel(mine_ref, other_ref, normed_ref, slot_ref, low_ref, up_t_ref, adapter):
        core = lax.rem(lax.axis_index("ad"), 2)
        me = lax.axis_index("req")
        count, rows, width = mine_ref.shape
        adapter[core] = mine_ref[...]
        adapter[1 - core] = other_ref[...]
        low = dot_nt(adapter[0].reshape(count * rows, width), normed_ref[...]).astype(BF16)
        slot = slot_ref[...]
        for j, code in enumerate(codes):
            mine = slot == me ^ code
            for part in range(2):
                r = (2 * j + part) * rank
                low_ref[part, j * rank : (j + 1) * rank, :] = jnp.where(mine, low[r : r + rank, :], jnp.zeros((), BF16))
        for part in range(2):
            stop = min(width, up_t_ref.shape[0] - part * width)
            step = 3 * LANES
            for start in range(0, stop, step):
                piece = adapter[1, :, part * rank : (part + 1) * rank, start : start + step]
                up_t_ref[part * width + start : part * width + start + step, :] = piece.reshape(count * rank, step).T

    return kernel


def project_kernel(w_ref, normed_ref, *out_refs):
    rows = dot_nt(w_ref[...].reshape(CHUNKS * CHUNK_ROWS, w_ref.shape[-1]), normed_ref[...])
    for i, out_ref in enumerate(out_refs):
        out_ref[...] = rows[i * CHUNK_ROWS : (i + 1) * CHUNK_ROWS, :]


def project_own_kernel(w_ref, normed_ref, down_ref, up_ref, down_y_ref, up_y_ref, *out_refs):
    pack(0, down_ref, up_ref, out_refs[-1])
    pack(1, down_y_ref, up_y_ref, out_refs[-1])
    project_kernel(w_ref, normed_ref, *out_refs[:-1])


def project_shared_kernel(near_x, near_xy, far_x, far_xy, normed_ref, *rest):
    out_refs, weight = rest[:-1], rest[-1]
    half = lax.rem(lax.axis_index("req"), 2)
    core = lax.rem(lax.axis_index("ad"), 2)
    for n in range(len(out_refs)):
        weight[n, core, half] = near_x[n]
        weight[n, core, 1 - half] = near_xy[n]
        weight[n, 1 - core, half] = far_x[n]
        weight[n, 1 - core, 1 - half] = far_xy[n]
    project_chunks(weight, normed_ref, out_refs)


def project_direct_kernel(near_x, far_x, normed_ref, *rest):
    out_refs, weight = rest[:-1], rest[-1]
    core = lax.rem(lax.axis_index("ad"), 2)
    for n in range(len(out_refs)):
        weight[n, core] = near_x[n]
        weight[n, 1 - core] = far_x[n]
    project_chunks(weight, normed_ref, out_refs)


def project_chunks(weight, normed_ref, out_refs):
    step = 4 * HEAD_DIM
    rows = dot_nt(weight[...].reshape(len(out_refs) * step, weight.shape[-1]), normed_ref[...])
    for n, out_ref in enumerate(out_refs):
        out_ref[...] = rows[n * step : (n + 1) * step, :].reshape(out_ref.shape)


def put_rotated(target, index, lanes, rows, rope_ref, base):
    cosine = rope_ref[base : base + HALF, lanes]
    sine = rope_ref[base + HALF : base + 2 * HALF, lanes]
    first, second = rows[:HALF, :], rows[HALF:, :]
    target[index + (slice(0, HALF), lanes)] = (first * cosine - second * sine).astype(BF16)
    target[index + (slice(HALF, HEAD_DIM), lanes)] = (second * cosine + first * sine).astype(BF16)


def make_attend_kernel(i):
    def run(query_rows, key_rows, value_rows, rope_ref, low_ref, up_t_ref, bias_ref, out_ref, parts):
        query_up = jnp.concatenate(
            [up_t_ref[start : start + CHUNK_ROWS, :] for start in (i * CHUNK_ROWS, (SHARD_HEADS + 2 * i) * HEAD_DIM)],
            axis=0,
        )
        value_up = jnp.concatenate(
            [up_t_ref[start : start + HEAD_DIM, :] for start in ((HEADS + i) * HEAD_DIM, (HEADS + i + 4) * HEAD_DIM)],
            axis=0,
        )

        def fill(g):
            lanes = slice(2 * g * LANES, 2 * (g + 1) * LANES)
            query_delta = dot_nn(query_up, low_ref[0, :, lanes])
            value_delta = dot_nn(value_up, low_ref[1, :, lanes])
            for p in range(2):
                put_rotated(parts, (2, p), lanes, key_rows(p, lanes), rope_ref, 0)
                for c in range(2):
                    row = (2 * c + p) * HEAD_DIM
                    rows = query_rows(c, p, lanes) + query_delta[row : row + HEAD_DIM, :]
                    put_rotated(parts, (c, p), lanes, rows, rope_ref, 2 * HALF)
                rows = value_rows(p, lanes) + value_delta[p * HEAD_DIM : (p + 1) * HEAD_DIM, :]
                parts[3, p, :, lanes] = rows.astype(BF16)

        def lanes_of(b):
            return slice(b * LANES, (b + 1) * LANES)

        def score(b, p):
            lanes = lanes_of(b)
            key = parts[2, p, :, lanes].T[:BLOCK, :]
            query = jnp.concatenate([parts[p, 0, :, lanes], parts[p, 1, :, lanes]], axis=1)
            return dot_nn(key, query)

        def soften(b, scores):
            bias = bias_ref[b]
            scores = scores + jnp.concatenate([bias, bias], axis=1)
            weights = jnp.exp2(scores - jnp.max(scores, axis=0, keepdims=True))
            probs = (weights * (1.0 / jnp.sum(weights, axis=0, keepdims=True))).astype(BF16)
            return jnp.concatenate([probs, jnp.zeros((LANES - BLOCK, 2 * LANES), BF16)], axis=0)

        def mingle(b, p, probs):
            result = dot_nn(parts[3, p, :, lanes_of(b)], probs).astype(BF16)
            return [result[:, :LANES], result[:, LANES:]]

        blocks = bias_ref.shape[0]
        work = [(b, p) for b in range(blocks) for p in range(2)]
        ahead = 3
        filled = 0
        scores, results = {}, {}
        for n in range(len(work) + ahead + 1):
            if n < len(work):
                while filled < blocks // 2 and 2 * filled <= min(work[n][0] + 2, blocks - 1):
                    fill(filled)
                    filled += 1
                scores[n] = score(*work[n])
            m = n - ahead
            if 0 <= m < len(work):
                scores[m] = soften(work[m][0], scores[m])
            m -= 1
            if 0 <= m < len(work):
                b, p = work[m]
                results[p] = mingle(b, p, scores.pop(m))
                if p == 1:
                    heads = jnp.concatenate(results.pop(0) + results.pop(1), axis=0)
                    out_ref[b * BLOCK : (b + 1) * BLOCK, :] = heads.T[:BLOCK, :]

    def kernel(own_ref, near_ref, remote_ref, rope_ref, low_ref, up_t_ref, bias_ref, out_ref, local, parts):
        shard = lax.axis_index("ad")
        side, core = shard // 2, lax.rem(shard, 2)
        local[core] = own_ref[...].reshape(local.shape[1:])
        local[1 - core] = near_ref[...].reshape(local.shape[1:])
        rest = (rope_ref, low_ref, up_t_ref, bias_ref, out_ref, parts)

        @pl.when(side == 0)
        def _():
            run(
                lambda c, p, lanes: local[c, p, :, lanes],
                lambda p, lanes: remote_ref[0, p, :, lanes],
                lambda p, lanes: remote_ref[1, p, :, lanes],
                *rest,
            )

        @pl.when(side == 1)
        def _():
            run(
                lambda c, p, lanes: remote_ref[c, p, :, lanes],
                lambda p, lanes: local[0, p, :, lanes],
                lambda p, lanes: local[1, p, :, lanes],
                *rest,
            )

    return kernel


def mix_kernel(x_ref, w_ref, *rest):
    parts, out_hbm, ready, sems = rest[:CHUNKS], rest[CHUNKS], rest[CHUNKS + 1], rest[CHUNKS + 2]
    half = SHARD_HEADS * HEAD_DIM
    groups = sems.shape[0]
    rows = ready.shape[0] // groups
    weight = jnp.concatenate(
        [
            w_ref[c * half + i * CHUNK_ROWS : c * half + (i + 1) * CHUNK_ROWS, :]
            for i in range(CHUNKS)
            for c in range(2)
        ],
        axis=0,
    )
    copies = []
    for n in range(groups):
        part = slice(n * rows, (n + 1) * rows)
        attended = jnp.concatenate([part_ref[part, :] for part_ref in parts], axis=1)
        ready[part, :] = (x_ref[part, :].astype(F32) + dot_nn(attended, weight)).astype(BF16)
        copies.append(pltpu.make_async_copy(ready.at[part], out_hbm.at[part], sems.at[n]))
        copies[-1].start()
    for copy in copies:
        copy.wait()


def after(value, *others):
    return lax.optimization_barrier((value,) + others)[0]


def body(
    layer_input_hidden,
    input_norm_scale,
    query_key_value_weight,
    output_weight,
    adapter_down_weight,
    adapter_up_weight,
    prompt_token_length,
    request_adapter_index,
    adapter_holder_index,
):
    tokens, width = layer_input_hidden.shape
    blocks = tokens // BLOCK
    padded = blocks * LANES
    rank = adapter_up_weight.shape[1]
    features = adapter_up_weight.shape[2]
    shard_cols = query_key_value_weight.shape[1]
    shards, requests = lax.axis_size("ad"), lax.axis_size("req")
    other_side = [(a, a ^ 2) for a in range(shards)]
    other_core = [(a, a ^ 1) for a in range(shards)]

    def other_row(bit):
        return [(r, r ^ bit) for r in range(requests)]

    turned = pl.pallas_call(
        turn_kernel,
        out_shape=[jax.ShapeDtypeStruct((CHUNKS, 2, HEAD_DIM, width), BF16)]
        + [jax.ShapeDtypeStruct((len(chunks), HEAD_DIM, width), BF16) for chunks in SHARED]
        + [jax.ShapeDtypeStruct((len(DIRECT), 2, HEAD_DIM, width), BF16)],
        in_specs=[VMEM],
        out_specs=[VMEM] * (2 + len(SHARED)),
        scratch_shapes=[pltpu.VMEM((shard_cols, width), BF16)],
        compiler_params=params(20),
        name="turn_weight",
    )(query_key_value_weight)
    own, sends = turned[0], turned[1:]

    down_y = lax.ppermute(adapter_down_weight, "req", other_row(1))
    up_y = lax.ppermute(adapter_up_weight, "req", other_row(1))
    normed, rope, bias, slot = pl.pallas_call(
        norm_kernel,
        out_shape=[
            jax.ShapeDtypeStruct((padded, width), BF16),
            jax.ShapeDtypeStruct((4 * HALF, padded), F32),
            jax.ShapeDtypeStruct((blocks, BLOCK, LANES), F32),
            jax.ShapeDtypeStruct((1, padded), jnp.int32),
        ],
        in_specs=[VMEM] * 3 + [SMEM] * 3,
        out_specs=[VMEM] * 4,
        compiler_params=params(16),
        cost_estimate=NO_COST,
        name="norm_tokens",
    )(
        layer_input_hidden, input_norm_scale, jnp.asarray(rope_tables()),
        prompt_token_length, request_adapter_index, adapter_holder_index,
    )

    def project(weight, name):
        return pl.pallas_call(
            project_kernel,
            out_shape=[jax.ShapeDtypeStruct((CHUNK_ROWS, padded), F32)] * CHUNKS,
            in_specs=[VMEM] * 2,
            out_specs=[VMEM] * CHUNKS,
            compiler_params=params(24),
            cost_estimate=NO_COST,
            name=name,
        )(weight, normed)

    def project_remote(kernel, chunks, arrays, token):
        return pl.pallas_call(
            kernel,
            out_shape=[jax.ShapeDtypeStruct((2, 2, HEAD_DIM, padded), F32)] * len(chunks),
            in_specs=[VMEM] * (len(arrays) + 1),
            out_specs=[VMEM] * len(chunks),
            scratch_shapes=[pltpu.VMEM((len(chunks), 2, 2, HEAD_DIM, width), BF16)],
            compiler_params=params(20),
            cost_estimate=NO_COST,
            name=f"project_{chunks[0]}",
        )(*arrays, after(normed, token))

    def attend(i, rows):
        return pl.pallas_call(
            make_attend_kernel(i),
            out_shape=jax.ShapeDtypeStruct((tokens, 4 * HEAD_DIM), BF16),
            in_specs=[VMEM] * 7,
            out_specs=VMEM,
            scratch_shapes=[
                pltpu.VMEM((2, 2, HEAD_DIM, padded), F32),
                pltpu.VMEM((4, 2, HEAD_DIM, padded), BF16),
            ],
            compiler_params=params(16 if len(codes) <= 8 else 24),
            cost_estimate=NO_COST,
            name=f"attend_{i}",
        )(own_parts[i], near_parts[i], rows, rope, low, up_t, bias)

    def gather_adapters(packed, codes, bit, before, then):
        got = after(lax.ppermute(after(packed, before), "req", other_row(bit)), then)
        return jnp.concatenate([packed, got], axis=0), codes + [code ^ bit for code in codes]

    def along(piece, token):
        return lax.ppermute(after(piece, token), "req", other_row(1))

    def beside(piece, token):
        return lax.ppermute(after(piece, token), "ad", other_core)

    x = [lax.ppermute(send, "ad", other_side) for send in sends]
    near = beside(own, own)
    xy, far_x, far_xy, rows, attended = [], [], [], [], []

    def project_shared(i, *tokens):
        arrays = (x[i], xy[i], far_x[i], far_xy[i])
        rows.extend(project_remote(project_shared_kernel, SHARED[i], arrays, *tokens))

    bits = []
    while 2 ** len(bits) < requests:
        bits.append(2 ** len(bits))
    bits = bits[:0:-1]
    codes = [0, 1]
    *own_parts, packed = pl.pallas_call(
        project_own_kernel,
        out_shape=[jax.ShapeDtypeStruct((CHUNK_ROWS, padded), F32)] * CHUNKS
        + [jax.ShapeDtypeStruct((2, 2 * rank, width), BF16)],
        in_specs=[VMEM] * 6,
        out_specs=[VMEM] * (CHUNKS + 1),
        compiler_params=params(24),
        cost_estimate=NO_COST,
        name="project_own",
    )(after(own, normed), normed, adapter_down_weight, adapter_up_weight, down_y, up_y)
    xy.append(along(x[0], normed))
    far_x.append(beside(x[0], own_parts[0]))
    near_parts = project(after(near, x[0]), "project_near")
    for bit in bits[:1]:
        packed, codes = gather_adapters(packed, codes, bit, normed, near_parts[0])
    xy.append(along(x[1], near_parts[0]))
    far_x.append(beside(x[1], own_parts[0]))
    far_xy.append(beside(xy[0], x[1]))
    for bit in bits[1:]:
        packed, codes = gather_adapters(packed, codes, bit, own_parts[0], own_parts[0])
    packed_other = beside(packed, own_parts[0])
    project_shared(0, near_parts[0])
    low, up_t = pl.pallas_call(
        make_low_kernel(codes, rank),
        out_shape=[
            jax.ShapeDtypeStruct((2, len(codes) * rank, padded), BF16),
            jax.ShapeDtypeStruct((features, len(codes) * rank), BF16),
        ],
        in_specs=[VMEM] * 4,
        out_specs=[VMEM] * 2,
        scratch_shapes=[pltpu.VMEM((2,) + packed.shape, BF16)],
        compiler_params=params(16 if len(codes) <= 8 else 48),
        cost_estimate=NO_COST,
        name="adapter_low",
    )(packed, packed_other, after(normed, rows[0]), slot)
    attended = [attend(i, rows[i]) for i in SHARED[0]]
    far_x.append(beside(x[2], rows[0]))
    far_xy.append(beside(xy[1], attended[0]))
    project_shared(1, attended[1])
    attended.append(attend(2, rows[2]))
    rows.extend(project_remote(project_direct_kernel, DIRECT, (x[2], far_x[2]), attended[2]))
    attended.append(attend(CHUNKS - 1, rows[-1]))
    return pl.pallas_call(
        mix_kernel,
        out_shape=jax.ShapeDtypeStruct((tokens, width), BF16),
        in_specs=[VMEM] * (2 + CHUNKS),
        out_specs=HBM,
        scratch_shapes=[
            pltpu.VMEM((tokens, width), BF16),
            pltpu.SemaphoreType.DMA((tokens // (2 * BLOCK),)),
        ],
        compiler_params=params(20),
        name="mix_output",
    )(layer_input_hidden, output_weight, *attended)


def solution(mesh):
    placed = (
        P(("req", "ad"), None),
        P(),
        P(None, "ad"),
        P(),
        P("req", None, None),
        P("req", None, None),
        P(("req", "ad"), None),
        P(("req", "ad"), None),
        P(),
    )
    return jax.shard_map(
        body, mesh=mesh, in_specs=placed, out_specs=P(("req", "ad"), None), check_vma=False
    )
```

```python
import math

import jax
import jax.numpy as jnp
import numpy as np
from jax import lax
from jax.experimental import pallas as pl
from jax.experimental.pallas import tpu as pltpu
from jax.sharding import PartitionSpec as P

HEADS = 16
KV_HEADS = 8
HEAD_DIM = 96
HALF = HEAD_DIM // 2
MAXLEN = 16
PAIR = 28
EPS = 1e-05
ROPE_THETA = 100000.0

GROUP = 4
BLOCK = GROUP * PAIR
LANES = 128
CHUNKS = 4
SHARD_HEADS = 8
CHUNK_ROWS = 2 * HEAD_DIM
SHARED = ((0, 1), (2,))
DIRECT = (3,)
LOG2E = 1.4426950408889634

F32 = jnp.float32
BF16 = jnp.bfloat16
VMEM = pl.BlockSpec(memory_space=pltpu.VMEM)
SMEM = pl.BlockSpec(memory_space=pltpu.SMEM)
HBM = pl.BlockSpec(memory_space=pltpu.HBM)
NO_COST = pl.CostEstimate(flops=0, bytes_accessed=0, transcendentals=0)


def params(mib):
    return pltpu.CompilerParams(vmem_limit_bytes=mib * 1024 * 1024)


def dot_nt(left, right):
    return lax.dot_general(left, right, (((1,), (1,)), ((), ())), preferred_element_type=F32)


def dot_nn(left, right):
    return lax.dot_general(left, right, (((1,), (0,)), ((), ())), preferred_element_type=F32)


def rope_tables():
    inverse = np.exp(-math.log(ROPE_THETA) * 2.0 * np.arange(HALF, dtype=np.float64) / HEAD_DIM)
    angles = inverse[:, None] * np.arange(MAXLEN, dtype=np.float64)[None, :]
    cosine, sine = np.cos(angles), np.sin(angles)
    scale = LOG2E / math.sqrt(HEAD_DIM)
    return np.concatenate([cosine, sine, cosine * scale, sine * scale], axis=0).astype(np.float32)


def group_of(index):
    found = jnp.zeros_like(index)
    for edge in range(1, GROUP + 1):
        found = found + jnp.where(index >= edge * PAIR, 1, 0)
    return found


def turn_kernel(w_ref, own_ref, *rest):
    send_refs, turned = rest[:-1], rest[-1]
    shard = lax.axis_index("ad")
    half = lax.rem(lax.axis_index("req"), 2)
    step = 4 * HEAD_DIM
    for g in range(w_ref.shape[1] // step):
        turned[g * step : (g + 1) * step, :] = w_ref[:, g * step : (g + 1) * step].T
    is_kv = shard >= 2
    for i in range(CHUNKS):
        for p in range(2):
            head = jnp.where(is_kv, i + 4 * p, 2 * i + p)
            own_ref[i, p] = turned[pl.ds(pl.multiple_of(head * HEAD_DIM, HEAD_DIM), HEAD_DIM), :]
    for send_ref, chunks in zip(send_refs, SHARED):
        for n, i in enumerate(chunks):
            send_ref[n] = own_ref[i, half]
    for n, i in enumerate(DIRECT):
        send_refs[-1][n] = own_ref[i]


def pack(n, down_ref, up_ref, out_ref):
    core = lax.rem(lax.axis_index("ad"), 2)
    rank, width = up_ref.shape[1], down_ref.shape[2]
    value_cols = up_ref.shape[2] - width

    @pl.when(core == 0)
    def _():
        out_ref[n] = down_ref[0]

    @pl.when(core == 1)
    def _():
        out_ref[n, :rank, :] = up_ref[0, :, :width]
        out_ref[n, rank:, :value_cols] = up_ref[0, :, width:]
        out_ref[n, rank:, value_cols:] = jnp.zeros((rank, width - value_cols), BF16)


def norm_kernel(
    x_ref, scale_ref, table_ref, len_ref, adapter_ref, holder_ref, normed_ref, rope_ref, bias_ref, slot_ref
):
    gain = scale_ref[...].reshape(1, scale_ref.shape[0])
    lane = lax.broadcasted_iota(jnp.int32, (1, LANES), 1)
    group = group_of(lane)
    within = lane - PAIR * group
    key_row = lax.broadcasted_iota(jnp.int32, (BLOCK, LANES), 0)
    query_col = lax.broadcasted_iota(jnp.int32, (BLOCK, LANES), 1)
    key_group = group_of(key_row)
    key_within = key_row - PAIR * key_group
    query_group = group_of(query_col)
    query_within = query_col - PAIR * query_group
    same_pair = (key_group == query_group) & (key_row <= query_col)
    dead = query_col >= BLOCK
    position_row = lax.broadcasted_iota(jnp.int32, (MAXLEN, LANES), 0)
    for b in range(bias_ref.shape[0]):
        lanes = slice(b * LANES, (b + 1) * LANES)
        first = jnp.zeros((1, LANES), jnp.int32)
        slot_first = jnp.zeros((1, LANES), jnp.int32)
        slot_second = jnp.zeros((1, LANES), jnp.int32)
        for g in range(GROUP):
            r = 2 * (GROUP * b + g)
            first = jnp.where(group == g, len_ref[0, r], first)
            slot_first = jnp.where(group == g, holder_ref[adapter_ref[0, r]], slot_first)
            slot_second = jnp.where(group == g, holder_ref[adapter_ref[0, r + 1]], slot_second)
        position = jnp.where(within < first, within, within - first)
        slot_ref[:, lanes] = jnp.where(within < first, slot_first, slot_second)
        onehot = jnp.where(position_row == position, 1.0, 0.0).astype(F32)
        rope_ref[:, lanes] = jnp.dot(
            table_ref[...], onehot, preferred_element_type=F32, precision=lax.Precision.HIGHEST
        )
        split = (key_within >= first) | (query_within < first)
        bias_ref[b] = jnp.where((same_pair & split) | dead, 0.0, -jnp.inf).astype(F32)
        rows = x_ref[b * BLOCK : (b + 1) * BLOCK, :].astype(F32)
        mean = jnp.mean(rows * rows, axis=-1, keepdims=True)
        normed_ref[b * LANES : b * LANES + BLOCK, :] = (rows * lax.rsqrt(mean + EPS) * gain).astype(BF16)
        normed_ref[b * LANES + BLOCK : (b + 1) * LANES, :] = jnp.zeros((LANES - BLOCK, rows.shape[1]), BF16)


def make_low_kernel(codes, rank):
    def kernel(mine_ref, other_ref, normed_ref, slot_ref, low_ref, up_t_ref, adapter):
        core = lax.rem(lax.axis_index("ad"), 2)
        me = lax.axis_index("req")
        count, rows, width = mine_ref.shape
        adapter[core] = mine_ref[...]
        adapter[1 - core] = other_ref[...]
        low = dot_nt(adapter[0].reshape(count * rows, width), normed_ref[...]).astype(BF16)
        slot = slot_ref[...]
        for j, code in enumerate(codes):
            mine = slot == me ^ code
            for part in range(2):
                r = (2 * j + part) * rank
                low_ref[part, j * rank : (j + 1) * rank, :] = jnp.where(mine, low[r : r + rank, :], jnp.zeros((), BF16))
        for part in range(2):
            stop = min(width, up_t_ref.shape[0] - part * width)
            step = 3 * LANES
            for start in range(0, stop, step):
                piece = adapter[1, :, part * rank : (part + 1) * rank, start : start + step]
                up_t_ref[part * width + start : part * width + start + step, :] = piece.reshape(count * rank, step).T

    return kernel


def project_kernel(w_ref, normed_ref, *out_refs):
    rows = dot_nt(w_ref[...].reshape(CHUNKS * CHUNK_ROWS, w_ref.shape[-1]), normed_ref[...])
    for i, out_ref in enumerate(out_refs):
        out_ref[...] = rows[i * CHUNK_ROWS : (i + 1) * CHUNK_ROWS, :]


def project_own_kernel(w_ref, normed_ref, down_ref, up_ref, down_y_ref, up_y_ref, *out_refs):
    pack(0, down_ref, up_ref, out_refs[-1])
    pack(1, down_y_ref, up_y_ref, out_refs[-1])
    project_kernel(w_ref, normed_ref, *out_refs[:-1])


def project_shared_kernel(near_x, near_xy, far_x, far_xy, normed_ref, *rest):
    out_refs, weight = rest[:-1], rest[-1]
    half = lax.rem(lax.axis_index("req"), 2)
    core = lax.rem(lax.axis_index("ad"), 2)
    for n in range(len(out_refs)):
        weight[n, core, half] = near_x[n]
        weight[n, core, 1 - half] = near_xy[n]
        weight[n, 1 - core, half] = far_x[n]
        weight[n, 1 - core, 1 - half] = far_xy[n]
    project_chunks(weight, normed_ref, out_refs)


def project_chunks(weight, normed_ref, out_refs):
    step = 4 * HEAD_DIM
    rows = dot_nt(weight[...].reshape(len(out_refs) * step, weight.shape[-1]), normed_ref[...])
    for n, out_ref in enumerate(out_refs):
        out_ref[...] = rows[n * step : (n + 1) * step, :].reshape(out_ref.shape)


def put_rotated(target, index, lanes, rows, rope_ref, base):
    cosine = rope_ref[base : base + HALF, lanes]
    sine = rope_ref[base + HALF : base + 2 * HALF, lanes]
    first, second = rows[:HALF, :], rows[HALF:, :]
    target[index + (slice(0, HALF), lanes)] = (first * cosine - second * sine).astype(BF16)
    target[index + (slice(HALF, HEAD_DIM), lanes)] = (second * cosine + first * sine).astype(BF16)


def make_attend_kernel(i):
    def run(prepare, query_rows, key_rows, value_rows, rope_ref, low_ref, up_t_ref, bias_ref, out_ref, parts):
        query_up = jnp.concatenate(
            [up_t_ref[start : start + CHUNK_ROWS, :] for start in (i * CHUNK_ROWS, (SHARD_HEADS + 2 * i) * HEAD_DIM)],
            axis=0,
        )
        value_up = jnp.concatenate(
            [up_t_ref[start : start + HEAD_DIM, :] for start in ((HEADS + i) * HEAD_DIM, (HEADS + i + 4) * HEAD_DIM)],
            axis=0,
        )

        def fill(g):
            lanes = slice(2 * g * LANES, 2 * (g + 1) * LANES)
            prepare(lanes)
            query_delta = dot_nn(query_up, low_ref[0, :, lanes])
            value_delta = dot_nn(value_up, low_ref[1, :, lanes])
            for p in range(2):
                put_rotated(parts, (2, p), lanes, key_rows(p, lanes), rope_ref, 0)
                for c in range(2):
                    row = (2 * c + p) * HEAD_DIM
                    rows = query_rows(c, p, lanes) + query_delta[row : row + HEAD_DIM, :]
                    put_rotated(parts, (c, p), lanes, rows, rope_ref, 2 * HALF)
                rows = value_rows(p, lanes) + value_delta[p * HEAD_DIM : (p + 1) * HEAD_DIM, :]
                parts[3, p, :, lanes] = rows.astype(BF16)

        def lanes_of(b):
            return slice(b * LANES, (b + 1) * LANES)

        def score(b, p):
            lanes = lanes_of(b)
            key = parts[2, p, :, lanes].T[:BLOCK, :]
            query = jnp.concatenate([parts[p, 0, :, lanes], parts[p, 1, :, lanes]], axis=1)
            return dot_nn(key, query)

        def soften(b, scores):
            bias = bias_ref[b]
            scores = scores + jnp.concatenate([bias, bias], axis=1)
            weights = jnp.exp2(scores - jnp.max(scores, axis=0, keepdims=True))
            probs = (weights * (1.0 / jnp.sum(weights, axis=0, keepdims=True))).astype(BF16)
            return jnp.concatenate([probs, jnp.zeros((LANES - BLOCK, 2 * LANES), BF16)], axis=0)

        def mingle(b, p, probs):
            result = dot_nn(parts[3, p, :, lanes_of(b)], probs).astype(BF16)
            return [result[:, :LANES], result[:, LANES:]]

        blocks = bias_ref.shape[0]
        work = [(b, p) for b in range(blocks) for p in range(2)]
        ahead = 3
        filled = 0
        scores, results = {}, {}
        for n in range(len(work) + ahead + 1):
            if n < len(work):
                while filled < blocks // 2 and 2 * filled <= min(work[n][0] + 2, blocks - 1):
                    fill(filled)
                    filled += 1
                scores[n] = score(*work[n])
            m = n - ahead
            if 0 <= m < len(work):
                scores[m] = soften(work[m][0], scores[m])
            m -= 1
            if 0 <= m < len(work):
                b, p = work[m]
                results[p] = mingle(b, p, scores.pop(m))
                if p == 1:
                    heads = jnp.concatenate(results.pop(0) + results.pop(1), axis=0)
                    out_ref[b * BLOCK : (b + 1) * BLOCK, :] = heads.T[:BLOCK, :]

    def attend(local, remote, prepare, own_ref, near_ref, *rest):
        shard = lax.axis_index("ad")
        side, core = shard // 2, lax.rem(shard, 2)
        local[core] = own_ref[...].reshape(local.shape[1:])
        local[1 - core] = near_ref[...].reshape(local.shape[1:])

        def held(c, p, lanes):
            return local[c, p, :, lanes]

        @pl.when(side == 0)
        def _():
            run(prepare, held, lambda p, lanes: remote(0, p, lanes), lambda p, lanes: remote(1, p, lanes), *rest)

        @pl.when(side == 1)
        def _():
            run(prepare, remote, lambda p, lanes: held(0, p, lanes), lambda p, lanes: held(1, p, lanes), *rest)

    def kernel(own_ref, near_ref, remote_ref, rope_ref, low_ref, up_t_ref, bias_ref, out_ref, local, parts):
        attend(
            local, lambda c, p, lanes: remote_ref[c, p, :, lanes], lambda lanes: None,
            own_ref, near_ref, rope_ref, low_ref, up_t_ref, bias_ref, out_ref, parts,
        )

    def project_kernel_of(pieces, normed_ref, own_ref, near_ref, rope_ref, low_ref, up_t_ref, bias_ref, out_ref, *scratch):
        local, parts, weight = scratch
        half = lax.rem(lax.axis_index("req"), 2)
        core = lax.rem(lax.axis_index("ad"), 2)
        if len(pieces) == 4:
            near_x, near_xy, far_x, far_xy = pieces
            weight[core, half] = near_x[0]
            weight[core, 1 - half] = near_xy[0]
            weight[1 - core, half] = far_x[0]
            weight[1 - core, 1 - half] = far_xy[0]
        else:
            near_x, far_x = pieces
            weight[core] = near_x[0]
            weight[1 - core] = far_x[0]
        made = {}

        def prepare(lanes):
            rows = weight[...].reshape(4 * HEAD_DIM, weight.shape[-1])
            made[lanes.start] = dot_nt(rows, normed_ref[lanes, :])

        def remote(c, p, lanes):
            row = (2 * c + p) * HEAD_DIM
            return made[lanes.start][row : row + HEAD_DIM, :]

        attend(local, remote, prepare, own_ref, near_ref, rope_ref, low_ref, up_t_ref, bias_ref, out_ref, parts)

    def shared_kernel(a, b, c, d, *rest):
        project_kernel_of((a, b, c, d), *rest)

    def direct_kernel(a, b, *rest):
        project_kernel_of((a, b), *rest)

    return kernel, shared_kernel, direct_kernel


def mix_kernel(x_ref, w_ref, *rest):
    parts, out_hbm, ready, sems = rest[:CHUNKS], rest[CHUNKS], rest[CHUNKS + 1], rest[CHUNKS + 2]
    half = SHARD_HEADS * HEAD_DIM
    groups = sems.shape[0]
    rows = ready.shape[0] // groups
    weight = jnp.concatenate(
        [
            w_ref[c * half + i * CHUNK_ROWS : c * half + (i + 1) * CHUNK_ROWS, :]
            for i in range(CHUNKS)
            for c in range(2)
        ],
        axis=0,
    )
    copies = []
    for n in range(groups):
        part = slice(n * rows, (n + 1) * rows)
        attended = jnp.concatenate([part_ref[part, :] for part_ref in parts], axis=1)
        ready[part, :] = (x_ref[part, :].astype(F32) + dot_nn(attended, weight)).astype(BF16)
        copies.append(pltpu.make_async_copy(ready.at[part], out_hbm.at[part], sems.at[n]))
        copies[-1].start()
    for copy in copies:
        copy.wait()


def after(value, *others):
    return lax.optimization_barrier((value,) + others)[0]


def body(
    layer_input_hidden,
    input_norm_scale,
    query_key_value_weight,
    output_weight,
    adapter_down_weight,
    adapter_up_weight,
    prompt_token_length,
    request_adapter_index,
    adapter_holder_index,
):
    tokens, width = layer_input_hidden.shape
    blocks = tokens // BLOCK
    padded = blocks * LANES
    rank = adapter_up_weight.shape[1]
    features = adapter_up_weight.shape[2]
    shard_cols = query_key_value_weight.shape[1]
    shards, requests = lax.axis_size("ad"), lax.axis_size("req")
    other_side = [(a, a ^ 2) for a in range(shards)]
    other_core = [(a, a ^ 1) for a in range(shards)]

    def other_row(bit):
        return [(r, r ^ bit) for r in range(requests)]

    turned = pl.pallas_call(
        turn_kernel,
        out_shape=[jax.ShapeDtypeStruct((CHUNKS, 2, HEAD_DIM, width), BF16)]
        + [jax.ShapeDtypeStruct((len(chunks), HEAD_DIM, width), BF16) for chunks in SHARED]
        + [jax.ShapeDtypeStruct((len(DIRECT), 2, HEAD_DIM, width), BF16)],
        in_specs=[VMEM],
        out_specs=[VMEM] * (2 + len(SHARED)),
        scratch_shapes=[pltpu.VMEM((shard_cols, width), BF16)],
        compiler_params=params(20),
        name="turn_weight",
    )(query_key_value_weight)
    own, sends = turned[0], turned[1:]

    down_y = lax.ppermute(adapter_down_weight, "req", other_row(1))
    up_y = lax.ppermute(adapter_up_weight, "req", other_row(1))
    normed, rope, bias, slot = pl.pallas_call(
        norm_kernel,
        out_shape=[
            jax.ShapeDtypeStruct((padded, width), BF16),
            jax.ShapeDtypeStruct((4 * HALF, padded), F32),
            jax.ShapeDtypeStruct((blocks, BLOCK, LANES), F32),
            jax.ShapeDtypeStruct((1, padded), jnp.int32),
        ],
        in_specs=[VMEM] * 3 + [SMEM] * 3,
        out_specs=[VMEM] * 4,
        compiler_params=params(16),
        cost_estimate=NO_COST,
        name="norm_tokens",
    )(
        layer_input_hidden, input_norm_scale, jnp.asarray(rope_tables()),
        prompt_token_length, request_adapter_index, adapter_holder_index,
    )

    def project(weight, name):
        return pl.pallas_call(
            project_kernel,
            out_shape=[jax.ShapeDtypeStruct((CHUNK_ROWS, padded), F32)] * CHUNKS,
            in_specs=[VMEM] * 2,
            out_specs=[VMEM] * CHUNKS,
            compiler_params=params(24),
            cost_estimate=NO_COST,
            name=name,
        )(weight, normed)

    def project_remote(kernel, chunks, arrays, token):
        return pl.pallas_call(
            kernel,
            out_shape=[jax.ShapeDtypeStruct((2, 2, HEAD_DIM, padded), F32)] * len(chunks),
            in_specs=[VMEM] * (len(arrays) + 1),
            out_specs=[VMEM] * len(chunks),
            scratch_shapes=[pltpu.VMEM((len(chunks), 2, 2, HEAD_DIM, width), BF16)],
            compiler_params=params(20),
            cost_estimate=NO_COST,
            name=f"project_{chunks[0]}",
        )(*arrays, after(normed, token))

    def attend(i, rows):
        return pl.pallas_call(
            make_attend_kernel(i)[0],
            out_shape=jax.ShapeDtypeStruct((tokens, 4 * HEAD_DIM), BF16),
            in_specs=[VMEM] * 7,
            out_specs=VMEM,
            scratch_shapes=[
                pltpu.VMEM((2, 2, HEAD_DIM, padded), F32),
                pltpu.VMEM((4, 2, HEAD_DIM, padded), BF16),
            ],
            compiler_params=params(16 if len(codes) <= 8 else 24),
            cost_estimate=NO_COST,
            name=f"attend_{i}",
        )(own_parts[i], near_parts[i], rows, rope, low, up_t, bias)

    def project_and_attend(i, arrays, token):
        return pl.pallas_call(
            make_attend_kernel(i)[1 if len(arrays) == 4 else 2],
            out_shape=jax.ShapeDtypeStruct((tokens, 4 * HEAD_DIM), BF16),
            in_specs=[VMEM] * (len(arrays) + 7),
            out_specs=VMEM,
            scratch_shapes=[
                pltpu.VMEM((2, 2, HEAD_DIM, padded), F32),
                pltpu.VMEM((4, 2, HEAD_DIM, padded), BF16),
                pltpu.VMEM((2, 2, HEAD_DIM, width), BF16),
            ],
            compiler_params=params(20 if len(codes) <= 8 else 28),
            cost_estimate=NO_COST,
            name=f"project_attend_{i}",
        )(*arrays, after(normed, token), own_parts[i], near_parts[i], rope, low, up_t, bias)

    def gather_adapters(packed, codes, bit, before, then):
        got = after(lax.ppermute(after(packed, before), "req", other_row(bit)), then)
        return jnp.concatenate([packed, got], axis=0), codes + [code ^ bit for code in codes]

    def along(piece, token):
        return lax.ppermute(after(piece, token), "req", other_row(1))

    def beside(piece, token):
        return lax.ppermute(after(piece, token), "ad", other_core)

    x = [lax.ppermute(send, "ad", other_side) for send in sends]
    near = beside(own, own)
    xy, far_x, far_xy, rows, attended = [], [], [], [], []

    def project_shared(i, *tokens):
        arrays = (x[i], xy[i], far_x[i], far_xy[i])
        rows.extend(project_remote(project_shared_kernel, SHARED[i], arrays, *tokens))

    bits = []
    while 2 ** len(bits) < requests:
        bits.append(2 ** len(bits))
    bits = bits[:0:-1]
    codes = [0, 1]
    *own_parts, packed = pl.pallas_call(
        project_own_kernel,
        out_shape=[jax.ShapeDtypeStruct((CHUNK_ROWS, padded), F32)] * CHUNKS
        + [jax.ShapeDtypeStruct((2, 2 * rank, width), BF16)],
        in_specs=[VMEM] * 6,
        out_specs=[VMEM] * (CHUNKS + 1),
        compiler_params=params(24),
        cost_estimate=NO_COST,
        name="project_own",
    )(after(own, normed), normed, adapter_down_weight, adapter_up_weight, down_y, up_y)
    xy.append(along(x[0], normed))
    far_x.append(beside(x[0], own_parts[0]))
    near_parts = project(after(near, x[0]), "project_near")
    for bit in bits[:1]:
        packed, codes = gather_adapters(packed, codes, bit, normed, near_parts[0])
    xy.append(along(x[1], near_parts[0]))
    far_x.append(beside(x[1], own_parts[0]))
    far_xy.append(beside(xy[0], x[1]))
    for bit in bits[1:]:
        packed, codes = gather_adapters(packed, codes, bit, own_parts[0], own_parts[0])
    packed_other = beside(packed, own_parts[0])
    project_shared(0, near_parts[0])
    low, up_t = pl.pallas_call(
        make_low_kernel(codes, rank),
        out_shape=[
            jax.ShapeDtypeStruct((2, len(codes) * rank, padded), BF16),
            jax.ShapeDtypeStruct((features, len(codes) * rank), BF16),
        ],
        in_specs=[VMEM] * 4,
        out_specs=[VMEM] * 2,
        scratch_shapes=[pltpu.VMEM((2,) + packed.shape, BF16)],
        compiler_params=params(16 if len(codes) <= 8 else 48),
        cost_estimate=NO_COST,
        name="adapter_low",
    )(packed, packed_other, after(normed, rows[0]), slot)
    attended = [attend(i, rows[i]) for i in SHARED[0]]
    far_x.append(beside(x[2], rows[0]))
    far_xy.append(beside(xy[1], attended[0]))
    attended.append(project_and_attend(2, (x[1], xy[1], far_x[1], far_xy[1]), attended[1]))
    attended.append(project_and_attend(3, (x[2], far_x[2]), attended[2]))
    return pl.pallas_call(
        mix_kernel,
        out_shape=jax.ShapeDtypeStruct((tokens, width), BF16),
        in_specs=[VMEM] * (2 + CHUNKS),
        out_specs=HBM,
        scratch_shapes=[
            pltpu.VMEM((tokens, width), BF16),
            pltpu.SemaphoreType.DMA((tokens // (2 * BLOCK),)),
        ],
        compiler_params=params(20),
        name="mix_output",
    )(layer_input_hidden, output_weight, *attended)


def solution(mesh):
    placed = (
        P(("req", "ad"), None),
        P(),
        P(None, "ad"),
        P(),
        P("req", None, None),
        P("req", None, None),
        P(("req", "ad"), None),
        P(("req", "ad"), None),
        P(),
    )
    return jax.shard_map(
        body, mesh=mesh, in_specs=placed, out_specs=P(("req", "ad"), None), check_vma=False
    )
```

```python
import math

import jax
import jax.numpy as jnp
import numpy as np
from jax import lax
from jax.experimental import pallas as pl
from jax.experimental.pallas import tpu as pltpu
from jax.sharding import PartitionSpec as P

HEADS = 16
KV_HEADS = 8
HEAD_DIM = 96
HALF = HEAD_DIM // 2
MAXLEN = 16
PAIR = 28
EPS = 1e-05
ROPE_THETA = 100000.0

GROUP = 4
BLOCK = GROUP * PAIR
LANES = 128
CHUNKS = 4
SHARD_HEADS = 8
CHUNK_ROWS = 2 * HEAD_DIM
SHARED = ((0, 1), (2,))
DIRECT = (3,)
LOG2E = 1.4426950408889634

F32 = jnp.float32
BF16 = jnp.bfloat16
VMEM = pl.BlockSpec(memory_space=pltpu.VMEM)
SMEM = pl.BlockSpec(memory_space=pltpu.SMEM)
HBM = pl.BlockSpec(memory_space=pltpu.HBM)
NO_COST = pl.CostEstimate(flops=0, bytes_accessed=0, transcendentals=0)


def params(mib):
    return pltpu.CompilerParams(vmem_limit_bytes=mib * 1024 * 1024)


def dot_nt(left, right):
    return lax.dot_general(left, right, (((1,), (1,)), ((), ())), preferred_element_type=F32)


def dot_nn(left, right):
    return lax.dot_general(left, right, (((1,), (0,)), ((), ())), preferred_element_type=F32)


def rope_tables():
    inverse = np.exp(-math.log(ROPE_THETA) * 2.0 * np.arange(HALF, dtype=np.float64) / HEAD_DIM)
    angles = inverse[:, None] * np.arange(MAXLEN, dtype=np.float64)[None, :]
    cosine, sine = np.cos(angles), np.sin(angles)
    scale = LOG2E / math.sqrt(HEAD_DIM)
    return np.concatenate([cosine, sine, cosine * scale, sine * scale], axis=0).astype(np.float32)


def group_of(index):
    found = jnp.zeros_like(index)
    for edge in range(1, GROUP + 1):
        found = found + jnp.where(index >= edge * PAIR, 1, 0)
    return found


def turn_kernel(w_ref, own_ref, *rest):
    send_refs, turned = rest[:-1], rest[-1]
    shard = lax.axis_index("ad")
    half = lax.rem(lax.axis_index("req"), 2)
    step = 4 * HEAD_DIM
    for g in range(w_ref.shape[1] // step):
        turned[g * step : (g + 1) * step, :] = w_ref[:, g * step : (g + 1) * step].T
    is_kv = shard >= 2
    for i in range(CHUNKS):
        for p in range(2):
            head = jnp.where(is_kv, i + 4 * p, 2 * i + p)
            own_ref[i, p] = turned[pl.ds(pl.multiple_of(head * HEAD_DIM, HEAD_DIM), HEAD_DIM), :]
    for send_ref, chunks in zip(send_refs, SHARED):
        for n, i in enumerate(chunks):
            send_ref[n] = own_ref[i, half]
    for n, i in enumerate(DIRECT):
        send_refs[-1][n] = own_ref[i]


def pack(n, down_ref, up_ref, out_ref):
    core = lax.rem(lax.axis_index("ad"), 2)
    rank, width = up_ref.shape[1], down_ref.shape[2]
    value_cols = up_ref.shape[2] - width

    @pl.when(core == 0)
    def _():
        out_ref[n] = down_ref[0]

    @pl.when(core == 1)
    def _():
        out_ref[n, :rank, :] = up_ref[0, :, :width]
        out_ref[n, rank:, :value_cols] = up_ref[0, :, width:]
        out_ref[n, rank:, value_cols:] = jnp.zeros((rank, width - value_cols), BF16)


def norm_kernel(
    x_ref, scale_ref, table_ref, len_ref, adapter_ref, holder_ref, normed_ref, rope_ref, bias_ref, slot_ref
):
    gain = scale_ref[...].reshape(1, scale_ref.shape[0])
    lane = lax.broadcasted_iota(jnp.int32, (1, LANES), 1)
    group = group_of(lane)
    within = lane - PAIR * group
    key_row = lax.broadcasted_iota(jnp.int32, (BLOCK, LANES), 0)
    query_col = lax.broadcasted_iota(jnp.int32, (BLOCK, LANES), 1)
    key_group = group_of(key_row)
    key_within = key_row - PAIR * key_group
    query_group = group_of(query_col)
    query_within = query_col - PAIR * query_group
    same_pair = (key_group == query_group) & (key_row <= query_col)
    dead = query_col >= BLOCK
    position_row = lax.broadcasted_iota(jnp.int32, (MAXLEN, LANES), 0)
    for b in range(bias_ref.shape[0]):
        lanes = slice(b * LANES, (b + 1) * LANES)
        first = jnp.zeros((1, LANES), jnp.int32)
        slot_first = jnp.zeros((1, LANES), jnp.int32)
        slot_second = jnp.zeros((1, LANES), jnp.int32)
        for g in range(GROUP):
            r = 2 * (GROUP * b + g)
            first = jnp.where(group == g, len_ref[0, r], first)
            slot_first = jnp.where(group == g, holder_ref[adapter_ref[0, r]], slot_first)
            slot_second = jnp.where(group == g, holder_ref[adapter_ref[0, r + 1]], slot_second)
        position = jnp.where(within < first, within, within - first)
        slot_ref[:, lanes] = jnp.where(within < first, slot_first, slot_second)
        onehot = jnp.where(position_row == position, 1.0, 0.0).astype(F32)
        rope_ref[:, lanes] = jnp.dot(
            table_ref[...], onehot, preferred_element_type=F32, precision=lax.Precision.HIGHEST
        )
        split = (key_within >= first) | (query_within < first)
        bias_ref[b] = jnp.where((same_pair & split) | dead, 0.0, -jnp.inf).astype(F32)
        rows = x_ref[b * BLOCK : (b + 1) * BLOCK, :].astype(F32)
        mean = jnp.mean(rows * rows, axis=-1, keepdims=True)
        normed_ref[b * LANES : b * LANES + BLOCK, :] = (rows * lax.rsqrt(mean + EPS) * gain).astype(BF16)
        normed_ref[b * LANES + BLOCK : (b + 1) * LANES, :] = jnp.zeros((LANES - BLOCK, rows.shape[1]), BF16)


def make_low_kernel(codes, rank):
    def kernel(mine_ref, other_ref, normed_ref, slot_ref, low_ref, up_t_ref, adapter):
        core = lax.rem(lax.axis_index("ad"), 2)
        me = lax.axis_index("req")
        count, rows, width = mine_ref.shape
        adapter[core] = mine_ref[...]
        adapter[1 - core] = other_ref[...]
        low = dot_nt(adapter[0].reshape(count * rows, width), normed_ref[...]).astype(BF16)
        slot = slot_ref[...]
        for j, code in enumerate(codes):
            mine = slot == me ^ code
            for part in range(2):
                r = (2 * j + part) * rank
                low_ref[part, j * rank : (j + 1) * rank, :] = jnp.where(mine, low[r : r + rank, :], jnp.zeros((), BF16))
        for part in range(2):
            stop = min(width, up_t_ref.shape[0] - part * width)
            step = 3 * LANES
            for start in range(0, stop, step):
                piece = adapter[1, :, part * rank : (part + 1) * rank, start : start + step]
                up_t_ref[part * width + start : part * width + start + step, :] = piece.reshape(count * rank, step).T

    return kernel


def project_kernel(w_ref, normed_ref, *out_refs):
    rows = dot_nt(w_ref[...].reshape(CHUNKS * CHUNK_ROWS, w_ref.shape[-1]), normed_ref[...])
    for i, out_ref in enumerate(out_refs):
        out_ref[...] = rows[i * CHUNK_ROWS : (i + 1) * CHUNK_ROWS, :]


def project_own_kernel(w_ref, normed_ref, down_ref, up_ref, down_y_ref, up_y_ref, *out_refs):
    pack(0, down_ref, up_ref, out_refs[-1])
    pack(1, down_y_ref, up_y_ref, out_refs[-1])
    project_kernel(w_ref, normed_ref, *out_refs[:-1])


def project_shared_kernel(near_x, near_xy, far_x, far_xy, normed_ref, *rest):
    out_refs, weight = rest[:-1], rest[-1]
    half = lax.rem(lax.axis_index("req"), 2)
    core = lax.rem(lax.axis_index("ad"), 2)
    for n in range(len(out_refs)):
        weight[n, core, half] = near_x[n]
        weight[n, core, 1 - half] = near_xy[n]
        weight[n, 1 - core, half] = far_x[n]
        weight[n, 1 - core, 1 - half] = far_xy[n]
    project_chunks(weight, normed_ref, out_refs)


def project_chunks(weight, normed_ref, out_refs):
    step = 4 * HEAD_DIM
    rows = dot_nt(weight[...].reshape(len(out_refs) * step, weight.shape[-1]), normed_ref[...])
    for n, out_ref in enumerate(out_refs):
        out_ref[...] = rows[n * step : (n + 1) * step, :].reshape(out_ref.shape)


def put_rotated(target, index, lanes, rows, rope_ref, base):
    cosine = rope_ref[base : base + HALF, lanes]
    sine = rope_ref[base + HALF : base + 2 * HALF, lanes]
    first, second = rows[:HALF, :], rows[HALF:, :]
    target[index + (slice(0, HALF), lanes)] = (first * cosine - second * sine).astype(BF16)
    target[index + (slice(HALF, HEAD_DIM), lanes)] = (second * cosine + first * sine).astype(BF16)


def make_attend_kernel(i):
    def run(prepare, query_rows, key_rows, value_rows, rope_ref, low_ref, up_t_ref, bias_ref, out_ref, parts):
        query_up = jnp.concatenate(
            [up_t_ref[start : start + CHUNK_ROWS, :] for start in (i * CHUNK_ROWS, (SHARD_HEADS + 2 * i) * HEAD_DIM)],
            axis=0,
        )
        value_up = jnp.concatenate(
            [up_t_ref[start : start + HEAD_DIM, :] for start in ((HEADS + i) * HEAD_DIM, (HEADS + i + 4) * HEAD_DIM)],
            axis=0,
        )

        def fill(g):
            lanes = slice(2 * g * LANES, 2 * (g + 1) * LANES)
            prepare(lanes)
            query_delta = dot_nn(query_up, low_ref[0, :, lanes])
            value_delta = dot_nn(value_up, low_ref[1, :, lanes])
            for p in range(2):
                put_rotated(parts, (2, p), lanes, key_rows(p, lanes), rope_ref, 0)
                for c in range(2):
                    row = (2 * c + p) * HEAD_DIM
                    rows = query_rows(c, p, lanes) + query_delta[row : row + HEAD_DIM, :]
                    put_rotated(parts, (c, p), lanes, rows, rope_ref, 2 * HALF)
                rows = value_rows(p, lanes) + value_delta[p * HEAD_DIM : (p + 1) * HEAD_DIM, :]
                parts[3, p, :, lanes] = rows.astype(BF16)

        def lanes_of(b):
            return slice(b * LANES, (b + 1) * LANES)

        def score(b, p):
            lanes = lanes_of(b)
            key = parts[2, p, :, lanes].T[:BLOCK, :]
            query = jnp.concatenate([parts[p, 0, :, lanes], parts[p, 1, :, lanes]], axis=1)
            return dot_nn(key, query)

        def soften(b, scores):
            bias = bias_ref[b]
            scores = scores + jnp.concatenate([bias, bias], axis=1)
            weights = jnp.exp2(scores - jnp.max(scores, axis=0, keepdims=True))
            probs = (weights * (1.0 / jnp.sum(weights, axis=0, keepdims=True))).astype(BF16)
            return jnp.concatenate([probs, jnp.zeros((LANES - BLOCK, 2 * LANES), BF16)], axis=0)

        def mingle(b, p, probs):
            result = dot_nn(parts[3, p, :, lanes_of(b)], probs).astype(BF16)
            return [result[:, :LANES], result[:, LANES:]]

        blocks = bias_ref.shape[0]
        work = [(b, p) for b in range(blocks) for p in range(2)]
        ahead = 4
        filled = 0
        scores, results = {}, {}
        for n in range(len(work) + ahead + 1):
            if n < len(work):
                while filled < blocks // 2 and 2 * filled <= min(work[n][0] + 2, blocks - 1):
                    fill(filled)
                    filled += 1
                scores[n] = score(*work[n])
            m = n - ahead
            if 0 <= m < len(work):
                scores[m] = soften(work[m][0], scores[m])
            m -= 1
            if 0 <= m < len(work):
                b, p = work[m]
                results[p] = mingle(b, p, scores.pop(m))
                if p == 1:
                    heads = jnp.concatenate(results.pop(0) + results.pop(1), axis=0)
                    out_ref[b * BLOCK : (b + 1) * BLOCK, :] = heads.T[:BLOCK, :]

    def attend(local, remote, prepare, own_ref, near_ref, *rest):
        shard = lax.axis_index("ad")
        side, core = shard // 2, lax.rem(shard, 2)
        local[core] = own_ref[...].reshape(local.shape[1:])
        local[1 - core] = near_ref[...].reshape(local.shape[1:])

        def held(c, p, lanes):
            return local[c, p, :, lanes]

        @pl.when(side == 0)
        def _():
            run(prepare, held, lambda p, lanes: remote(0, p, lanes), lambda p, lanes: remote(1, p, lanes), *rest)

        @pl.when(side == 1)
        def _():
            run(prepare, remote, lambda p, lanes: held(0, p, lanes), lambda p, lanes: held(1, p, lanes), *rest)

    def kernel(own_ref, near_ref, remote_ref, rope_ref, low_ref, up_t_ref, bias_ref, out_ref, local, parts):
        attend(
            local, lambda c, p, lanes: remote_ref[c, p, :, lanes], lambda lanes: None,
            own_ref, near_ref, rope_ref, low_ref, up_t_ref, bias_ref, out_ref, parts,
        )

    def project_kernel_of(pieces, normed_ref, own_ref, near_ref, rope_ref, low_ref, up_t_ref, bias_ref, out_ref, *scratch):
        local, parts, weight = scratch
        half = lax.rem(lax.axis_index("req"), 2)
        core = lax.rem(lax.axis_index("ad"), 2)
        if len(pieces) == 4:
            near_x, near_xy, far_x, far_xy = pieces
            weight[core, half] = near_x[0]
            weight[core, 1 - half] = near_xy[0]
            weight[1 - core, half] = far_x[0]
            weight[1 - core, 1 - half] = far_xy[0]
        else:
            near_x, far_x = pieces
            weight[core] = near_x[0]
            weight[1 - core] = far_x[0]
        made = {}

        def prepare(lanes):
            rows = weight[...].reshape(4 * HEAD_DIM, weight.shape[-1])
            made[lanes.start] = dot_nt(rows, normed_ref[lanes, :])

        def remote(c, p, lanes):
            row = (2 * c + p) * HEAD_DIM
            return made[lanes.start][row : row + HEAD_DIM, :]

        attend(local, remote, prepare, own_ref, near_ref, rope_ref, low_ref, up_t_ref, bias_ref, out_ref, parts)

    def shared_kernel(a, b, c, d, *rest):
        project_kernel_of((a, b, c, d), *rest)

    def direct_kernel(a, b, *rest):
        project_kernel_of((a, b), *rest)

    return kernel, shared_kernel, direct_kernel


def mix_kernel(x_ref, w_ref, *rest):
    parts, out_hbm, ready, sems = rest[:CHUNKS], rest[CHUNKS], rest[CHUNKS + 1], rest[CHUNKS + 2]
    half = SHARD_HEADS * HEAD_DIM
    tokens = ready.shape[0]
    bounds = (0, tokens * 3 // 7, tokens * 11 // 14, tokens)
    weight = jnp.concatenate(
        [
            w_ref[c * half + i * CHUNK_ROWS : c * half + (i + 1) * CHUNK_ROWS, :]
            for i in range(CHUNKS)
            for c in range(2)
        ],
        axis=0,
    )
    copies = []
    for n in range(len(bounds) - 1):
        part = slice(bounds[n], bounds[n + 1])
        attended = jnp.concatenate([part_ref[part, :] for part_ref in parts], axis=1)
        ready[part, :] = (x_ref[part, :].astype(F32) + dot_nn(attended, weight)).astype(BF16)
        copies.append(pltpu.make_async_copy(ready.at[part], out_hbm.at[part], sems.at[n]))
        copies[-1].start()
    for copy in copies:
        copy.wait()


def after(value, *others):
    return lax.optimization_barrier((value,) + others)[0]


def body(
    layer_input_hidden,
    input_norm_scale,
    query_key_value_weight,
    output_weight,
    adapter_down_weight,
    adapter_up_weight,
    prompt_token_length,
    request_adapter_index,
    adapter_holder_index,
):
    tokens, width = layer_input_hidden.shape
    blocks = tokens // BLOCK
    padded = blocks * LANES
    rank = adapter_up_weight.shape[1]
    features = adapter_up_weight.shape[2]
    shard_cols = query_key_value_weight.shape[1]
    shards, requests = lax.axis_size("ad"), lax.axis_size("req")
    other_side = [(a, a ^ 2) for a in range(shards)]
    other_core = [(a, a ^ 1) for a in range(shards)]

    def other_row(bit):
        return [(r, r ^ bit) for r in range(requests)]

    turned = pl.pallas_call(
        turn_kernel,
        out_shape=[jax.ShapeDtypeStruct((CHUNKS, 2, HEAD_DIM, width), BF16)]
        + [jax.ShapeDtypeStruct((len(chunks), HEAD_DIM, width), BF16) for chunks in SHARED]
        + [jax.ShapeDtypeStruct((len(DIRECT), 2, HEAD_DIM, width), BF16)],
        in_specs=[VMEM],
        out_specs=[VMEM] * (2 + len(SHARED)),
        scratch_shapes=[pltpu.VMEM((shard_cols, width), BF16)],
        compiler_params=params(20),
        name="turn_weight",
    )(query_key_value_weight)
    own, sends = turned[0], turned[1:]

    down_y = lax.ppermute(adapter_down_weight, "req", other_row(1))
    up_y = lax.ppermute(adapter_up_weight, "req", other_row(1))
    normed, rope, bias, slot = pl.pallas_call(
        norm_kernel,
        out_shape=[
            jax.ShapeDtypeStruct((padded, width), BF16),
            jax.ShapeDtypeStruct((4 * HALF, padded), F32),
            jax.ShapeDtypeStruct((blocks, BLOCK, LANES), F32),
            jax.ShapeDtypeStruct((1, padded), jnp.int32),
        ],
        in_specs=[VMEM] * 3 + [SMEM] * 3,
        out_specs=[VMEM] * 4,
        compiler_params=params(16),
        cost_estimate=NO_COST,
        name="norm_tokens",
    )(
        layer_input_hidden, input_norm_scale, jnp.asarray(rope_tables()),
        prompt_token_length, request_adapter_index, adapter_holder_index,
    )

    def project(weight, name):
        return pl.pallas_call(
            project_kernel,
            out_shape=[jax.ShapeDtypeStruct((CHUNK_ROWS, padded), F32)] * CHUNKS,
            in_specs=[VMEM] * 2,
            out_specs=[VMEM] * CHUNKS,
            compiler_params=params(24),
            cost_estimate=NO_COST,
            name=name,
        )(weight, normed)

    def project_remote(kernel, chunks, arrays, token):
        return pl.pallas_call(
            kernel,
            out_shape=[jax.ShapeDtypeStruct((2, 2, HEAD_DIM, padded), F32)] * len(chunks),
            in_specs=[VMEM] * (len(arrays) + 1),
            out_specs=[VMEM] * len(chunks),
            scratch_shapes=[pltpu.VMEM((len(chunks), 2, 2, HEAD_DIM, width), BF16)],
            compiler_params=params(20),
            cost_estimate=NO_COST,
            name=f"project_{chunks[0]}",
        )(*arrays, after(normed, token))

    def attend(i, rows):
        return pl.pallas_call(
            make_attend_kernel(i)[0],
            out_shape=jax.ShapeDtypeStruct((tokens, 4 * HEAD_DIM), BF16),
            in_specs=[VMEM] * 7,
            out_specs=VMEM,
            scratch_shapes=[
                pltpu.VMEM((2, 2, HEAD_DIM, padded), F32),
                pltpu.VMEM((4, 2, HEAD_DIM, padded), BF16),
            ],
            compiler_params=params(16 if len(codes) <= 8 else 24),
            cost_estimate=NO_COST,
            name=f"attend_{i}",
        )(own_parts[i], near_parts[i], rows, rope, low, up_t, bias)

    def project_and_attend(i, arrays, token):
        return pl.pallas_call(
            make_attend_kernel(i)[1 if len(arrays) == 4 else 2],
            out_shape=jax.ShapeDtypeStruct((tokens, 4 * HEAD_DIM), BF16),
            in_specs=[VMEM] * (len(arrays) + 7),
            out_specs=VMEM,
            scratch_shapes=[
                pltpu.VMEM((2, 2, HEAD_DIM, padded), F32),
                pltpu.VMEM((4, 2, HEAD_DIM, padded), BF16),
                pltpu.VMEM((2, 2, HEAD_DIM, width), BF16),
            ],
            compiler_params=params(20 if len(codes) <= 8 else 28),
            cost_estimate=NO_COST,
            name=f"project_attend_{i}",
        )(*arrays, after(normed, token), own_parts[i], near_parts[i], rope, low, up_t, bias)

    def gather_adapters(packed, codes, bit, before, then):
        got = after(lax.ppermute(after(packed, before), "req", other_row(bit)), then)
        return jnp.concatenate([packed, got], axis=0), codes + [code ^ bit for code in codes]

    def along(piece, token):
        return lax.ppermute(after(piece, token), "req", other_row(1))

    def beside(piece, token):
        return lax.ppermute(after(piece, token), "ad", other_core)

    x = [lax.ppermute(send, "ad", other_side) for send in sends]
    near = beside(own, own)
    xy, far_x, far_xy, rows, attended = [], [], [], [], []

    def project_shared(i, *tokens):
        arrays = (x[i], xy[i], far_x[i], far_xy[i])
        rows.extend(project_remote(project_shared_kernel, SHARED[i], arrays, *tokens))

    bits = []
    while 2 ** len(bits) < requests:
        bits.append(2 ** len(bits))
    bits = bits[:0:-1]
    codes = [0, 1]
    *own_parts, packed = pl.pallas_call(
        project_own_kernel,
        out_shape=[jax.ShapeDtypeStruct((CHUNK_ROWS, padded), F32)] * CHUNKS
        + [jax.ShapeDtypeStruct((2, 2 * rank, width), BF16)],
        in_specs=[VMEM] * 6,
        out_specs=[VMEM] * (CHUNKS + 1),
        compiler_params=params(24),
        cost_estimate=NO_COST,
        name="project_own",
    )(after(own, normed), normed, adapter_down_weight, adapter_up_weight, down_y, up_y)
    xy.append(along(x[0], normed))
    far_x.append(beside(x[0], own_parts[0]))
    near_parts = project(after(near, x[0]), "project_near")
    for bit in bits[:1]:
        packed, codes = gather_adapters(packed, codes, bit, normed, near_parts[0])
    xy.append(along(x[1], near_parts[0]))
    far_x.append(beside(x[1], own_parts[0]))
    far_xy.append(beside(xy[0], x[1]))
    for bit in bits[1:]:
        packed, codes = gather_adapters(packed, codes, bit, own_parts[0], own_parts[0])
    packed_other = beside(packed, own_parts[0])
    project_shared(0, near_parts[0])
    low, up_t = pl.pallas_call(
        make_low_kernel(codes, rank),
        out_shape=[
            jax.ShapeDtypeStruct((2, len(codes) * rank, padded), BF16),
            jax.ShapeDtypeStruct((features, len(codes) * rank), BF16),
        ],
        in_specs=[VMEM] * 4,
        out_specs=[VMEM] * 2,
        scratch_shapes=[pltpu.VMEM((2,) + packed.shape, BF16)],
        compiler_params=params(16 if len(codes) <= 8 else 48),
        cost_estimate=NO_COST,
        name="adapter_low",
    )(packed, packed_other, after(normed, rows[0]), slot)
    attended = [attend(i, rows[i]) for i in SHARED[0]]
    far_x.append(beside(x[2], rows[0]))
    far_xy.append(beside(xy[1], attended[0]))
    attended.append(project_and_attend(2, (x[1], xy[1], far_x[1], far_xy[1]), attended[1]))
    attended.append(project_and_attend(3, (x[2], far_x[2]), attended[2]))
    return pl.pallas_call(
        mix_kernel,
        out_shape=jax.ShapeDtypeStruct((tokens, width), BF16),
        in_specs=[VMEM] * (2 + CHUNKS),
        out_specs=HBM,
        scratch_shapes=[
            pltpu.VMEM((tokens, width), BF16),
            pltpu.SemaphoreType.DMA((3,)),
        ],
        compiler_params=params(20),
        name="mix_output",
    )(layer_input_hidden, output_weight, *attended)


def solution(mesh):
    placed = (
        P(("req", "ad"), None),
        P(),
        P(None, "ad"),
        P(),
        P("req", None, None),
        P("req", None, None),
        P(("req", "ad"), None),
        P(("req", "ad"), None),
        P(),
    )
    return jax.shard_map(
        body, mesh=mesh, in_specs=placed, out_specs=P(("req", "ad"), None), check_vma=False
    )
```
